128 devices in a mesh: lon: 16 (over x, z), lat: 8 (over y, core).
Axes of the slice: x: 4, y: 4, z: 4, core: 2. Of those that a mesh axis runs over, the one named last changes fastest.
Arguments:
- winds: float32 [2, 12, 256, 2048], P(None, None, 'lat', 'lon'), may hold values from -6 to 6
- coriolis: float32 [256], P('lat'), may hold values from 0.1 to 0.5
- rays: float32 [16, 8, 128, 4, 128], P('lon', 'lat'), as said below
- ray_cell: int32 [16, 8, 128, 128], P('lon', 'lat'), may hold values from 0 to 4095
- ray_level: int32 [16, 8, 128, 128], P('lon', 'lat'), may hold values from 0 to 11
- turning: int32 [16, 8, 128, 128], P('lon', 'lat'), may hold values 0 or 1
- leaving: int32 [16, 8, 8, 8], P('lon', 'lat'), may hold values from 0 to 127, as said below
- leave_count: int32 [16, 8, 8], P('lon', 'lat'), may hold values from 0 to 8, as said below
Outputs:
- rays_out: float32 [16, 8, 128, 4, 128], P('lon', 'lat')
- arrived: float32 [16, 8, 8, 8, 4, 128], P('lon', 'lat')
- tendency: float32 [2, 12, 256, 2048], P(None, None, 'lat', 'lon')
The draws below stay inside these ranges and needn't reach their ends.
Inputs may be any that keep to these rules, and one draw needn't show every extreme that they name: `rays`: the fourth ray field, the wave action, is positive. `leaving`: the block numbers in one tile's lists are distinct. `leave_count`: lists pointing beyond the latitude ends have count zero.
All inputs are finite; a program needn't handle non-finite values. No bound on the sum of `turning` on one device may be relied on, other than what follows from the above.
Results may differ from the reference program's by a relative error of at most 0.000078.
Values sent between devices are 32-bit elements; how exact they have to be, the bound alone decides.
A program may use at most 128 MiB of HBM per device.

```python
import math
import jax
import jax.numpy as jnp
from jax import lax

CX = 128
CY = 32
LEV = 12
NB = 128
BLK = 128
CAP = 8
LON_TILES = 16
LAT_TILES = 8
NLON = 2048
NLAT = 256
CELLS = 4096


def draw_rays(key, part):
    key_a = jax.random.fold_in(key, 11)
    key_b = jax.random.fold_in(key, 12)
    waves = jax.random.normal(key_a, (LON_TILES, LAT_TILES, NB, 3, BLK), jnp.float32)
    level = jax.random.uniform(key_b, (LON_TILES, LAT_TILES, NB, 1, BLK), jnp.float32, -2.302585, 0.0)
    action = jnp.exp(level)
    return jnp.concatenate([waves, action], axis=3)


def draw_leaving(key, part):
    scores = jax.random.randint(jax.random.fold_in(key, 21), (LON_TILES, LAT_TILES, NB), 0, 1048576)
    scores = scores * NB + jnp.arange(NB, dtype=jnp.int32)
    order = jnp.argsort(scores, axis=-1)[..., :8 * CAP]
    return order.reshape(LON_TILES, LAT_TILES, 8, CAP).astype(jnp.int32)


def draw_leave_count(key, part):
    counts = jax.random.randint(jax.random.fold_in(key, 31), (LON_TILES, LAT_TILES, 8), 0, CAP + 1)
    offset = jax.random.randint(jax.random.fold_in(key, 32), (), 0, 3)
    lon = jnp.arange(LON_TILES, dtype=jnp.int32)[:, None, None]
    lat = jnp.arange(LAT_TILES, dtype=jnp.int32)[None, :, None]
    direction = jnp.arange(8, dtype=jnp.int32)[None, None, :]
    full = ((lon + lat + offset) % 3 == 0) & (direction == 0)
    counts = jnp.where(full, CAP, counts)
    north = (direction == 2) | (direction == 4) | (direction == 5)
    south = (direction == 3) | (direction == 6) | (direction == 7)
    counts = jnp.where(north & (lat == LAT_TILES - 1), 0, counts)
    counts = jnp.where(south & (lat == 0), 0, counts)
    return counts.astype(jnp.int32)


def plant(entries, stream_key, smallest, high):
    shape = entries.shape
    index_at = [jax.random.randint(jax.random.fold_in(stream_key, axis), (), 0, shape[axis]) for axis in range(len(shape))]
    entries = entries.at[tuple(index_at)].set(smallest)
    longest = shape.index(max(shape))
    index_at[longest] = (index_at[longest] + 1) % shape[longest]
    return entries.at[tuple(index_at)].set(high)


def steps_of(rng, shape, cuts, least, high):
    def one(axis_at, blocks):
        heights = jax.random.uniform(jax.random.fold_in(jax.random.fold_in(rng, 6), axis_at), (blocks,), jnp.float32, least / len(cuts), high / len(cuts))
        return jnp.repeat(jnp.exp(heights), shape[axis_at] // blocks).reshape((-1,) + (1,) * (len(shape) - axis_at - 1))

    gain = one(*cuts[0])
    for cut in cuts[1:]:
        gain = gain * one(*cut)
    return gain


def bell_draw(stream_key, dims, spread, most, pieces=(), kind=jnp.bfloat16):
    values = jax.random.normal(stream_key, dims, jnp.float32) * spread
    if len(pieces) > 0:
        values = steps_of(stream_key, dims, pieces, -0.22, 0.18) * values
    return jnp.clip(values, min=-most, max=most).astype(kind)


def setup_inputs(seed: int = 0) -> dict:
    key_of = jax.random.split(jax.random.key(seed), 9)
    return {
        "winds": bell_draw(key_of[0], (2, LEV, NLAT, NLON), 1.0, 6.0, ((2, 8), (3, 16)), jnp.float32),
        "coriolis": jnp.clip(jnp.exp(math.log(0.5) - 1.609438 * jax.random.uniform(key_of[1], (NLAT,), jnp.float32) ** steps_of(key_of[1], (NLAT,), ((0, 8),), -0.2, 0.2)), 0.1, 0.5),
        "rays": draw_rays(jax.random.fold_in(key_of[8], 71), 0),
        "ray_cell": plant(jax.random.randint(key_of[3], (LON_TILES, LAT_TILES, NB, BLK), 0, CELLS), jax.random.fold_in(key_of[3], 1), 0, CELLS - 1).astype(jnp.int32),
        "ray_level": plant(jax.random.randint(key_of[4], (LON_TILES, LAT_TILES, NB, BLK), 0, LEV), jax.random.fold_in(key_of[4], 1), 0, LEV - 1).astype(jnp.int32),
        "turning": plant((jax.random.randint(key_of[5], (LON_TILES, LAT_TILES, NB, BLK), 0, 4) < 1).astype(jnp.int32), jax.random.fold_in(key_of[5], 1), 0, 1),
        "leaving": draw_leaving(jax.random.fold_in(key_of[8], 71), 0),
        "leave_count": draw_leave_count(jax.random.fold_in(key_of[8], 71), 0),
    }


STEP = 0.1
DIRS = ((0, 1), (0, -1), (1, 0), (-1, 0), (1, 1), (1, -1), (-1, 1), (-1, -1))

def diff_wrap(field, axis):
    return (jnp.roll(field, -1, axis) - jnp.roll(field, 1, axis)) * 0.5

def diff_open(field, axis):
    widths = [(1, 1) if a == axis else (0, 0) for a in range(field.ndim)]
    padded = jnp.pad(field, widths)
    count = field.shape[axis]
    upper = lax.slice_in_dim(padded, 2, count + 2, axis=axis)
    lower = lax.slice_in_dim(padded, 0, count, axis=axis)
    return (upper - lower) * 0.5

def propagate(wave_k, wave_l, wave_m, action, sample, fcor, turn):
    new_k = wave_k - STEP * (wave_k * sample[0] + wave_l * sample[1])
    new_l = wave_l - STEP * (wave_k * sample[2] + wave_l * sample[3])
    new_m = wave_m - STEP * (wave_k * sample[4] + wave_l * sample[5])
    new_m = jnp.where(turn == 1, -new_m, new_m)
    horiz = new_k * new_k + new_l * new_l
    total = horiz + new_m * new_m + 1.0
    fsq = fcor * fcor
    freq2 = (horiz + fsq * (new_m * new_m + 1.0)) / total
    freq = jnp.sqrt(freq2)
    group_x = new_k * (1.0 - freq2) / (freq * total)
    group_z = new_m * (fsq - freq2) / (freq * total)
    return (new_k, new_l, new_m, group_z * new_k * action, group_z * new_l * action, group_x * new_k * action)

def reference(winds, coriolis, rays, ray_cell, ray_level, turning, leaving, leave_count):
    grad = jnp.concatenate([diff_wrap(winds, 3), diff_open(winds, 2), diff_open(winds, 1)], axis=0)
    lon_tile = jnp.arange(LON_TILES, dtype=jnp.int32)[:, None, None, None]
    lat_tile = jnp.arange(LAT_TILES, dtype=jnp.int32)[None, :, None, None]
    ycell = lat_tile * CY + ray_cell // CX
    xcell = lon_tile * CX + ray_cell % CX
    sample = grad[:, ray_level, ycell, xcell]
    fcor = coriolis[ycell]
    new_k, new_l, new_m, flux_a, flux_b, flux_c = propagate(rays[:, :, :, 0], rays[:, :, :, 1], rays[:, :, :, 2], rays[:, :, :, 3], sample, fcor, turning)
    rays_out = jnp.stack([new_k, new_l, new_m, rays[:, :, :, 3]], axis=3)
    flat = ((ray_level * NLAT + ycell) * NLON + xcell).reshape(-1)
    fluxes = jnp.stack([flux_a, flux_b, flux_c]).reshape(3, -1)
    deposit = jnp.zeros((3, LEV * NLAT * NLON), jnp.float32).at[:, flat].add(fluxes)
    deposit = deposit.reshape(3, LEV, NLAT, NLON)
    east = -diff_open(deposit[0], 0) - diff_wrap(deposit[2], 2)
    north = -diff_open(deposit[1], 0)
    tendency = jnp.stack([east, north])
    jj = jnp.arange(LON_TILES, dtype=jnp.int32)[:, None, None, None]
    ii = jnp.arange(LAT_TILES, dtype=jnp.int32)[None, :, None, None]
    dd = jnp.arange(8, dtype=jnp.int32)[None, None, :, None]
    cc = jnp.arange(CAP, dtype=jnp.int32)[None, None, None, :]
    dlat = jnp.array([d[0] for d in DIRS], dtype=jnp.int32)[dd]
    dlon = jnp.array([d[1] for d in DIRS], dtype=jnp.int32)[dd]
    src_j = (jj - dlon) % LON_TILES
    src_i = ii - dlat
    valid = (src_i >= 0) & (src_i < LAT_TILES)
    src_c = jnp.clip(src_i, 0, LAT_TILES - 1)
    block = leaving[src_j, src_c, dd, cc]
    live = valid & (cc < leave_count[src_j, src_c, dd])
    arrived = jnp.where(live[..., None, None], rays_out[src_j, src_c, block], jnp.float32(0.0))
    return (rays_out, arrived, tendency)
```

```python
import jax
import jax.numpy as jnp
from jax import lax
from jax.experimental import pallas as pl
from jax.experimental.pallas import tpu as pltpu
from jax.sharding import PartitionSpec as P

STEP = 0.1
DIRS = ((0, 1), (0, -1), (1, 0), (-1, 0), (1, 1), (1, -1), (-1, 1), (-1, -1))
MESH = pl.DeviceIdType.MESH
LEV, CY, CX, NB = 12, 32, 128, 128
ROWS = LEV * CY
GRP = 8
SPAN = GRP * 128
STEPS = NB // GRP
F32, BF16 = jnp.float32, jnp.bfloat16


def propagate(wave_k, wave_l, wave_m, action, sample, fcor, turn):
    new_k = wave_k - STEP * (wave_k * sample[0] + wave_l * sample[1])
    new_l = wave_l - STEP * (wave_k * sample[2] + wave_l * sample[3])
    new_m = wave_m - STEP * (wave_k * sample[4] + wave_l * sample[5])
    new_m = jnp.where(turn == 1, -new_m, new_m)
    horiz = new_k * new_k + new_l * new_l
    total = horiz + new_m * new_m + 1.0
    fsq = fcor * fcor
    freq2 = (horiz + fsq * (new_m * new_m + 1.0)) / total
    freq = jnp.sqrt(freq2)
    group_x = new_k * (1.0 - freq2) / (freq * total)
    group_z = new_m * (fsq - freq2) / (freq * total)
    return (
        new_k,
        new_l,
        new_m,
        group_z * new_k * action,
        group_z * new_l * action,
        group_x * new_k * action,
    )


def level_diff(field):
    zero = jnp.zeros((CY, CX), F32)
    upper = jnp.concatenate([field[CY:], zero], axis=0)
    lower = jnp.concatenate([zero, field[:-CY]], axis=0)
    return (upper - lower) * 0.5


def split(value):
    high = value.astype(BF16)
    return high, (value - high.astype(F32)).astype(BF16)


def kernel(
    leaving, count, fcor, winds, rays, cell, level, turn,
    rays_out, arrived, tend,
    wind_t, table, hots, samples, fluxes, dep,
    lon_out, lon_in, lat_out, lat_in, edge_out, edge_in, box_out, box_in,
    send_sem, recv_sem,
):
    lon, lat = lax.axis_index("lon"), lax.axis_index("lat")
    nlon, nlat = lax.axis_size("lon"), lax.axis_size("lat")

    def at(dlat, dlon):
        return (lax.rem(lon + dlon + nlon, nlon), lax.rem(lat + dlat + nlat, nlat))

    def copy(src, dst, which, where):
        return pltpu.make_async_remote_copy(
            src_ref=src, dst_ref=dst, send_sem=send_sem.at[which], recv_sem=recv_sem.at[which],
            device_id=at(*where), device_id_type=MESH,
        )

    barrier = pltpu.get_barrier_semaphore()
    for where in DIRS:
        pl.semaphore_signal(barrier, inc=1, device_id=at(*where), device_id_type=MESH)

    for w in range(2):
        flipped = winds[w * ROWS : (w + 1) * ROWS, :].T
        wind_t[w] = flipped
        lon_out[0, w : w + 1, :] = flipped[CX - 1 : CX, :]
        lon_out[1, w : w + 1, :] = flipped[0:1, :]
    for half in range(2):
        lon_out[half, 2:8, :] = jnp.zeros((6, ROWS), F32)
    lat_out[0] = winds[pl.ds(CY - 1, 2 * LEV, stride=CY), :]
    lat_out[1] = winds[pl.ds(0, 2 * LEV, stride=CY), :]
    pl.semaphore_wait(barrier, 8)
    halos = [
        copy(lon_out.at[0], lon_in.at[0], 0, (0, 1)),
        copy(lon_out.at[1], lon_in.at[1], 1, (0, -1)),
        copy(lat_out.at[0], lat_in.at[0], 2, (1, 0)),
        copy(lat_out.at[1], lat_in.at[1], 3, (-1, 0)),
    ]
    for each in halos:
        each.start()

    def keep(field, flipped):
        high, low = split(flipped)
        table[field * CX : (field + 1) * CX, 0:ROWS] = high
        table[field * CX : (field + 1) * CX, ROWS : 2 * ROWS] = low

    for w in range(2):
        keep(4 + w, level_diff(winds[w * ROWS : (w + 1) * ROWS, :]).T)
    for each in halos:
        each.wait()

    column = lax.broadcasted_iota(jnp.int32, (CX, ROWS), 0)
    row = lax.rem(lax.broadcasted_iota(jnp.int32, (ROWS, CX), 0), CY)
    for w in range(2):
        flipped = wind_t[w]
        east = jnp.where(column == CX - 1, lon_in[1, w : w + 1, :], pltpu.roll(flipped, CX - 1, 0))
        west = jnp.where(column == 0, lon_in[0, w : w + 1, :], pltpu.roll(flipped, 1, 0))
        keep(w, (east - west) * 0.5)
        field = winds[w * ROWS : (w + 1) * ROWS, :]
        below = jnp.where(lat == 0, 0.0, lat_in[0, w * LEV : (w + 1) * LEV, :])
        above = jnp.where(lat == nlat - 1, 0.0, lat_in[1, w * LEV : (w + 1) * LEV, :])
        spread = lambda edge: jnp.broadcast_to(edge[:, None, :], (LEV, CY, CX)).reshape(ROWS, CX)
        north = jnp.where(row == CY - 1, spread(above), pltpu.roll(field, ROWS - 1, 0))
        south = jnp.where(row == 0, spread(below), pltpu.roll(field, 1, 0))
        keep(2 + w, ((north - south) * 0.5).T)

    x_ids = lax.broadcasted_iota(jnp.int32, (CX, 128), 0)
    r_ids = lax.broadcasted_iota(jnp.int32, (ROWS, 128), 0)

    def gather(c, carry):
        for i in range(GRP):
            cells = cell[pl.ds(c * GRP + i, 1), :]
            rows = level[pl.ds(c * GRP + i, 1), :] * CY + lax.shift_right_logical(cells, 7)
            hots[c, :, i * 128 : (i + 1) * 128] = jnp.where(r_ids == rows, 1.0, 0.0).astype(BF16)
        hot = hots[c]
        picked = lax.dot_general(
            table[...], jnp.concatenate([hot, hot], axis=0), (((1,), (0,)), ((), ())),
            preferred_element_type=F32,
        )
        for i in range(GRP):
            mask = x_ids == jnp.bitwise_and(cell[pl.ds(c * GRP + i, 1), :], CX - 1)
            for f in range(6):
                part = picked[f * CX : (f + 1) * CX, i * 128 : (i + 1) * 128]
                samples[f, i : i + 1, :] = jnp.sum(jnp.where(mask, part, 0.0), axis=0, keepdims=True)
        blocks = pl.ds(pl.multiple_of(c * GRP, GRP), GRP)
        y = lax.shift_right_logical(cell[blocks, :], 7)
        f_ray = jnp.zeros((GRP, 128), F32)
        for i in range(CY):
            f_ray = jnp.where(y == i, fcor[i], f_ray)
        fields = [rays[pl.ds(c * GRP * 4 + f, GRP, stride=4), :] for f in range(4)]
        out = propagate(*fields, [samples[f] for f in range(6)], f_ray, turn[blocks, :])
        for f, value in enumerate((*out[:3], fields[3])):
            rays_out[pl.ds(c * GRP * 4 + f, GRP, stride=4), :] = value
        for j in range(3):
            high = out[3 + j].astype(BF16).astype(F32)
            fluxes[2 * j, blocks, :] = high
            fluxes[2 * j + 1, blocks, :] = out[3 + j] - high
        return carry

    lax.fori_loop(0, STEPS, gather, 0)

    boxes = []
    for d, where in enumerate(DIRS):
        for slot in range(8):
            block = rays_out[pl.ds(leaving[d, slot] * 4, 4), :]
            box_out[d, slot * 4 : slot * 4 + 4, :] = jnp.where(slot < count[d], block, 0.0)
        boxes.append(copy(box_out.at[d], box_in.at[d], 4 + d, where))
        boxes[-1].start()

    def scatter(js):
        first = js[0]
        width = len(js) * 2 * CX

        def step(c, carry):
            parts = []
            for i in range(2 * GRP):
                at_row = pl.ds(c * 2 * GRP + i, 1)
                mask = x_ids == jnp.bitwise_and(cell[at_row, :], CX - 1)
                parts.append(
                    jnp.concatenate(
                        [
                            jnp.where(mask, fluxes[2 * j + p, at_row, :], 0.0).astype(BF16)
                            for j in js
                            for p in range(2)
                        ],
                        axis=0,
                    )
                )
            hot = jnp.concatenate([hots[2 * c], hots[2 * c + 1]], axis=1)
            dep[:, first * 2 * CX : first * 2 * CX + width] += lax.dot_general(
                hot, jnp.concatenate(parts, axis=1), (((1,), (1,)), ((), ())),
                preferred_element_type=F32,
            )
            return carry

        dep[:, first * 2 * CX : first * 2 * CX + width] = jnp.zeros((ROWS, width), F32)
        lax.fori_loop(0, STEPS // 2, step, 0)

    def deposit(j):
        return dep[:, j * 2 * CX : j * 2 * CX + CX] + dep[:, j * 2 * CX + CX : (j + 1) * 2 * CX]

    scatter((2,))
    zonal = deposit(2).T
    wind_t[0] = zonal
    for half in range(2):
        edge_out[half] = jnp.zeros((8, ROWS), F32)
    edge_out[0, 0:1, :] = zonal[CX - 1 : CX, :]
    edge_out[1, 0:1, :] = zonal[0:1, :]
    edges = [
        copy(edge_out.at[0], edge_in.at[0], 12, (0, 1)),
        copy(edge_out.at[1], edge_in.at[1], 13, (0, -1)),
    ]
    for each in edges:
        each.start()
    scatter((0, 1))
    tend[ROWS : 2 * ROWS, :] = -level_diff(deposit(1))
    for each in edges:
        each.wait()
    zonal = wind_t[0]
    east = jnp.where(column == CX - 1, edge_in[1, 0:1, :], pltpu.roll(zonal, CX - 1, 0))
    west = jnp.where(column == 0, edge_in[0, 0:1, :], pltpu.roll(zonal, 1, 0))
    tend[0:ROWS, :] = -level_diff(deposit(0)) - ((east - west) * 0.5).T
    for each in boxes:
        each.wait()
    arrived[...] = box_in[...]


def on_device(winds, coriolis, rays, ray_cell, ray_level, turning, leaving, leave_count):
    vmem = pl.BlockSpec(memory_space=pltpu.VMEM)
    smem = pl.BlockSpec(memory_space=pltpu.SMEM)
    rays_new, arrived, tendency = pl.pallas_call(
        kernel,
        out_shape=(
            jax.ShapeDtypeStruct((NB * 4, 128), F32),
            jax.ShapeDtypeStruct((8, 32, 128), F32),
            jax.ShapeDtypeStruct((2 * ROWS, CX), F32),
        ),
        in_specs=[smem] * 3 + [vmem] * 5,
        out_specs=(vmem, vmem, vmem),
        scratch_shapes=[
            pltpu.VMEM((2, CX, ROWS), F32),
            pltpu.VMEM((6 * CX, 2 * ROWS), BF16),
            pltpu.VMEM((STEPS, ROWS, SPAN), BF16),
            pltpu.VMEM((6, GRP, 128), F32),
            pltpu.VMEM((6, NB, 128), F32),
            pltpu.VMEM((ROWS, 6 * CX), F32),
            pltpu.VMEM((2, 8, ROWS), F32),
            pltpu.VMEM((2, 8, ROWS), F32),
            pltpu.VMEM((2, 2 * LEV, CX), F32),
            pltpu.VMEM((2, 2 * LEV, CX), F32),
            pltpu.VMEM((2, 8, ROWS), F32),
            pltpu.VMEM((2, 8, ROWS), F32),
            pltpu.VMEM((8, 32, 128), F32),
            pltpu.VMEM((8, 32, 128), F32),
            pltpu.SemaphoreType.DMA((14,)),
            pltpu.SemaphoreType.DMA((14,)),
        ],
        compiler_params=pltpu.CompilerParams(
            collective_id=0, has_side_effects=True, vmem_limit_bytes=50 << 20
        ),
        cost_estimate=pl.CostEstimate(flops=30_000_000_000, bytes_accessed=2_000_000, transcendentals=0),
    )(
        leaving.reshape(8, 8),
        leave_count.reshape(8),
        coriolis,
        winds.reshape(2 * ROWS, CX),
        rays.reshape(NB * 4, 128),
        ray_cell.reshape(NB, 128),
        ray_level.reshape(NB, 128),
        turning.reshape(NB, 128),
    )
    return (
        rays_new.reshape(rays.shape),
        arrived.reshape(1, 1, 8, 8, 4, 128),
        tendency.reshape(winds.shape),
    )


def solution(mesh):
    placed = (
        P(None, None, "lat", "lon"),
        P("lat"),
        P("lon", "lat", None, None, None),
        P("lon", "lat", None, None),
        P("lon", "lat", None, None),
        P("lon", "lat", None, None),
        P("lon", "lat", None, None),
        P("lon", "lat", None),
    )
    return jax.shard_map(
        on_device,
        mesh=mesh,
        in_specs=placed,
        out_specs=(
            P("lon", "lat", None, None, None),
            P("lon", "lat", None, None, None, None),
            P(None, None, "lat", "lon"),
        ),
        check_vma=False,
    )
```

```python
import jax
import jax.numpy as jnp
from jax import lax
from jax.experimental import pallas as pl
from jax.experimental.pallas import tpu as pltpu
from jax.sharding import PartitionSpec as P

STEP = 0.1
DIRS = ((0, 1), (0, -1), (1, 0), (-1, 0), (1, 1), (1, -1), (-1, 1), (-1, -1))
MESH = pl.DeviceIdType.MESH
LEV, CY, CX, NB = 12, 32, 128, 128
ROWS = LEV * CY
GRP = 8
SPAN = GRP * 128
STEPS = NB // GRP
UNIT = 5461.0
F32, BF16 = jnp.float32, jnp.bfloat16


def propagate(wave_k, wave_l, wave_m, action, sample, fcor, turn):
    new_k = wave_k - STEP * (wave_k * sample[0] + wave_l * sample[1])
    new_l = wave_l - STEP * (wave_k * sample[2] + wave_l * sample[3])
    new_m = wave_m - STEP * (wave_k * sample[4] + wave_l * sample[5])
    new_m = jnp.where(turn == 1, -new_m, new_m)
    horiz = new_k * new_k + new_l * new_l
    total = horiz + new_m * new_m + 1.0
    fsq = fcor * fcor
    freq2 = (horiz + fsq * (new_m * new_m + 1.0)) / total
    freq = jnp.sqrt(freq2)
    group_x = new_k * (1.0 - freq2) / (freq * total)
    group_z = new_m * (fsq - freq2) / (freq * total)
    return (
        new_k,
        new_l,
        new_m,
        group_z * new_k * action,
        group_z * new_l * action,
        group_x * new_k * action,
    )


def level_diff(field):
    zero = jnp.zeros((CY, CX), F32)
    upper = jnp.concatenate([field[CY:], zero], axis=0)
    lower = jnp.concatenate([zero, field[:-CY]], axis=0)
    return (upper - lower) * 0.5


def split(value):
    high = value.astype(BF16)
    return high, (value - high.astype(F32)).astype(BF16)


def pack(first, second):
    high = jnp.round(first * UNIT).astype(jnp.int32)
    low = jnp.round(second * UNIT).astype(jnp.int32)
    return high * 65536 + (low + 32768)


def unpack(word):
    high = lax.shift_right_arithmetic(word, 16)
    low = jnp.bitwise_and(word, 65535) - 32768
    return high.astype(F32) * (1.0 / UNIT), low.astype(F32) * (1.0 / UNIT)


def kernel(
    leaving_in, count_in, fcor_in, winds_in, rays_in, cell_in, level_in, turn_in,
    rays_out, arrived, tend,
    leaving, count, fcor, winds, rays, cell, level, turn,
    wind_t, table, words, hots, samples, fluxes, dep,
    lon_out, lon_in, lat_out, lat_in, edge_out, edge_in, box_out, box_in,
    load_sem, send_sem, recv_sem,
):
    loads = [
        pltpu.make_async_copy(src, dst, load_sem.at[i])
        for i, (src, dst) in enumerate(
            (
                (winds_in, winds),
                (cell_in, cell),
                (level_in, level),
                (rays_in, rays),
                (turn_in, turn),
                (fcor_in, fcor),
                (leaving_in, leaving),
                (count_in, count),
            )
        )
    ]
    for each in loads:
        each.start()
    lon, lat = lax.axis_index("lon"), lax.axis_index("lat")
    nlon, nlat = lax.axis_size("lon"), lax.axis_size("lat")

    def at(dlat, dlon):
        return (lax.rem(lon + dlon + nlon, nlon), lax.rem(lat + dlat + nlat, nlat))

    def copy(src, dst, which, where):
        return pltpu.make_async_remote_copy(
            src_ref=src, dst_ref=dst, send_sem=send_sem.at[which], recv_sem=recv_sem.at[which],
            device_id=at(*where), device_id_type=MESH,
        )

    barrier = pltpu.get_barrier_semaphore()
    for where in DIRS:
        pl.semaphore_signal(barrier, inc=1, device_id=at(*where), device_id_type=MESH)

    loads[0].wait()
    for w in range(2):
        flipped = winds[w * ROWS : (w + 1) * ROWS, :].T
        wind_t[w] = flipped
        lon_out[0, w : w + 1, :] = flipped[CX - 1 : CX, :]
        lon_out[1, w : w + 1, :] = flipped[0:1, :]
    for half in range(2):
        lon_out[half, 2:8, :] = jnp.zeros((6, ROWS), F32)
    lat_out[0] = winds[pl.ds(CY - 1, 2 * LEV, stride=CY), :]
    lat_out[1] = winds[pl.ds(0, 2 * LEV, stride=CY), :]
    pl.semaphore_wait(barrier, 8)
    halos = [
        copy(lon_out.at[0], lon_in.at[0], 0, (0, 1)),
        copy(lon_out.at[1], lon_in.at[1], 1, (0, -1)),
        copy(lat_out.at[0], lat_in.at[0], 2, (1, 0)),
        copy(lat_out.at[1], lat_in.at[1], 3, (-1, 0)),
    ]
    for each in halos:
        each.start()

    def keep(field, flipped):
        high, low = split(flipped)
        table[field * CX : (field + 1) * CX, 0:ROWS] = high
        table[field * CX : (field + 1) * CX, ROWS : 2 * ROWS] = low

    for w in range(2):
        keep(w, level_diff(winds[w * ROWS : (w + 1) * ROWS, :]).T)
    hots[0] = jnp.zeros((ROWS, SPAN), BF16)
    fluxes[:, 0:GRP, :] = jnp.zeros((6, GRP, 128), F32)
    dep[...] = jnp.zeros((ROWS, 6 * CX), F32)
    for each in halos:
        each.wait()

    column = lax.broadcasted_iota(jnp.int32, (CX, ROWS), 0)
    row = lax.rem(lax.broadcasted_iota(jnp.int32, (ROWS, CX), 0), CY)
    along, across = [], []
    for w in range(2):
        flipped = wind_t[w]
        east = jnp.where(column == CX - 1, lon_in[1, w : w + 1, :], pltpu.roll(flipped, CX - 1, 0))
        west = jnp.where(column == 0, lon_in[0, w : w + 1, :], pltpu.roll(flipped, 1, 0))
        along.append((east - west) * 0.5)
        field = winds[w * ROWS : (w + 1) * ROWS, :]
        below = jnp.where(lat == 0, 0.0, lat_in[0, w * LEV : (w + 1) * LEV, :])
        above = jnp.where(lat == nlat - 1, 0.0, lat_in[1, w * LEV : (w + 1) * LEV, :])
        spread = lambda edge: jnp.broadcast_to(edge[:, None, :], (LEV, CY, CX)).reshape(ROWS, CX)
        north = jnp.where(row == CY - 1, spread(above), pltpu.roll(field, ROWS - 1, 0))
        south = jnp.where(row == 0, spread(below), pltpu.roll(field, 1, 0))
        across.append((north - south) * 0.5)
    words[0] = pack(*along).T
    words[1] = pack(*across)
    for each in loads[1:]:
        each.wait()

    x_ids = lax.broadcasted_iota(jnp.int32, (CX, 128), 0)
    r_ids = lax.broadcasted_iota(jnp.int32, (ROWS, 128), 0)

    def gather(c):
        for i in range(GRP):
            cells = cell[pl.ds(c * GRP + i, 1), :]
            rows = level[pl.ds(c * GRP + i, 1), :] * CY + lax.shift_right_logical(cells, 7)
            hots[c + 1, :, i * 128 : (i + 1) * 128] = jnp.where(r_ids == rows, 1.0, 0.0).astype(BF16)
        hot = hots[c + 1]
        picked = lax.dot_general(
            table[...], jnp.concatenate([hot, hot], axis=0), (((1,), (0,)), ((), ())),
            preferred_element_type=F32,
        )
        for i in range(GRP):
            mask = x_ids == jnp.bitwise_and(cell[pl.ds(c * GRP + i, 1), :], CX - 1)
            for f in range(2):
                part = picked[f * CX : (f + 1) * CX, i * 128 : (i + 1) * 128]
                samples[f, i : i + 1, :] = jnp.sum(jnp.where(mask, part, 0.0), axis=0, keepdims=True)
        blocks = pl.ds(pl.multiple_of(c * GRP, GRP), GRP)
        cells = cell[blocks, :]
        x = jnp.bitwise_and(cells, CX - 1)
        y = lax.shift_right_logical(cells, 7)
        rows = level[blocks, :] * CY + y
        found = [jnp.zeros((GRP, 128), jnp.int32)] * 2
        for r in range(ROWS):
            here = rows == r
            for w in range(2):
                line = jnp.broadcast_to(words[w, r : r + 1, :], (GRP, CX))
                got = jnp.take_along_axis(line, x, axis=1, mode="promise_in_bounds")
                found[w] = jnp.where(here, got, found[w])
        f_ray = jnp.zeros((GRP, 128), F32)
        for i in range(CY):
            f_ray = jnp.where(y == i, fcor[i], f_ray)
        fields = [rays[pl.ds(c * GRP * 4 + f, GRP, stride=4), :] for f in range(4)]
        sample = (*unpack(found[0]), *unpack(found[1]), samples[0], samples[1])
        out = propagate(*fields, sample, f_ray, turn[blocks, :])
        for f, value in enumerate((*out[:3], fields[3])):
            rays_out[pl.ds(c * GRP * 4 + f, GRP, stride=4), :] = value
        after = pl.ds(pl.multiple_of(c * GRP + GRP, GRP), GRP)
        for j in range(3):
            high = out[3 + j].astype(BF16).astype(F32)
            fluxes[2 * j, after, :] = high
            fluxes[2 * j + 1, after, :] = out[3 + j] - high

    def scatter(js, c, steps):
        parts = []
        for i in range(steps * GRP):
            mask = x_ids == jnp.bitwise_and(cell[pl.ds(jnp.maximum(c * GRP, 0) + i, 1), :], CX - 1)
            parts.append(
                jnp.concatenate(
                    [
                        jnp.where(mask, fluxes[2 * j + p, pl.ds(c * GRP + GRP + i, 1), :], 0.0).astype(BF16)
                        for j in js
                        for p in range(2)
                    ],
                    axis=0,
                )
            )
        hot = jnp.concatenate([hots[c + 1 + i] for i in range(steps)], axis=1)
        lanes = slice(js[0] * 2 * CX, (js[-1] + 1) * 2 * CX)
        dep[:, lanes] += lax.dot_general(
            hot, jnp.concatenate(parts, axis=1), (((1,), (1,)), ((), ())),
            preferred_element_type=F32,
        )

    def both(c, carry):
        scatter((1, 2), c - 1, 1)
        gather(c)
        return carry

    lax.fori_loop(0, STEPS, both, 0)

    boxes = []
    for d, where in enumerate(DIRS):
        for slot in range(8):
            block = rays_out[pl.ds(leaving[d, slot] * 4, 4), :]
            box_out[d, slot * 4 : slot * 4 + 4, :] = jnp.where(slot < count[d], block, 0.0)
        boxes.append(copy(box_out.at[d], box_in.at[d], 4 + d, where))
        boxes[-1].start()

    def deposit(j):
        return dep[:, j * 2 * CX : j * 2 * CX + CX] + dep[:, j * 2 * CX + CX : (j + 1) * 2 * CX]

    scatter((1, 2), STEPS - 1, 1)
    zonal = deposit(2).T
    wind_t[0] = zonal
    for half in range(2):
        edge_out[half] = jnp.zeros((8, ROWS), F32)
    edge_out[0, 0:1, :] = zonal[CX - 1 : CX, :]
    edge_out[1, 0:1, :] = zonal[0:1, :]
    edges = [
        copy(edge_out.at[0], edge_in.at[0], 12, (0, 1)),
        copy(edge_out.at[1], edge_in.at[1], 13, (0, -1)),
    ]
    for each in edges:
        each.start()
    lax.fori_loop(0, STEPS // 2, lambda c, carry: (scatter((0,), 2 * c, 2), carry)[1], 0)
    tend[ROWS : 2 * ROWS, :] = -level_diff(deposit(1))
    for each in edges:
        each.wait()
    zonal = wind_t[0]
    east = jnp.where(column == CX - 1, edge_in[1, 0:1, :], pltpu.roll(zonal, CX - 1, 0))
    west = jnp.where(column == 0, edge_in[0, 0:1, :], pltpu.roll(zonal, 1, 0))
    tend[0:ROWS, :] = -level_diff(deposit(0)) - ((east - west) * 0.5).T
    for each in boxes:
        each.wait()
    arrived[...] = box_in[...]


def on_device(winds, coriolis, rays, ray_cell, ray_level, turning, leaving, leave_count):
    vmem = pl.BlockSpec(memory_space=pltpu.VMEM)
    hbm = pl.BlockSpec(memory_space=pltpu.HBM)
    rays_new, arrived, tendency = pl.pallas_call(
        kernel,
        out_shape=(
            jax.ShapeDtypeStruct((NB * 4, 128), F32),
            jax.ShapeDtypeStruct((8, 32, 128), F32),
            jax.ShapeDtypeStruct((2 * ROWS, CX), F32),
        ),
        in_specs=[hbm] * 8,
        out_specs=(vmem, vmem, vmem),
        scratch_shapes=[
            pltpu.SMEM((8, 8), jnp.int32),
            pltpu.SMEM((8,), jnp.int32),
            pltpu.SMEM((32,), F32),
            pltpu.VMEM((2 * ROWS, CX), F32),
            pltpu.VMEM((NB * 4, 128), F32),
            pltpu.VMEM((NB, 128), jnp.int32),
            pltpu.VMEM((NB, 128), jnp.int32),
            pltpu.VMEM((NB, 128), jnp.int32),
            pltpu.VMEM((2, CX, ROWS), F32),
            pltpu.VMEM((2 * CX, 2 * ROWS), BF16),
            pltpu.VMEM((2, ROWS, CX), jnp.int32),
            pltpu.VMEM((STEPS + 1, ROWS, SPAN), BF16),
            pltpu.VMEM((2, GRP, 128), F32),
            pltpu.VMEM((6, NB + GRP, 128), F32),
            pltpu.VMEM((ROWS, 6 * CX), F32),
            pltpu.VMEM((2, 8, ROWS), F32),
            pltpu.VMEM((2, 8, ROWS), F32),
            pltpu.VMEM((2, 2 * LEV, CX), F32),
            pltpu.VMEM((2, 2 * LEV, CX), F32),
            pltpu.VMEM((2, 8, ROWS), F32),
            pltpu.VMEM((2, 8, ROWS), F32),
            pltpu.VMEM((8, 32, 128), F32),
            pltpu.VMEM((8, 32, 128), F32),
            pltpu.SemaphoreType.DMA((8,)),
            pltpu.SemaphoreType.DMA((14,)),
            pltpu.SemaphoreType.DMA((14,)),
        ],
        compiler_params=pltpu.CompilerParams(
            collective_id=0, has_side_effects=True, vmem_limit_bytes=62 << 20
        ),
        cost_estimate=pl.CostEstimate(flops=30_000_000_000, bytes_accessed=2_000_000, transcendentals=0),
    )(
        leaving.reshape(8, 8),
        leave_count.reshape(8),
        coriolis,
        winds.reshape(2 * ROWS, CX),
        rays.reshape(NB * 4, 128),
        ray_cell.reshape(NB, 128),
        ray_level.reshape(NB, 128),
        turning.reshape(NB, 128),
    )
    return (
        rays_new.reshape(rays.shape),
        arrived.reshape(1, 1, 8, 8, 4, 128),
        tendency.reshape(winds.shape),
    )


def solution(mesh):
    placed = (
        P(None, None, "lat", "lon"),
        P("lat"),
        P("lon", "lat", None, None, None),
        P("lon", "lat", None, None),
        P("lon", "lat", None, None),
        P("lon", "lat", None, None),
        P("lon", "lat", None, None),
        P("lon", "lat", None),
    )
    return jax.shard_map(
        on_device,
        mesh=mesh,
        in_specs=placed,
        out_specs=(
            P("lon", "lat", None, None, None),
            P("lon", "lat", None, None, None, None),
            P(None, None, "lat", "lon"),
        ),
        check_vma=False,
    )
```

```python
import jax
import jax.numpy as jnp
from jax import lax
from jax.experimental import pallas as pl
from jax.experimental.pallas import tpu as pltpu
from jax.sharding import PartitionSpec as P

STEP = 0.1
DIRS = ((0, 1), (0, -1), (1, 0), (-1, 0), (1, 1), (1, -1), (-1, 1), (-1, -1))
MESH = pl.DeviceIdType.MESH
LEV, CY, CX, NB = 12, 32, 128, 128
ROWS = LEV * CY
LOW = 128
LAG = 4
GRP = 8
SPAN = GRP * 128
STEPS = NB // GRP
UNIT = 5461.0
F32, BF16 = jnp.float32, jnp.bfloat16


def propagate(wave_k, wave_l, wave_m, action, sample, fcor, turn):
    new_k = wave_k - STEP * (wave_k * sample[0] + wave_l * sample[1])
    new_l = wave_l - STEP * (wave_k * sample[2] + wave_l * sample[3])
    new_m = wave_m - STEP * (wave_k * sample[4] + wave_l * sample[5])
    new_m = jnp.where(turn == 1, -new_m, new_m)
    horiz = new_k * new_k + new_l * new_l
    total = horiz + new_m * new_m + 1.0
    fsq = fcor * fcor
    freq2 = (horiz + fsq * (new_m * new_m + 1.0)) / total
    freq = jnp.sqrt(freq2)
    group_x = new_k * (1.0 - freq2) / (freq * total)
    group_z = new_m * (fsq - freq2) / (freq * total)
    return (
        new_k,
        new_l,
        new_m,
        group_z * new_k * action,
        group_z * new_l * action,
        group_x * new_k * action,
    )


def level_diff(field):
    zero = jnp.zeros((CY, CX), F32)
    upper = jnp.concatenate([field[CY:], zero], axis=0)
    lower = jnp.concatenate([zero, field[:-CY]], axis=0)
    return (upper - lower) * 0.5


def split(value):
    high = value.astype(BF16)
    return high, (value - high.astype(F32)).astype(BF16)


def pack(first, second):
    high = jnp.round(first * UNIT).astype(jnp.int32)
    low = jnp.round(second * UNIT).astype(jnp.int32)
    return high * 65536 + (low + 32768)


def unpack(word):
    high = lax.shift_right_arithmetic(word, 16)
    low = jnp.bitwise_and(word, 65535) - 32768
    return high.astype(F32) * (1.0 / UNIT), low.astype(F32) * (1.0 / UNIT)


def kernel(
    leaving_in, count_in, fcor_in, winds_in, rays_in, cell_in, level_in, turn_in,
    rays_out, arrived, tend,
    leaving, count, fcor, winds, rays, cell, level, turn,
    wind_t, table, words, lat_edge, lon_edge, fresh, hots, found, samples, fluxes, dep,
    lon_out, lon_in, lat_out, lat_in, edge_out, edge_in, box_out, box_in,
    load_sem, send_sem, recv_sem,
):
    loads = [
        pltpu.make_async_copy(src, dst, load_sem.at[i])
        for i, (src, dst) in enumerate(
            (
                (winds_in, winds),
                (cell_in, cell),
                (level_in, level),
                (rays_in, rays),
                (turn_in, turn),
                (fcor_in, fcor),
                (leaving_in, leaving),
                (count_in, count),
            )
        )
    ]
    for each in loads:
        each.start()
    lon, lat = lax.axis_index("lon"), lax.axis_index("lat")
    nlon, nlat = lax.axis_size("lon"), lax.axis_size("lat")

    def at(dlat, dlon):
        return (lax.rem(lon + dlon + nlon, nlon), lax.rem(lat + dlat + nlat, nlat))

    def copy(src, dst, which, where):
        return pltpu.make_async_remote_copy(
            src_ref=src, dst_ref=dst, send_sem=send_sem.at[which], recv_sem=recv_sem.at[which],
            device_id=at(*where), device_id_type=MESH,
        )

    barrier = pltpu.get_barrier_semaphore()
    for where in DIRS:
        pl.semaphore_signal(barrier, inc=1, device_id=at(*where), device_id_type=MESH)

    loads[0].wait()
    for w in range(2):
        flipped = winds[w * ROWS : (w + 1) * ROWS, :].T
        wind_t[w] = flipped
        lon_out[0, w : w + 1, :] = flipped[CX - 1 : CX, :]
        lon_out[1, w : w + 1, :] = flipped[0:1, :]
    for half in range(2):
        lon_out[half, 2:8, :] = jnp.zeros((6, ROWS), F32)
    lat_out[0] = winds[pl.ds(CY - 1, 2 * LEV, stride=CY), :]
    lat_out[1] = winds[pl.ds(0, 2 * LEV, stride=CY), :]
    pl.semaphore_wait(barrier, 8)
    halos = [
        copy(lon_out.at[0], lon_in.at[0], 0, (0, 1)),
        copy(lon_out.at[1], lon_in.at[1], 1, (0, -1)),
        copy(lat_out.at[0], lat_in.at[0], 2, (1, 0)),
        copy(lat_out.at[1], lat_in.at[1], 3, (-1, 0)),
    ]
    for each in halos:
        each.start()

    def keep(field, flipped):
        high, low = split(flipped)
        lines = slice(field * CX, (field + 1) * CX)
        table[lines, 0:LOW] = high[:, :LOW]
        table[lines, LOW : 2 * LOW] = low[:, :LOW]
        table[lines, 2 * LOW : ROWS + LOW] = high[:, LOW:]
        table[lines, ROWS + LOW : 2 * ROWS] = low[:, LOW:]

    for w in range(2):
        keep(w, level_diff(winds[w * ROWS : (w + 1) * ROWS, :]).T)
    column = lax.broadcasted_iota(jnp.int32, (CX, ROWS), 0)
    row = lax.rem(lax.broadcasted_iota(jnp.int32, (ROWS, CX), 0), CY)
    lane = lax.broadcasted_iota(jnp.int32, (ROWS, CX), 1)
    along, across = [], []
    for w in range(2):
        field = winds[w * ROWS : (w + 1) * ROWS, :]
        east = jnp.where(lane == CX - 1, 0.0, pltpu.roll(field, CX - 1, 1))
        west = jnp.where(lane == 0, 0.0, pltpu.roll(field, 1, 1))
        along.append((east - west) * 0.5)
        north = jnp.where(row == CY - 1, 0.0, pltpu.roll(field, ROWS - 1, 0))
        south = jnp.where(row == 0, 0.0, pltpu.roll(field, 1, 0))
        across.append((north - south) * 0.5)
    words[0] = pack(*along)
    words[1] = pack(*across)
    words[2] = pack(*[level_diff(winds[w * ROWS : (w + 1) * ROWS, :]) for w in range(2)])
    dep[...] = jnp.zeros((ROWS, 6 * CX), F32)
    for each in loads[1:]:
        each.wait()

    x_ids = lax.broadcasted_iota(jnp.int32, (CX, 128), 0)
    r_ids = lax.broadcasted_iota(jnp.int32, (ROWS, 128), 0)

    def blocks_of(c):
        return pl.ds(pl.multiple_of(c * GRP, GRP), GRP)

    def place(c):
        cells = cell[blocks_of(c), :]
        y = lax.shift_right_logical(cells, 7)
        return jnp.bitwise_and(cells, CX - 1), y, level[blocks_of(c), :] * CY + y

    def rise(c, whole):
        for i in range(GRP):
            cells = cell[pl.ds(c * GRP + i, 1), :]
            rows = level[pl.ds(c * GRP + i, 1), :] * CY + lax.shift_right_logical(cells, 7)
            hot = jnp.where(r_ids == rows, 1.0, 0.0).astype(BF16)
            fresh[:, i * 128 : (i + 1) * 128] = hot
            hots[c, :, i * 128 : (i + 1) * 128] = hot
        first, rest = fresh[:LOW, :], fresh[LOW:, :]
        picked = lax.dot_general(
            table[...] if whole else table[:, 2 * LOW :],
            jnp.concatenate([first, first, rest, rest] if whole else [rest, rest], axis=0),
            (((1,), (0,)), ((), ())),
            preferred_element_type=F32,
        )
        for i in range(GRP):
            mask = x_ids == jnp.bitwise_and(cell[pl.ds(c * GRP + i, 1), :], CX - 1)
            for f in range(2):
                part = picked[f * CX : (f + 1) * CX, i * 128 : (i + 1) * 128]
                samples[f, pl.ds(c * GRP + i, 1), :] = jnp.sum(
                    jnp.where(mask, part, 0.0), axis=0, keepdims=True
                )

    def pick(c, whole):
        x, _, rows = place(c)
        nought = jnp.full((GRP, 128), 32768, jnp.int32)
        got = [nought] * 3
        for r in range(ROWS):
            here = rows == r
            for w in range(2 if whole or r >= LOW else 3):
                line = jnp.broadcast_to(words[w, r : r + 1, :], (GRP, CX))
                taken = jnp.take_along_axis(line, x, axis=1, mode="promise_in_bounds")
                got[w] = jnp.where(here, taken, got[w])
        for w in range(3):
            found[w, blocks_of(c), :] = got[w]

    def advance(c):
        x, y, rows = place(c)
        levels = level[blocks_of(c), :]
        sample = [*unpack(found[0, blocks_of(c), :]), *unpack(found[1, blocks_of(c), :])]
        for f, value in enumerate(unpack(found[2, blocks_of(c), :])):
            sample.append(value + samples[f, blocks_of(c), :])
        lanes, tiles = jnp.bitwise_and(rows, 127), lax.shift_right_logical(rows, 7)
        nought = jnp.full((GRP, 128), 32768, jnp.int32)
        for side, end in ((0, 0), (1, CX - 1)):
            word = nought
            for t in range(ROWS // 128):
                line = jnp.broadcast_to(lon_edge[side, t : t + 1, :], (GRP, 128))
                taken = jnp.take_along_axis(line, lanes, axis=1, mode="promise_in_bounds")
                word = jnp.where(jnp.logical_and(tiles == t, x == end), taken, word)
            for f, value in enumerate(unpack(word)):
                sample[f] += value
        for side, end in ((0, 0), (1, CY - 1)):
            word = nought
            for z in range(LEV):
                line = jnp.broadcast_to(lat_edge[side, z : z + 1, :], (GRP, 128))
                taken = jnp.take_along_axis(line, x, axis=1, mode="promise_in_bounds")
                word = jnp.where(jnp.logical_and(levels == z, y == end), taken, word)
            for f, value in enumerate(unpack(word)):
                sample[2 + f] += value
        f_ray = jnp.zeros((GRP, 128), F32)
        for i in range(CY):
            f_ray = jnp.where(y == i, fcor[i], f_ray)
        fields = [rays[pl.ds(c * GRP * 4 + f, GRP, stride=4), :] for f in range(4)]
        out = propagate(*fields, sample, f_ray, turn[blocks_of(c), :])
        for f, value in enumerate((*out[:3], fields[3])):
            rays_out[pl.ds(c * GRP * 4 + f, GRP, stride=4), :] = value
        for j in range(3):
            high = out[3 + j].astype(BF16).astype(F32)
            fluxes[2 * j, blocks_of(c), :] = high
            fluxes[2 * j + 1, blocks_of(c), :] = out[3 + j] - high

    def scatter(js, c, hot):
        parts = []
        for i in range(len(hot) * GRP):
            at_row = pl.ds(c * GRP + i, 1)
            mask = x_ids == jnp.bitwise_and(cell[at_row, :], CX - 1)
            parts.append(
                jnp.concatenate(
                    [
                        jnp.where(mask, fluxes[2 * j + p, at_row, :], 0.0).astype(BF16)
                        for j in js
                        for p in range(2)
                    ],
                    axis=0,
                )
            )
        lanes = slice(js[0] * 2 * CX, (js[-1] + 1) * 2 * CX)
        dep[:, lanes] += lax.dot_general(
            jnp.concatenate(hot, axis=1), jnp.concatenate(parts, axis=1), (((1,), (1,)), ((), ())),
            preferred_element_type=F32,
        )

    def before(c, carry):
        rise(c, True)
        pick(c, True)
        return carry

    lax.fori_loop(0, LAG, before, 0)

    for each in halos:
        each.wait()
    for side, sign in ((0, -0.5), (1, 0.5)):
        ends = [lon_in[side, w : w + 1, :] * sign for w in range(2)]
        word = pack(*ends)
        for t in range(ROWS // 128):
            lon_edge[side, t : t + 1, :] = word[:, t * 128 : (t + 1) * 128]
        closed = lat == (0 if side == 0 else nlat - 1)
        lat_edge[side] = pack(
            *[jnp.where(closed, 0.0, lat_in[side, w * LEV : (w + 1) * LEV, :] * sign) for w in range(2)]
        )
    advance(0)

    def after(c, carry):
        scatter((0, 1, 2), c - LAG, [hots[c - LAG]])
        advance(c - LAG + 1)
        pick(c, False)
        rise(c, False)
        return carry

    lax.fori_loop(LAG, STEPS, after, 0)
    lax.fori_loop(STEPS - LAG + 1, STEPS, lambda c, carry: (advance(c), carry)[1], 0)

    boxes = []
    for d, where in enumerate(DIRS):
        for slot in range(8):
            block = rays_out[pl.ds(leaving[d, slot] * 4, 4), :]
            box_out[d, slot * 4 : slot * 4 + 4, :] = jnp.where(slot < count[d], block, 0.0)
        boxes.append(copy(box_out.at[d], box_in.at[d], 4 + d, where))
        boxes[-1].start()

    def deposit(j):
        return dep[:, j * 2 * CX : j * 2 * CX + CX] + dep[:, j * 2 * CX + CX : (j + 1) * 2 * CX]


    def last(js, first, count):
        def step(c, carry):
            scatter(js, first + 2 * c, [hots[first + 2 * c], hots[first + 2 * c + 1]])
            return carry

        lax.fori_loop(0, count // 2, step, 0)

    last((2,), STEPS - LAG, LAG)
    zonal = deposit(2).T
    wind_t[0] = zonal
    for half in range(2):
        edge_out[half] = jnp.zeros((8, ROWS), F32)
    edge_out[0, 0:1, :] = zonal[CX - 1 : CX, :]
    edge_out[1, 0:1, :] = zonal[0:1, :]
    edges = [
        copy(edge_out.at[0], edge_in.at[0], 12, (0, 1)),
        copy(edge_out.at[1], edge_in.at[1], 13, (0, -1)),
    ]
    for each in edges:
        each.start()
    last((0, 1), STEPS - LAG, LAG)
    tend[ROWS : 2 * ROWS, :] = -level_diff(deposit(1))
    for each in edges:
        each.wait()
    zonal = wind_t[0]
    east = jnp.where(column == CX - 1, edge_in[1, 0:1, :], pltpu.roll(zonal, CX - 1, 0))
    west = jnp.where(column == 0, edge_in[0, 0:1, :], pltpu.roll(zonal, 1, 0))
    tend[0:ROWS, :] = -level_diff(deposit(0)) - ((east - west) * 0.5).T
    for each in boxes:
        each.wait()
    arrived[...] = box_in[...]


def on_device(winds, coriolis, rays, ray_cell, ray_level, turning, leaving, leave_count):
    vmem = pl.BlockSpec(memory_space=pltpu.VMEM)
    hbm = pl.BlockSpec(memory_space=pltpu.HBM)
    rays_new, arrived, tendency = pl.pallas_call(
        kernel,
        out_shape=(
            jax.ShapeDtypeStruct((NB * 4, 128), F32),
            jax.ShapeDtypeStruct((8, 32, 128), F32),
            jax.ShapeDtypeStruct((2 * ROWS, CX), F32),
        ),
        in_specs=[hbm] * 8,
        out_specs=(vmem, vmem, vmem),
        scratch_shapes=[
            pltpu.SMEM((8, 8), jnp.int32),
            pltpu.SMEM((8,), jnp.int32),
            pltpu.SMEM((32,), F32),
            pltpu.VMEM((2 * ROWS, CX), F32),
            pltpu.VMEM((NB * 4, 128), F32),
            pltpu.VMEM((NB, 128), jnp.int32),
            pltpu.VMEM((NB, 128), jnp.int32),
            pltpu.VMEM((NB, 128), jnp.int32),
            pltpu.VMEM((2, CX, ROWS), F32),
            pltpu.VMEM((2 * CX, 2 * ROWS), BF16),
            pltpu.VMEM((3, ROWS, CX), jnp.int32),
            pltpu.VMEM((2, LEV, CX), jnp.int32),
            pltpu.VMEM((2, ROWS // 128, 128), jnp.int32),
            pltpu.VMEM((ROWS, SPAN), BF16),
            pltpu.VMEM((STEPS, ROWS, SPAN), BF16),
            pltpu.VMEM((3, NB, 128), jnp.int32),
            pltpu.VMEM((2, NB, 128), F32),
            pltpu.VMEM((6, NB, 128), F32),
            pltpu.VMEM((ROWS, 6 * CX), F32),
            pltpu.VMEM((2, 8, ROWS), F32),
            pltpu.VMEM((2, 8, ROWS), F32),
            pltpu.VMEM((2, 2 * LEV, CX), F32),
            pltpu.VMEM((2, 2 * LEV, CX), F32),
            pltpu.VMEM((2, 8, ROWS), F32),
            pltpu.VMEM((2, 8, ROWS), F32),
            pltpu.VMEM((8, 32, 128), F32),
            pltpu.VMEM((8, 32, 128), F32),
            pltpu.SemaphoreType.DMA((8,)),
            pltpu.SemaphoreType.DMA((14,)),
            pltpu.SemaphoreType.DMA((14,)),
        ],
        compiler_params=pltpu.CompilerParams(
            collective_id=0, has_side_effects=True, vmem_limit_bytes=62 << 20
        ),
        cost_estimate=pl.CostEstimate(flops=30_000_000_000, bytes_accessed=2_000_000, transcendentals=0),
    )(
        leaving.reshape(8, 8),
        leave_count.reshape(8),
        coriolis,
        winds.reshape(2 * ROWS, CX),
        rays.reshape(NB * 4, 128),
        ray_cell.reshape(NB, 128),
        ray_level.reshape(NB, 128),
        turning.reshape(NB, 128),
    )
    return (
        rays_new.reshape(rays.shape),
        arrived.reshape(1, 1, 8, 8, 4, 128),
        tendency.reshape(winds.shape),
    )


def solution(mesh):
    placed = (
        P(None, None, "lat", "lon"),
        P("lat"),
        P("lon", "lat", None, None, None),
        P("lon", "lat", None, None),
        P("lon", "lat", None, None),
        P("lon", "lat", None, None),
        P("lon", "lat", None, None),
        P("lon", "lat", None),
    )
    return jax.shard_map(
        on_device,
        mesh=mesh,
        in_specs=placed,
        out_specs=(
            P("lon", "lat", None, None, None),
            P("lon", "lat", None, None, None, None),
            P(None, None, "lat", "lon"),
        ),
        check_vma=False,
    )
```

```python
import jax
import jax.numpy as jnp
from jax import lax
from jax.experimental import pallas as pl
from jax.experimental.pallas import tpu as pltpu
from jax.sharding import PartitionSpec as P

STEP = 0.1
DIRS = ((0, 1), (0, -1), (1, 0), (-1, 0), (1, 1), (1, -1), (-1, 1), (-1, -1))
MESH = pl.DeviceIdType.MESH
LEV, CY, CX, NB = 12, 32, 128, 128
ROWS = LEV * CY
LAG = 8
GREET = 3
GRP = 8
SPAN = GRP * 128
STEPS = NB // GRP
UNIT = 5461.0
F32, BF16 = jnp.float32, jnp.bfloat16


def propagate(wave_k, wave_l, wave_m, action, sample, fcor, turn):
    new_k = wave_k - STEP * (wave_k * sample[0] + wave_l * sample[1])
    new_l = wave_l - STEP * (wave_k * sample[2] + wave_l * sample[3])
    new_m = wave_m - STEP * (wave_k * sample[4] + wave_l * sample[5])
    new_m = jnp.where(turn == 1, -new_m, new_m)
    horiz = new_k * new_k + new_l * new_l
    total = horiz + new_m * new_m + 1.0
    fsq = fcor * fcor
    freq2 = (horiz + fsq * (new_m * new_m + 1.0)) / total
    freq = jnp.sqrt(freq2)
    group_x = new_k * (1.0 - freq2) / (freq * total)
    group_z = new_m * (fsq - freq2) / (freq * total)
    return (
        new_k,
        new_l,
        new_m,
        group_z * new_k * action,
        group_z * new_l * action,
        group_x * new_k * action,
    )


def level_diff(field):
    zero = jnp.zeros((CY, CX), F32)
    upper = jnp.concatenate([field[CY:], zero], axis=0)
    lower = jnp.concatenate([zero, field[:-CY]], axis=0)
    return (upper - lower) * 0.5


def split(value):
    high = value.astype(BF16)
    return high, (value - high.astype(F32)).astype(BF16)


def pack(first, second):
    high = jnp.round(first * UNIT).astype(jnp.int32)
    low = jnp.round(second * UNIT).astype(jnp.int32)
    return high * 65536 + (low + 32768)


def unpack(word):
    high = lax.shift_right_arithmetic(word, 16)
    low = jnp.bitwise_and(word, 65535) - 32768
    return high.astype(F32) * (1.0 / UNIT), low.astype(F32) * (1.0 / UNIT)


def kernel(
    leaving_in, count_in, fcor_in, winds_in, rays_in, cell_in, level_in, turn_in,
    rays_out, arrived, tend,
    leaving, count, fcor, winds, rays, cell, level, turn,
    wind_t, table, words, lat_edge, lon_edge, fresh, hots, found, samples, fluxes, dep,
    lon_out, lon_in, lat_out, lat_in, edge_out, edge_in, box_out, box_in,
    load_sem, send_sem, recv_sem,
):
    loads = [
        pltpu.make_async_copy(src, dst, load_sem.at[i])
        for i, (src, dst) in enumerate(
            (
                (winds_in, winds),
                (cell_in, cell),
                (level_in, level),
                (rays_in, rays),
                (turn_in, turn),
                (fcor_in, fcor),
                (leaving_in, leaving),
                (count_in, count),
            )
        )
    ]
    for each in loads:
        each.start()
    lon, lat = lax.axis_index("lon"), lax.axis_index("lat")
    nlon, nlat = lax.axis_size("lon"), lax.axis_size("lat")

    def at(dlat, dlon):
        return (lax.rem(lon + dlon + nlon, nlon), lax.rem(lat + dlat + nlat, nlat))

    def copy(src, dst, which, where):
        return pltpu.make_async_remote_copy(
            src_ref=src, dst_ref=dst, send_sem=send_sem.at[which], recv_sem=recv_sem.at[which],
            device_id=at(*where), device_id_type=MESH,
        )

    barrier = pltpu.get_barrier_semaphore()
    for where in DIRS:
        pl.semaphore_signal(barrier, inc=1, device_id=at(*where), device_id_type=MESH)

    loads[0].wait()
    for w in range(2):
        flipped = winds[w * ROWS : (w + 1) * ROWS, :].T
        wind_t[w] = flipped
        lon_out[0, w : w + 1, :] = flipped[CX - 1 : CX, :]
        lon_out[1, w : w + 1, :] = flipped[0:1, :]
    for half in range(2):
        lon_out[half, 2:8, :] = jnp.zeros((6, ROWS), F32)
    lat_out[0] = winds[pl.ds(CY - 1, 2 * LEV, stride=CY), :]
    lat_out[1] = winds[pl.ds(0, 2 * LEV, stride=CY), :]
    halos = [
        copy(lon_out.at[0], lon_in.at[0], 0, (0, 1)),
        copy(lon_out.at[1], lon_in.at[1], 1, (0, -1)),
        copy(lat_out.at[0], lat_in.at[0], 2, (1, 0)),
        copy(lat_out.at[1], lat_in.at[1], 3, (-1, 0)),
    ]
    def keep(field, flipped):
        high, low = split(flipped)
        table[field * CX : (field + 1) * CX, 0:ROWS] = high
        table[field * CX : (field + 1) * CX, ROWS : 2 * ROWS] = low

    for w in range(2):
        keep(w, level_diff(winds[w * ROWS : (w + 1) * ROWS, :]).T)
    column = lax.broadcasted_iota(jnp.int32, (CX, ROWS), 0)
    row = lax.rem(lax.broadcasted_iota(jnp.int32, (ROWS, CX), 0), CY)
    lane = lax.broadcasted_iota(jnp.int32, (ROWS, CX), 1)
    along, across = [], []
    for w in range(2):
        field = winds[w * ROWS : (w + 1) * ROWS, :]
        east = jnp.where(lane == CX - 1, 0.0, pltpu.roll(field, CX - 1, 1))
        west = jnp.where(lane == 0, 0.0, pltpu.roll(field, 1, 1))
        along.append((east - west) * 0.5)
        north = jnp.where(row == CY - 1, 0.0, pltpu.roll(field, ROWS - 1, 0))
        south = jnp.where(row == 0, 0.0, pltpu.roll(field, 1, 0))
        across.append((north - south) * 0.5)
    words[0] = pack(*along)
    words[1] = pack(*across)
    dep[...] = jnp.zeros((ROWS, 6 * CX), F32)
    for each in loads[1:]:
        each.wait()

    x_ids = lax.broadcasted_iota(jnp.int32, (CX, 128), 0)
    r_ids = lax.broadcasted_iota(jnp.int32, (ROWS, 128), 0)

    def blocks_of(c):
        return pl.ds(pl.multiple_of(c * GRP, GRP), GRP)

    def place(c):
        cells = cell[blocks_of(c), :]
        y = lax.shift_right_logical(cells, 7)
        return jnp.bitwise_and(cells, CX - 1), y, level[blocks_of(c), :] * CY + y

    def rise(c, at):
        for i in range(GRP):
            cells = cell[pl.ds(c * GRP + i, 1), :]
            rows = level[pl.ds(c * GRP + i, 1), :] * CY + lax.shift_right_logical(cells, 7)
            hot = jnp.where(r_ids == rows, 1.0, 0.0).astype(BF16)
            fresh[at, :, i * 128 : (i + 1) * 128] = hot
            hots[c, :, i * 128 : (i + 1) * 128] = hot
        hot = fresh[at]
        picked = lax.dot_general(
            table[...], jnp.concatenate([hot, hot], axis=0), (((1,), (0,)), ((), ())),
            preferred_element_type=F32,
        )
        for i in range(GRP):
            mask = x_ids == jnp.bitwise_and(cell[pl.ds(c * GRP + i, 1), :], CX - 1)
            for f in range(2):
                part = picked[f * CX : (f + 1) * CX, i * 128 : (i + 1) * 128]
                samples[f, pl.ds(c * GRP + i, 1), :] = jnp.sum(
                    jnp.where(mask, part, 0.0), axis=0, keepdims=True
                )

    def pick(c):
        x, _, rows = place(c)
        got = [jnp.zeros((GRP, 128), jnp.int32)] * 2
        for r in range(ROWS):
            here = rows == r
            for w in range(2):
                line = jnp.broadcast_to(words[w, r : r + 1, :], (GRP, CX))
                taken = jnp.take_along_axis(line, x, axis=1, mode="promise_in_bounds")
                got[w] = jnp.where(here, taken, got[w])
        for w in range(2):
            found[w, blocks_of(c), :] = got[w]

    def advance(c):
        x, y, rows = place(c)
        levels = level[blocks_of(c), :]
        sample = [*unpack(found[0, blocks_of(c), :]), *unpack(found[1, blocks_of(c), :])]
        sample += [samples[0, blocks_of(c), :], samples[1, blocks_of(c), :]]
        lanes, tiles = jnp.bitwise_and(rows, 127), lax.shift_right_logical(rows, 7)
        nought = jnp.full((GRP, 128), 32768, jnp.int32)
        for side, end in ((0, 0), (1, CX - 1)):
            word = nought
            for t in range(ROWS // 128):
                line = jnp.broadcast_to(lon_edge[side, t : t + 1, :], (GRP, 128))
                taken = jnp.take_along_axis(line, lanes, axis=1, mode="promise_in_bounds")
                word = jnp.where(jnp.logical_and(tiles == t, x == end), taken, word)
            for f, value in enumerate(unpack(word)):
                sample[f] += value
        for side, end in ((0, 0), (1, CY - 1)):
            word = nought
            for z in range(LEV):
                line = jnp.broadcast_to(lat_edge[side, z : z + 1, :], (GRP, 128))
                taken = jnp.take_along_axis(line, x, axis=1, mode="promise_in_bounds")
                word = jnp.where(jnp.logical_and(levels == z, y == end), taken, word)
            for f, value in enumerate(unpack(word)):
                sample[2 + f] += value
        f_ray = jnp.zeros((GRP, 128), F32)
        for i in range(CY):
            f_ray = jnp.where(y == i, fcor[i], f_ray)
        fields = [rays[pl.ds(c * GRP * 4 + f, GRP, stride=4), :] for f in range(4)]
        out = propagate(*fields, sample, f_ray, turn[blocks_of(c), :])
        for f, value in enumerate((*out[:3], fields[3])):
            rays_out[pl.ds(c * GRP * 4 + f, GRP, stride=4), :] = value
        for j in range(3):
            high = out[3 + j].astype(BF16).astype(F32)
            fluxes[2 * j, blocks_of(c), :] = high
            fluxes[2 * j + 1, blocks_of(c), :] = out[3 + j] - high

    def scatter(js, c, hot):
        parts = []
        for i in range(len(hot) * GRP):
            at_row = pl.ds(c * GRP + i, 1)
            mask = x_ids == jnp.bitwise_and(cell[at_row, :], CX - 1)
            parts.append(
                jnp.concatenate(
                    [
                        jnp.where(mask, fluxes[2 * j + p, at_row, :], 0.0).astype(BF16)
                        for j in js
                        for p in range(2)
                    ],
                    axis=0,
                )
            )
        lanes = slice(js[0] * 2 * CX, (js[-1] + 1) * 2 * CX)
        dep[:, lanes] += lax.dot_general(
            jnp.concatenate(hot, axis=1), jnp.concatenate(parts, axis=1), (((1,), (1,)), ((), ())),
            preferred_element_type=F32,
        )

    def before(c, carry):
        @pl.when(c == GREET)
        def _():
            pl.semaphore_wait(barrier, 8)
            for each in halos:
                each.start()

        rise(2 * c, 0)
        rise(2 * c + 1, 1)
        pick(c)
        return carry

    lax.fori_loop(0, LAG, before, 0)

    for each in halos:
        each.wait()
    for side, sign in ((0, -0.5), (1, 0.5)):
        ends = [lon_in[side, w : w + 1, :] * sign for w in range(2)]
        word = pack(*ends)
        for t in range(ROWS // 128):
            lon_edge[side, t : t + 1, :] = word[:, t * 128 : (t + 1) * 128]
        closed = lat == (0 if side == 0 else nlat - 1)
        lat_edge[side] = pack(
            *[jnp.where(closed, 0.0, lat_in[side, w * LEV : (w + 1) * LEV, :] * sign) for w in range(2)]
        )
    advance(0)

    def after(c, carry):
        scatter((0, 1, 2), c - LAG, [hots[c - LAG]])
        advance(c - LAG + 1)
        pick(c)
        return carry

    lax.fori_loop(LAG, STEPS, after, 0)

    def finish(c, carry):
        scatter((2,), c, [hots[c]])
        advance(c + 1)
        return carry

    lax.fori_loop(STEPS - LAG, STEPS - 1, finish, 0)

    boxes = []
    for d, where in enumerate(DIRS):
        for slot in range(8):
            block = rays_out[pl.ds(leaving[d, slot] * 4, 4), :]
            box_out[d, slot * 4 : slot * 4 + 4, :] = jnp.where(slot < count[d], block, 0.0)
        boxes.append(copy(box_out.at[d], box_in.at[d], 4 + d, where))
        boxes[-1].start()

    def deposit(j):
        return dep[:, j * 2 * CX : j * 2 * CX + CX] + dep[:, j * 2 * CX + CX : (j + 1) * 2 * CX]


    def last(js, first, count):
        def step(c, carry):
            scatter(js, first + 2 * c, [hots[first + 2 * c], hots[first + 2 * c + 1]])
            return carry

        lax.fori_loop(0, count // 2, step, 0)

    scatter((2,), STEPS - 1, [hots[STEPS - 1]])
    zonal = deposit(2).T
    wind_t[0] = zonal
    for half in range(2):
        edge_out[half] = jnp.zeros((8, ROWS), F32)
    edge_out[0, 0:1, :] = zonal[CX - 1 : CX, :]
    edge_out[1, 0:1, :] = zonal[0:1, :]
    edges = [
        copy(edge_out.at[0], edge_in.at[0], 12, (0, 1)),
        copy(edge_out.at[1], edge_in.at[1], 13, (0, -1)),
    ]
    for each in edges:
        each.start()
    last((0, 1), STEPS - LAG, LAG)
    tend[ROWS : 2 * ROWS, :] = -level_diff(deposit(1))
    for each in edges:
        each.wait()
    zonal = wind_t[0]
    east = jnp.where(column == CX - 1, edge_in[1, 0:1, :], pltpu.roll(zonal, CX - 1, 0))
    west = jnp.where(column == 0, edge_in[0, 0:1, :], pltpu.roll(zonal, 1, 0))
    tend[0:ROWS, :] = -level_diff(deposit(0)) - ((east - west) * 0.5).T
    for each in boxes:
        each.wait()
    arrived[...] = box_in[...]


def deliver(*refs):
    ins, outs, held, sem_in, sem_out = refs[:3], refs[3:6], refs[6:9], refs[9], refs[10]
    loads = [pltpu.make_async_copy(ins[i], held[i], sem_in.at[i]) for i in range(3)]
    stores = [pltpu.make_async_copy(held[i], outs[i], sem_out.at[i]) for i in range(3)]
    for each in loads:
        each.start()
    for load, store in zip(loads, stores):
        load.wait()
        store.start()
    for each in stores:
        each.wait()


def on_device(winds, coriolis, rays, ray_cell, ray_level, turning, leaving, leave_count):
    vmem = pl.BlockSpec(memory_space=pltpu.VMEM)
    hbm = pl.BlockSpec(memory_space=pltpu.HBM)
    rays_new, arrived, tendency = pl.pallas_call(
        kernel,
        out_shape=(
            jax.ShapeDtypeStruct((NB * 4, 128), F32),
            jax.ShapeDtypeStruct((8, 32, 128), F32),
            jax.ShapeDtypeStruct((2 * ROWS, CX), F32),
        ),
        in_specs=[hbm] * 8,
        out_specs=(vmem, vmem, vmem),
        scratch_shapes=[
            pltpu.SMEM((8, 8), jnp.int32),
            pltpu.SMEM((8,), jnp.int32),
            pltpu.SMEM((32,), F32),
            pltpu.VMEM((2 * ROWS, CX), F32),
            pltpu.VMEM((NB * 4, 128), F32),
            pltpu.VMEM((NB, 128), jnp.int32),
            pltpu.VMEM((NB, 128), jnp.int32),
            pltpu.VMEM((NB, 128), jnp.int32),
            pltpu.VMEM((2, CX, ROWS), F32),
            pltpu.VMEM((2 * CX, 2 * ROWS), BF16),
            pltpu.VMEM((2, ROWS, CX), jnp.int32),
            pltpu.VMEM((2, LEV, CX), jnp.int32),
            pltpu.VMEM((2, ROWS // 128, 128), jnp.int32),
            pltpu.VMEM((2, ROWS, SPAN), BF16),
            pltpu.VMEM((STEPS, ROWS, SPAN), BF16),
            pltpu.VMEM((2, NB, 128), jnp.int32),
            pltpu.VMEM((2, NB, 128), F32),
            pltpu.VMEM((6, NB, 128), F32),
            pltpu.VMEM((ROWS, 6 * CX), F32),
            pltpu.VMEM((2, 8, ROWS), F32),
            pltpu.VMEM((2, 8, ROWS), F32),
            pltpu.VMEM((2, 2 * LEV, CX), F32),
            pltpu.VMEM((2, 2 * LEV, CX), F32),
            pltpu.VMEM((2, 8, ROWS), F32),
            pltpu.VMEM((2, 8, ROWS), F32),
            pltpu.VMEM((8, 32, 128), F32),
            pltpu.VMEM((8, 32, 128), F32),
            pltpu.SemaphoreType.DMA((8,)),
            pltpu.SemaphoreType.DMA((14,)),
            pltpu.SemaphoreType.DMA((14,)),
        ],
        compiler_params=pltpu.CompilerParams(
            collective_id=0, has_side_effects=True, vmem_limit_bytes=62 << 20
        ),
        cost_estimate=pl.CostEstimate(flops=30_000_000_000, bytes_accessed=2_000_000, transcendentals=0),
    )(
        leaving.reshape(8, 8),
        leave_count.reshape(8),
        coriolis,
        winds.reshape(2 * ROWS, CX),
        rays.reshape(NB * 4, 128),
        ray_cell.reshape(NB, 128),
        ray_level.reshape(NB, 128),
        turning.reshape(NB, 128),
    )
    hbm = pl.BlockSpec(memory_space=pltpu.HBM)
    rays_new, arrived, tendency = pl.pallas_call(
        deliver,
        out_shape=tuple(jax.ShapeDtypeStruct(each.shape, F32) for each in (rays_new, arrived, tendency)),
        in_specs=[hbm] * 3,
        out_specs=(hbm,) * 3,
        scratch_shapes=[pltpu.VMEM(each.shape, F32) for each in (rays_new, arrived, tendency)]
        + [pltpu.SemaphoreType.DMA((3,)), pltpu.SemaphoreType.DMA((3,))],
        compiler_params=pltpu.CompilerParams(vmem_limit_bytes=62 << 20),
    )(rays_new, arrived, tendency)
    return (
        rays_new.reshape(rays.shape),
        arrived.reshape(1, 1, 8, 8, 4, 128),
        tendency.reshape(winds.shape),
    )


def solution(mesh):
    placed = (
        P(None, None, "lat", "lon"),
        P("lat"),
        P("lon", "lat", None, None, None),
        P("lon", "lat", None, None),
        P("lon", "lat", None, None),
        P("lon", "lat", None, None),
        P("lon", "lat", None, None),
        P("lon", "lat", None),
    )
    return jax.shard_map(
        on_device,
        mesh=mesh,
        in_specs=placed,
        out_specs=(
            P("lon", "lat", None, None, None),
            P("lon", "lat", None, None, None, None),
            P(None, None, "lat", "lon"),
        ),
        check_vma=False,
    )
```

```python
import jax
import jax.numpy as jnp
from jax import lax
from jax.experimental import pallas as pl
from jax.experimental.pallas import tpu as pltpu
from jax.sharding import PartitionSpec as P

STEP = 0.1
DIRS = ((0, 1), (0, -1), (1, 0), (-1, 0), (1, 1), (1, -1), (-1, 1), (-1, -1))
MESH = pl.DeviceIdType.MESH
LEV, CY, CX, NB = 12, 32, 128, 128
ROWS = LEV * CY
LAG = 8
GREET = 4
GRP = 8
SPAN = GRP * 128
HALF = SPAN // 2
STEPS = NB // GRP
UNIT = 5461.0
F32, BF16 = jnp.float32, jnp.bfloat16


def propagate(wave_k, wave_l, wave_m, action, sample, fcor, turn):
    new_k = wave_k - STEP * (wave_k * sample[0] + wave_l * sample[1])
    new_l = wave_l - STEP * (wave_k * sample[2] + wave_l * sample[3])
    new_m = wave_m - STEP * (wave_k * sample[4] + wave_l * sample[5])
    new_m = jnp.where(turn == 1, -new_m, new_m)
    horiz = new_k * new_k + new_l * new_l
    total = horiz + new_m * new_m + 1.0
    fsq = fcor * fcor
    freq2 = (horiz + fsq * (new_m * new_m + 1.0)) / total
    freq = jnp.sqrt(freq2)
    group_x = new_k * (1.0 - freq2) / (freq * total)
    group_z = new_m * (fsq - freq2) / (freq * total)
    return (
        new_k,
        new_l,
        new_m,
        group_z * new_k * action,
        group_z * new_l * action,
        group_x * new_k * action,
    )


def level_diff(field):
    zero = jnp.zeros((CY, CX), F32)
    upper = jnp.concatenate([field[CY:], zero], axis=0)
    lower = jnp.concatenate([zero, field[:-CY]], axis=0)
    return (upper - lower) * 0.5


def split(value):
    high = value.astype(BF16)
    return high, (value - high.astype(F32)).astype(BF16)


def pack(first, second):
    high = jnp.round(first * UNIT).astype(jnp.int32)
    low = jnp.round(second * UNIT).astype(jnp.int32)
    return high * 65536 + (low + 32768)


def unpack(word):
    high = lax.shift_right_arithmetic(word, 16)
    low = jnp.bitwise_and(word, 65535) - 32768
    return high.astype(F32) * (1.0 / UNIT), low.astype(F32) * (1.0 / UNIT)


def kernel(
    leaving_in, count_in, fcor_in, winds_in, rays_in, cell_in, level_in, turn_in,
    rays_new, arrived, tendency,
    rays_out, tend, leaving, count, fcor, winds, rays, cell, level, turn,
    wind_t, table, words, lat_edge, lon_edge, fresh, hots, found, samples, fluxes, dep,
    lon_out, lon_in, lat_out, lat_in, edge_out, edge_in, box_out,
    load_sem, store_sem, send_sem, recv_sem,
):
    loads = [
        pltpu.make_async_copy(src, dst, load_sem.at[i])
        for i, (src, dst) in enumerate(
            (
                (winds_in, winds),
                (cell_in, cell),
                (level_in, level),
                (rays_in, rays),
                (turn_in, turn),
                (fcor_in, fcor),
                (leaving_in, leaving),
                (count_in, count),
            )
        )
    ]
    for each in loads:
        each.start()
    lon, lat = lax.axis_index("lon"), lax.axis_index("lat")
    nlon, nlat = lax.axis_size("lon"), lax.axis_size("lat")

    def at(dlat, dlon):
        return (lax.rem(lon + dlon + nlon, nlon), lax.rem(lat + dlat + nlat, nlat))

    def copy(src, dst, which, where):
        return pltpu.make_async_remote_copy(
            src_ref=src, dst_ref=dst, send_sem=send_sem.at[which], recv_sem=recv_sem.at[which],
            device_id=at(*where), device_id_type=MESH,
        )

    barrier = pltpu.get_barrier_semaphore()
    for where in DIRS:
        pl.semaphore_signal(barrier, inc=1, device_id=at(*where), device_id_type=MESH)

    loads[0].wait()
    for w in range(2):
        flipped = winds[w * ROWS : (w + 1) * ROWS, :].T
        wind_t[w] = flipped
        lon_out[0, w : w + 1, :] = flipped[CX - 1 : CX, :]
        lon_out[1, w : w + 1, :] = flipped[0:1, :]
    for half in range(2):
        lon_out[half, 2:8, :] = jnp.zeros((6, ROWS), F32)
    lat_out[0] = winds[pl.ds(CY - 1, 2 * LEV, stride=CY), :]
    lat_out[1] = winds[pl.ds(0, 2 * LEV, stride=CY), :]
    halos = [
        copy(lon_out.at[0], lon_in.at[0], 0, (0, 1)),
        copy(lon_out.at[1], lon_in.at[1], 1, (0, -1)),
        copy(lat_out.at[0], lat_in.at[0], 2, (1, 0)),
        copy(lat_out.at[1], lat_in.at[1], 3, (-1, 0)),
    ]
    def keep(field, flipped):
        high, low = split(flipped)
        table[field * CX : (field + 1) * CX, 0:ROWS] = high
        table[field * CX : (field + 1) * CX, ROWS : 2 * ROWS] = low

    for w in range(2):
        keep(w, level_diff(winds[w * ROWS : (w + 1) * ROWS, :]).T)
    column = lax.broadcasted_iota(jnp.int32, (CX, ROWS), 0)
    row = lax.rem(lax.broadcasted_iota(jnp.int32, (ROWS, CX), 0), CY)
    lane = lax.broadcasted_iota(jnp.int32, (ROWS, CX), 1)
    along, across = [], []
    for w in range(2):
        field = winds[w * ROWS : (w + 1) * ROWS, :]
        east = jnp.where(lane == CX - 1, 0.0, pltpu.roll(field, CX - 1, 1))
        west = jnp.where(lane == 0, 0.0, pltpu.roll(field, 1, 1))
        along.append((east - west) * 0.5)
        north = jnp.where(row == CY - 1, 0.0, pltpu.roll(field, ROWS - 1, 0))
        south = jnp.where(row == 0, 0.0, pltpu.roll(field, 1, 0))
        across.append((north - south) * 0.5)
    words[0] = pack(*along)
    words[1] = pack(*across)
    dep[...] = jnp.zeros((ROWS, 6 * CX), F32)
    for each in loads[1:]:
        each.wait()

    x_ids = lax.broadcasted_iota(jnp.int32, (CX, 128), 0)
    r_ids = lax.broadcasted_iota(jnp.int32, (ROWS, 128), 0)

    def blocks_of(c):
        return pl.ds(pl.multiple_of(c * GRP, GRP), GRP)

    def place(c):
        cells = cell[blocks_of(c), :]
        y = lax.shift_right_logical(cells, 7)
        return jnp.bitwise_and(cells, CX - 1), y, level[blocks_of(c), :] * CY + y

    def rise(h, halves, at):
        first = h * (GRP // 2)
        for i in range(halves * GRP // 2):
            cells = cell[pl.ds(first + i, 1), :]
            rows = level[pl.ds(first + i, 1), :] * CY + lax.shift_right_logical(cells, 7)
            hot = jnp.where(r_ids == rows, 1.0, 0.0).astype(BF16)
            fresh[at, :, i * 128 : (i + 1) * 128] = hot
            lanes = slice(i % (GRP // 2) * 128, (i % (GRP // 2) + 1) * 128)
            hots[h + i // (GRP // 2), :, lanes] = hot
        hot = fresh[at, :, : halves * HALF]
        picked = lax.dot_general(
            table[...], jnp.concatenate([hot, hot], axis=0), (((1,), (0,)), ((), ())),
            preferred_element_type=F32,
        )
        for i in range(halves * GRP // 2):
            mask = x_ids == jnp.bitwise_and(cell[pl.ds(first + i, 1), :], CX - 1)
            for f in range(2):
                part = picked[f * CX : (f + 1) * CX, i * 128 : (i + 1) * 128]
                samples[f, pl.ds(first + i, 1), :] = jnp.sum(
                    jnp.where(mask, part, 0.0), axis=0, keepdims=True
                )

    def pick(c):
        x, _, rows = place(c)
        got = [jnp.zeros((GRP, 128), jnp.int32)] * 2
        for r in range(ROWS):
            here = rows == r
            for w in range(2):
                line = jnp.broadcast_to(words[w, r : r + 1, :], (GRP, CX))
                taken = jnp.take_along_axis(line, x, axis=1, mode="promise_in_bounds")
                got[w] = jnp.where(here, taken, got[w])
        for w in range(2):
            found[w, blocks_of(c), :] = got[w]

    def advance(c):
        x, y, rows = place(c)
        levels = level[blocks_of(c), :]
        sample = [*unpack(found[0, blocks_of(c), :]), *unpack(found[1, blocks_of(c), :])]
        sample += [samples[0, blocks_of(c), :], samples[1, blocks_of(c), :]]
        lanes, tiles = jnp.bitwise_and(rows, 127), lax.shift_right_logical(rows, 7)
        nought = jnp.full((GRP, 128), 32768, jnp.int32)
        for side, end in ((0, 0), (1, CX - 1)):
            word = nought
            for t in range(ROWS // 128):
                line = jnp.broadcast_to(lon_edge[side, t : t + 1, :], (GRP, 128))
                taken = jnp.take_along_axis(line, lanes, axis=1, mode="promise_in_bounds")
                word = jnp.where(jnp.logical_and(tiles == t, x == end), taken, word)
            for f, value in enumerate(unpack(word)):
                sample[f] += value
        for side, end in ((0, 0), (1, CY - 1)):
            word = nought
            for z in range(LEV):
                line = jnp.broadcast_to(lat_edge[side, z : z + 1, :], (GRP, 128))
                taken = jnp.take_along_axis(line, x, axis=1, mode="promise_in_bounds")
                word = jnp.where(jnp.logical_and(levels == z, y == end), taken, word)
            for f, value in enumerate(unpack(word)):
                sample[2 + f] += value
        f_ray = jnp.zeros((GRP, 128), F32)
        for i in range(CY):
            f_ray = jnp.where(y == i, fcor[i], f_ray)
        fields = [rays[pl.ds(c * GRP * 4 + f, GRP, stride=4), :] for f in range(4)]
        out = propagate(*fields, sample, f_ray, turn[blocks_of(c), :])
        for f, value in enumerate((*out[:3], fields[3])):
            rays_out[pl.ds(c * GRP * 4 + f, GRP, stride=4), :] = value
        for j in range(3):
            high = out[3 + j].astype(BF16).astype(F32)
            fluxes[2 * j, blocks_of(c), :] = high
            fluxes[2 * j + 1, blocks_of(c), :] = out[3 + j] - high

    def hot_of(c, steps):
        return [hots[2 * c + i] for i in range(2 * steps)]

    def scatter(js, c, hot, source=None):
        source = c if source is None else source
        parts = []
        for i in range(len(hot) * GRP // 2):
            mask = x_ids == jnp.bitwise_and(cell[pl.ds(c * GRP + i, 1), :], CX - 1)
            parts.append(
                jnp.concatenate(
                    [
                        jnp.where(mask, fluxes[2 * j + p, pl.ds(source * GRP + i, 1), :], 0.0).astype(BF16)
                        for j in js
                        for p in range(2)
                    ],
                    axis=0,
                )
            )
        lanes = slice(js[0] * 2 * CX, (js[-1] + 1) * 2 * CX)
        dep[:, lanes] += lax.dot_general(
            jnp.concatenate(hot, axis=1), jnp.concatenate(parts, axis=1), (((1,), (1,)), ((), ())),
            preferred_element_type=F32,
        )

    def before(c, carry):
        @pl.when(c == GREET)
        def _():
            pl.semaphore_wait(barrier, 8)
            for each in halos:
                each.start()

        rise(2 * c, 2, 0)
        rise(2 * LAG + c, 1, 1)
        pick(c)
        return carry

    lax.fori_loop(0, LAG, before, 0)

    for each in halos:
        each.wait()
    for side, sign in ((0, -0.5), (1, 0.5)):
        ends = [lon_in[side, w : w + 1, :] * sign for w in range(2)]
        word = pack(*ends)
        for t in range(ROWS // 128):
            lon_edge[side, t : t + 1, :] = word[:, t * 128 : (t + 1) * 128]
        closed = lat == (0 if side == 0 else nlat - 1)
        lat_edge[side] = pack(
            *[jnp.where(closed, 0.0, lat_in[side, w * LEV : (w + 1) * LEV, :] * sign) for w in range(2)]
        )
    advance(0)
    advance(1)
    fluxes[:, NB : NB + 2 * GRP, :] = jnp.zeros((6, 2 * GRP, 128), F32)

    def after(i, carry):
        pair = jnp.maximum(2 * i - 2, 0)
        source = jnp.where(i == 0, STEPS, 2 * i - 2)
        scatter((2,), pair, hot_of(pair, 2), source)
        advance(jnp.minimum(2 * i + 2, LAG - 2 + i))
        advance(jnp.minimum(2 * i + 3, LAG - 1 + i))
        rise(3 * LAG + i, 1, 0)
        pick(LAG + i)
        return carry

    lax.fori_loop(0, STEPS - LAG, after, 0)
    advance(STEPS - 1)

    boxes = []
    for d, where in enumerate(DIRS):
        for slot in range(8):
            block = rays_out[pl.ds(leaving[d, slot] * 4, 4), :]
            box_out[d, slot * 4 : slot * 4 + 4, :] = jnp.where(slot < count[d], block, 0.0)
        boxes.append(copy(box_out.at[d], arrived.at[d], 4 + d, where))
        boxes[-1].start()

    def deposit(j):
        return dep[:, j * 2 * CX : j * 2 * CX + CX] + dep[:, j * 2 * CX + CX : (j + 1) * 2 * CX]


    def last(js, first, count):
        def step(c, carry):
            scatter(js, first + 2 * c, hot_of(first + 2 * c, 2))
            return carry

        lax.fori_loop(0, count // 2, step, 0)

    stores = [pltpu.make_async_copy(rays_out, rays_new, store_sem.at[0])]
    stores[0].start()
    last((2,), STEPS - 2, 2)
    zonal = deposit(2).T
    for half in range(2):
        edge_out[half] = jnp.zeros((8, ROWS), F32)
    edge_out[0, 0:1, :] = zonal[CX - 1 : CX, :]
    edge_out[1, 0:1, :] = zonal[0:1, :]
    edges = [
        copy(edge_out.at[0], edge_in.at[0], 12, (0, 1)),
        copy(edge_out.at[1], edge_in.at[1], 13, (0, -1)),
    ]
    for each in edges:
        each.start()
    last((0, 1), 0, STEPS)
    tend[ROWS : 2 * ROWS, :] = -level_diff(deposit(1))
    half = pl.ds(ROWS, ROWS)
    stores.append(pltpu.make_async_copy(tend.at[half], tendency.at[half], store_sem.at[1]))
    stores[1].start()
    zonal = deposit(2)
    east = jnp.where(lane == CX - 1, 0.0, pltpu.roll(zonal, CX - 1, 1))
    west = jnp.where(lane == 0, 0.0, pltpu.roll(zonal, 1, 1))
    tend[0:ROWS, :] = -level_diff(deposit(0)) - (east - west) * 0.5
    for each in edges:
        each.wait()
    beyond = jnp.where(column == CX - 1, edge_in[1, 0:1, :] * -0.5, 0.0)
    tend[0:ROWS, :] += jnp.where(column == 0, edge_in[0, 0:1, :] * 0.5, beyond).T
    half = pl.ds(0, ROWS)
    stores.append(pltpu.make_async_copy(tend.at[half], tendency.at[half], store_sem.at[2]))
    stores[2].start()
    for each in (*boxes, *stores):
        each.wait()


def deliver(*refs):
    ins, outs, held, sem_in, sem_out = refs[:3], refs[3:6], refs[6:9], refs[9], refs[10]
    loads = [pltpu.make_async_copy(ins[i], held[i], sem_in.at[i]) for i in range(3)]
    stores = [pltpu.make_async_copy(held[i], outs[i], sem_out.at[i]) for i in range(3)]
    for each in loads:
        each.start()
    for load, store in zip(loads, stores):
        load.wait()
        store.start()
    for each in stores:
        each.wait()


def on_device(winds, coriolis, rays, ray_cell, ray_level, turning, leaving, leave_count):
    hbm = pl.BlockSpec(memory_space=pltpu.HBM)
    rays_new, arrived, tendency = pl.pallas_call(
        kernel,
        out_shape=(
            jax.ShapeDtypeStruct((NB * 4, 128), F32),
            jax.ShapeDtypeStruct((8, 32, 128), F32),
            jax.ShapeDtypeStruct((2 * ROWS, CX), F32),
        ),
        in_specs=[hbm] * 8,
        out_specs=(hbm,) * 3,
        scratch_shapes=[
            pltpu.VMEM((NB * 4, 128), F32),
            pltpu.VMEM((2 * ROWS, CX), F32),
            pltpu.SMEM((8, 8), jnp.int32),
            pltpu.SMEM((8,), jnp.int32),
            pltpu.SMEM((32,), F32),
            pltpu.VMEM((2 * ROWS, CX), F32),
            pltpu.VMEM((NB * 4, 128), F32),
            pltpu.VMEM((NB, 128), jnp.int32),
            pltpu.VMEM((NB, 128), jnp.int32),
            pltpu.VMEM((NB, 128), jnp.int32),
            pltpu.VMEM((2, CX, ROWS), F32),
            pltpu.VMEM((2 * CX, 2 * ROWS), BF16),
            pltpu.VMEM((2, ROWS, CX), jnp.int32),
            pltpu.VMEM((2, LEV, CX), jnp.int32),
            pltpu.VMEM((2, ROWS // 128, 128), jnp.int32),
            pltpu.VMEM((2, ROWS, SPAN), BF16),
            pltpu.VMEM((2 * STEPS, ROWS, HALF), BF16),
            pltpu.VMEM((2, NB, 128), jnp.int32),
            pltpu.VMEM((2, NB, 128), F32),
            pltpu.VMEM((6, NB + 2 * GRP, 128), F32),
            pltpu.VMEM((ROWS, 6 * CX), F32),
            pltpu.VMEM((2, 8, ROWS), F32),
            pltpu.VMEM((2, 8, ROWS), F32),
            pltpu.VMEM((2, 2 * LEV, CX), F32),
            pltpu.VMEM((2, 2 * LEV, CX), F32),
            pltpu.VMEM((2, 8, ROWS), F32),
            pltpu.VMEM((2, 8, ROWS), F32),
            pltpu.VMEM((8, 32, 128), F32),
            pltpu.SemaphoreType.DMA((8,)),
            pltpu.SemaphoreType.DMA((3,)),
            pltpu.SemaphoreType.DMA((14,)),
            pltpu.SemaphoreType.DMA((14,)),
        ],
        compiler_params=pltpu.CompilerParams(
            collective_id=0, has_side_effects=True, vmem_limit_bytes=62 << 20
        ),
        cost_estimate=pl.CostEstimate(flops=30_000_000_000, bytes_accessed=2_000_000, transcendentals=0),
    )(
        leaving.reshape(8, 8),
        leave_count.reshape(8),
        coriolis,
        winds.reshape(2 * ROWS, CX),
        rays.reshape(NB * 4, 128),
        ray_cell.reshape(NB, 128),
        ray_level.reshape(NB, 128),
        turning.reshape(NB, 128),
    )
    rays_new, arrived, tendency = pl.pallas_call(
        deliver,
        out_shape=tuple(jax.ShapeDtypeStruct(each.shape, F32) for each in (rays_new, arrived, tendency)),
        in_specs=[hbm] * 3,
        out_specs=(hbm,) * 3,
        scratch_shapes=[pltpu.VMEM(each.shape, F32) for each in (rays_new, arrived, tendency)]
        + [pltpu.SemaphoreType.DMA((3,)), pltpu.SemaphoreType.DMA((3,))],
        compiler_params=pltpu.CompilerParams(vmem_limit_bytes=62 << 20),
    )(rays_new, arrived, tendency)
    return (
        rays_new.reshape(rays.shape),
        arrived.reshape(1, 1, 8, 8, 4, 128),
        tendency.reshape(winds.shape),
    )


def solution(mesh):
    placed = (
        P(None, None, "lat", "lon"),
        P("lat"),
        P("lon", "lat", None, None, None),
        P("lon", "lat", None, None),
        P("lon", "lat", None, None),
        P("lon", "lat", None, None),
        P("lon", "lat", None, None),
        P("lon", "lat", None),
    )
    return jax.shard_map(
        on_device,
        mesh=mesh,
        in_specs=placed,
        out_specs=(
            P("lon", "lat", None, None, None),
            P("lon", "lat", None, None, None, None),
            P(None, None, "lat", "lon"),
        ),
        check_vma=False,
    )
```

```python
import jax
import jax.numpy as jnp
from jax import lax
from jax.experimental import pallas as pl
from jax.experimental.pallas import tpu as pltpu
from jax.sharding import PartitionSpec as P

STEP = 0.1
DIRS = ((0, 1), (0, -1), (1, 0), (-1, 0), (1, 1), (1, -1), (-1, 1), (-1, -1))
MESH = pl.DeviceIdType.MESH
LEV, CY, CX, NB = 12, 32, 128, 128
ROWS = LEV * CY
LAG = 8
GREET = 2
GRP = 8
SPAN = GRP * 128
HALF = SPAN // 2
STEPS = NB // GRP
UNIT = 5461.0
F32, BF16 = jnp.float32, jnp.bfloat16


def propagate(wave_k, wave_l, wave_m, action, sample, fcor, turn):
    new_k = wave_k - STEP * (wave_k * sample[0] + wave_l * sample[1])
    new_l = wave_l - STEP * (wave_k * sample[2] + wave_l * sample[3])
    new_m = wave_m - STEP * (wave_k * sample[4] + wave_l * sample[5])
    new_m = jnp.where(turn == 1, -new_m, new_m)
    horiz = new_k * new_k + new_l * new_l
    total = horiz + new_m * new_m + 1.0
    fsq = fcor * fcor
    freq2 = (horiz + fsq * (new_m * new_m + 1.0)) / total
    freq = jnp.sqrt(freq2)
    group_x = new_k * (1.0 - freq2) / (freq * total)
    group_z = new_m * (fsq - freq2) / (freq * total)
    return (
        new_k,
        new_l,
        new_m,
        group_z * new_k * action,
        group_z * new_l * action,
        group_x * new_k * action,
    )


def level_diff(field):
    zero = jnp.zeros((CY, CX), F32)
    upper = jnp.concatenate([field[CY:], zero], axis=0)
    lower = jnp.concatenate([zero, field[:-CY]], axis=0)
    return (upper - lower) * 0.5


def split(value):
    high = value.astype(BF16)
    return high, (value - high.astype(F32)).astype(BF16)


def pack(first, second):
    high = jnp.round(first * UNIT).astype(jnp.int32)
    low = jnp.round(second * UNIT).astype(jnp.int32)
    return high * 65536 + (low + 32768)


def unpack(word):
    high = lax.shift_right_arithmetic(word, 16)
    low = jnp.bitwise_and(word, 65535) - 32768
    return high.astype(F32) * (1.0 / UNIT), low.astype(F32) * (1.0 / UNIT)


def kernel(
    leaving_in, count_in, fcor_in, winds_in, rays_in, cell_in, level_in, turn_in,
    rays_new, arrived, tendency,
    rays_out, tend, leaving, count, fcor, winds, rays, cell, level, turn,
    wind_t, table, words, lat_edge, lon_edge, fresh, hots, found, samples, fluxes, dep,
    lon_out, lon_in, lat_out, lat_in, edge_out, edge_in, box_out,
    load_sem, store_sem, send_sem, recv_sem,
):
    loads = [
        pltpu.make_async_copy(src, dst, load_sem.at[i])
        for i, (src, dst) in enumerate(
            (
                (winds_in, winds),
                (cell_in, cell),
                (level_in, level),
                (rays_in, rays),
                (turn_in, turn),
                (fcor_in, fcor),
                (leaving_in, leaving),
                (count_in, count),
            )
        )
    ]
    for each in loads:
        each.start()
    lon, lat = lax.axis_index("lon"), lax.axis_index("lat")
    nlon, nlat = lax.axis_size("lon"), lax.axis_size("lat")

    def at(dlat, dlon):
        return (lax.rem(lon + dlon + nlon, nlon), lax.rem(lat + dlat + nlat, nlat))

    def copy(src, dst, which, where):
        return pltpu.make_async_remote_copy(
            src_ref=src, dst_ref=dst, send_sem=send_sem.at[which], recv_sem=recv_sem.at[which],
            device_id=at(*where), device_id_type=MESH,
        )

    barrier = pltpu.get_barrier_semaphore()
    for where in DIRS:
        pl.semaphore_signal(barrier, inc=1, device_id=at(*where), device_id_type=MESH)

    dep[...] = jnp.zeros((ROWS, 6 * CX), F32)
    fluxes[:, NB : NB + 2 * GRP, :] = jnp.zeros((6, 2 * GRP, 128), F32)
    for half in range(2):
        lon_out[half, 2:8, :] = jnp.zeros((6, ROWS), F32)
        edge_out[half] = jnp.zeros((8, ROWS), F32)
    loads[0].wait()
    for w in range(2):
        flipped = winds[w * ROWS : (w + 1) * ROWS, :].T
        wind_t[w] = flipped
        lon_out[0, w : w + 1, :] = flipped[CX - 1 : CX, :]
        lon_out[1, w : w + 1, :] = flipped[0:1, :]
    lat_out[0] = winds[pl.ds(CY - 1, 2 * LEV, stride=CY), :]
    lat_out[1] = winds[pl.ds(0, 2 * LEV, stride=CY), :]
    halos = [
        copy(lon_out.at[0], lon_in.at[0], 0, (0, 1)),
        copy(lon_out.at[1], lon_in.at[1], 1, (0, -1)),
        copy(lat_out.at[0], lat_in.at[0], 2, (1, 0)),
        copy(lat_out.at[1], lat_in.at[1], 3, (-1, 0)),
    ]
    def keep(field, flipped):
        high, low = split(flipped)
        table[field * CX : (field + 1) * CX, 0:ROWS] = high
        table[field * CX : (field + 1) * CX, ROWS : 2 * ROWS] = low

    for w in range(2):
        keep(w, level_diff(winds[w * ROWS : (w + 1) * ROWS, :]).T)
    column = lax.broadcasted_iota(jnp.int32, (CX, ROWS), 0)
    row = lax.rem(lax.broadcasted_iota(jnp.int32, (ROWS, CX), 0), CY)
    lane = lax.broadcasted_iota(jnp.int32, (ROWS, CX), 1)
    along, across = [], []
    for w in range(2):
        field = winds[w * ROWS : (w + 1) * ROWS, :]
        east = jnp.where(lane == CX - 1, 0.0, pltpu.roll(field, CX - 1, 1))
        west = jnp.where(lane == 0, 0.0, pltpu.roll(field, 1, 1))
        along.append((east - west) * 0.5)
        north = jnp.where(row == CY - 1, 0.0, pltpu.roll(field, ROWS - 1, 0))
        south = jnp.where(row == 0, 0.0, pltpu.roll(field, 1, 0))
        across.append((north - south) * 0.5)
    words[0] = pack(*along)
    words[1] = pack(*across)
    for each in loads[1:]:
        each.wait()

    x_ids = lax.broadcasted_iota(jnp.int32, (CX, 128), 0)
    r_ids = lax.broadcasted_iota(jnp.int32, (ROWS, 128), 0)

    def blocks_of(c):
        return pl.ds(pl.multiple_of(c * GRP, GRP), GRP)

    def place(c):
        cells = cell[blocks_of(c), :]
        y = lax.shift_right_logical(cells, 7)
        return jnp.bitwise_and(cells, CX - 1), y, level[blocks_of(c), :] * CY + y

    def rise(h, halves, at):
        first = h * (GRP // 2)
        for i in range(halves * GRP // 2):
            cells = cell[pl.ds(first + i, 1), :]
            rows = level[pl.ds(first + i, 1), :] * CY + lax.shift_right_logical(cells, 7)
            hot = jnp.where(r_ids == rows, 1.0, 0.0).astype(BF16)
            fresh[at, :, i * 128 : (i + 1) * 128] = hot
            lanes = slice(i % (GRP // 2) * 128, (i % (GRP // 2) + 1) * 128)
            hots[h + i // (GRP // 2), :, lanes] = hot
        hot = fresh[at, :, : halves * HALF]
        picked = lax.dot_general(
            table[...], jnp.concatenate([hot, hot], axis=0), (((1,), (0,)), ((), ())),
            preferred_element_type=F32,
        )
        for i in range(halves * GRP // 2):
            mask = x_ids == jnp.bitwise_and(cell[pl.ds(first + i, 1), :], CX - 1)
            for f in range(2):
                part = picked[f * CX : (f + 1) * CX, i * 128 : (i + 1) * 128]
                samples[f, pl.ds(first + i, 1), :] = jnp.sum(
                    jnp.where(mask, part, 0.0), axis=0, keepdims=True
                )

    def pick(c):
        x, _, rows = place(c)
        got = [jnp.zeros((GRP, 128), jnp.int32)] * 2
        for r in range(ROWS):
            here = rows == r
            for w in range(2):
                line = jnp.broadcast_to(words[w, r : r + 1, :], (GRP, CX))
                taken = jnp.take_along_axis(line, x, axis=1, mode="promise_in_bounds")
                got[w] = jnp.where(here, taken, got[w])
        for w in range(2):
            found[w, blocks_of(c), :] = got[w]

    def advance(c):
        x, y, rows = place(c)
        levels = level[blocks_of(c), :]
        sample = [*unpack(found[0, blocks_of(c), :]), *unpack(found[1, blocks_of(c), :])]
        sample += [samples[0, blocks_of(c), :], samples[1, blocks_of(c), :]]
        lanes, tiles = jnp.bitwise_and(rows, 127), lax.shift_right_logical(rows, 7)
        nought = jnp.full((GRP, 128), 32768, jnp.int32)
        for side, end in ((0, 0), (1, CX - 1)):
            word = nought
            for t in range(ROWS // 128):
                line = jnp.broadcast_to(lon_edge[side, t : t + 1, :], (GRP, 128))
                taken = jnp.take_along_axis(line, lanes, axis=1, mode="promise_in_bounds")
                word = jnp.where(jnp.logical_and(tiles == t, x == end), taken, word)
            for f, value in enumerate(unpack(word)):
                sample[f] += value
        for side, end in ((0, 0), (1, CY - 1)):
            word = nought
            for z in range(LEV):
                line = jnp.broadcast_to(lat_edge[side, z : z + 1, :], (GRP, 128))
                taken = jnp.take_along_axis(line, x, axis=1, mode="promise_in_bounds")
                word = jnp.where(jnp.logical_and(levels == z, y == end), taken, word)
            for f, value in enumerate(unpack(word)):
                sample[2 + f] += value
        f_ray = jnp.zeros((GRP, 128), F32)
        for i in range(CY):
            f_ray = jnp.where(y == i, fcor[i], f_ray)
        fields = [rays[pl.ds(c * GRP * 4 + f, GRP, stride=4), :] for f in range(4)]
        out = propagate(*fields, sample, f_ray, turn[blocks_of(c), :])
        for f, value in enumerate((*out[:3], fields[3])):
            rays_out[pl.ds(c * GRP * 4 + f, GRP, stride=4), :] = value
        for j in range(3):
            high = out[3 + j].astype(BF16).astype(F32)
            fluxes[2 * j, blocks_of(c), :] = high
            fluxes[2 * j + 1, blocks_of(c), :] = out[3 + j] - high

    def hot_of(c, steps):
        return [hots[2 * c + i] for i in range(2 * steps)]

    def scatter(js, c, hot, source=None):
        source = c if source is None else source
        parts = []
        for i in range(len(hot) * GRP // 2):
            mask = x_ids == jnp.bitwise_and(cell[pl.ds(c * GRP + i, 1), :], CX - 1)
            parts.append(
                jnp.concatenate(
                    [
                        jnp.where(mask, fluxes[2 * j + p, pl.ds(source * GRP + i, 1), :], 0.0).astype(BF16)
                        for j in js
                        for p in range(2)
                    ],
                    axis=0,
                )
            )
        lanes = slice(js[0] * 2 * CX, (js[-1] + 1) * 2 * CX)
        dep[:, lanes] += lax.dot_general(
            jnp.concatenate(hot, axis=1), jnp.concatenate(parts, axis=1), (((1,), (1,)), ((), ())),
            preferred_element_type=F32,
        )

    def before(c, carry):
        @pl.when(c == GREET)
        def _():
            pl.semaphore_wait(barrier, 8)
            for each in halos:
                each.start()

        rise(2 * c, 2, 0)
        rise(2 * LAG + c, 1, 1)
        pick(c)
        return carry

    lax.fori_loop(0, LAG, before, 0)

    for each in halos:
        each.wait()
    for side, sign in ((0, -0.5), (1, 0.5)):
        ends = [lon_in[side, w : w + 1, :] * sign for w in range(2)]
        word = pack(*ends)
        for t in range(ROWS // 128):
            lon_edge[side, t : t + 1, :] = word[:, t * 128 : (t + 1) * 128]
        closed = lat == (0 if side == 0 else nlat - 1)
        lat_edge[side] = pack(
            *[jnp.where(closed, 0.0, lat_in[side, w * LEV : (w + 1) * LEV, :] * sign) for w in range(2)]
        )
    advance(0)
    advance(1)

    def after(i, carry):
        pair = jnp.maximum(2 * i - 2, 0)
        source = jnp.where(i == 0, STEPS, 2 * i - 2)
        scatter((2,), pair, hot_of(pair, 2), source)
        advance(jnp.minimum(2 * i + 2, LAG - 2 + i))
        advance(jnp.minimum(2 * i + 3, LAG - 1 + i))
        rise(3 * LAG + i, 1, 0)
        pick(LAG + i)
        return carry

    lax.fori_loop(0, STEPS - LAG, after, 0)
    advance(STEPS - 1)

    boxes = []
    for d, where in enumerate(DIRS):
        for slot in range(8):
            block = rays_out[pl.ds(leaving[d, slot] * 4, 4), :]
            box_out[d, slot * 4 : slot * 4 + 4, :] = jnp.where(slot < count[d], block, 0.0)
        boxes.append(copy(box_out.at[d], arrived.at[d], 4 + d, where))
        boxes[-1].start()

    def deposit(j):
        return dep[:, j * 2 * CX : j * 2 * CX + CX] + dep[:, j * 2 * CX + CX : (j + 1) * 2 * CX]


    def last(js, first, count):
        def step(c, carry):
            scatter(js, first + 2 * c, hot_of(first + 2 * c, 2))
            return carry

        lax.fori_loop(0, count // 2, step, 0)

    stores = [pltpu.make_async_copy(rays_out, rays_new, store_sem.at[0])]
    stores[0].start()
    last((2,), STEPS - 2, 2)
    zonal = deposit(2).T
    edge_out[0, 0:1, :] = zonal[CX - 1 : CX, :]
    edge_out[1, 0:1, :] = zonal[0:1, :]
    edges = [
        copy(edge_out.at[0], edge_in.at[0], 12, (0, 1)),
        copy(edge_out.at[1], edge_in.at[1], 13, (0, -1)),
    ]
    for each in edges:
        each.start()
    last((0, 1), 0, STEPS)
    tend[ROWS : 2 * ROWS, :] = -level_diff(deposit(1))
    half = pl.ds(ROWS, ROWS)
    stores.append(pltpu.make_async_copy(tend.at[half], tendency.at[half], store_sem.at[1]))
    stores[1].start()
    zonal = deposit(2)
    east = jnp.where(lane == CX - 1, 0.0, pltpu.roll(zonal, CX - 1, 1))
    west = jnp.where(lane == 0, 0.0, pltpu.roll(zonal, 1, 1))
    tend[0:ROWS, :] = -level_diff(deposit(0)) - (east - west) * 0.5
    for each in edges:
        each.wait()
    beyond = jnp.where(column == CX - 1, edge_in[1, 0:1, :] * -0.5, 0.0)
    tend[0:ROWS, :] += jnp.where(column == 0, edge_in[0, 0:1, :] * 0.5, beyond).T
    half = pl.ds(0, ROWS)
    stores.append(pltpu.make_async_copy(tend.at[half], tendency.at[half], store_sem.at[2]))
    stores[2].start()
    for each in (*boxes, *stores):
        each.wait()


def deliver(*refs):
    ins, outs, held, sem_in, sem_out = refs[:3], refs[3:6], refs[6:9], refs[9], refs[10]
    loads = [pltpu.make_async_copy(ins[i], held[i], sem_in.at[i]) for i in range(3)]
    stores = [pltpu.make_async_copy(held[i], outs[i], sem_out.at[i]) for i in range(3)]
    for each in loads:
        each.start()
    for load, store in zip(loads, stores):
        load.wait()
        store.start()
    for each in stores:
        each.wait()


def on_device(winds, coriolis, rays, ray_cell, ray_level, turning, leaving, leave_count):
    hbm = pl.BlockSpec(memory_space=pltpu.HBM)
    rays_new, arrived, tendency = pl.pallas_call(
        kernel,
        out_shape=(
            jax.ShapeDtypeStruct((NB * 4, 128), F32),
            jax.ShapeDtypeStruct((8, 32, 128), F32),
            jax.ShapeDtypeStruct((2 * ROWS, CX), F32),
        ),
        in_specs=[hbm] * 8,
        out_specs=(hbm,) * 3,
        scratch_shapes=[
            pltpu.VMEM((NB * 4, 128), F32),
            pltpu.VMEM((2 * ROWS, CX), F32),
            pltpu.SMEM((8, 8), jnp.int32),
            pltpu.SMEM((8,), jnp.int32),
            pltpu.SMEM((32,), F32),
            pltpu.VMEM((2 * ROWS, CX), F32),
            pltpu.VMEM((NB * 4, 128), F32),
            pltpu.VMEM((NB, 128), jnp.int32),
            pltpu.VMEM((NB, 128), jnp.int32),
            pltpu.VMEM((NB, 128), jnp.int32),
            pltpu.VMEM((2, CX, ROWS), F32),
            pltpu.VMEM((2 * CX, 2 * ROWS), BF16),
            pltpu.VMEM((2, ROWS, CX), jnp.int32),
            pltpu.VMEM((2, LEV, CX), jnp.int32),
            pltpu.VMEM((2, ROWS // 128, 128), jnp.int32),
            pltpu.VMEM((2, ROWS, SPAN), BF16),
            pltpu.VMEM((2 * STEPS, ROWS, HALF), BF16),
            pltpu.VMEM((2, NB, 128), jnp.int32),
            pltpu.VMEM((2, NB, 128), F32),
            pltpu.VMEM((6, NB + 2 * GRP, 128), F32),
            pltpu.VMEM((ROWS, 6 * CX), F32),
            pltpu.VMEM((2, 8, ROWS), F32),
            pltpu.VMEM((2, 8, ROWS), F32),
            pltpu.VMEM((2, 2 * LEV, CX), F32),
            pltpu.VMEM((2, 2 * LEV, CX), F32),
            pltpu.VMEM((2, 8, ROWS), F32),
            pltpu.VMEM((2, 8, ROWS), F32),
            pltpu.VMEM((8, 32, 128), F32),
            pltpu.SemaphoreType.DMA((8,)),
            pltpu.SemaphoreType.DMA((3,)),
            pltpu.SemaphoreType.DMA((14,)),
            pltpu.SemaphoreType.DMA((14,)),
        ],
        compiler_params=pltpu.CompilerParams(
            collective_id=0, has_side_effects=True, vmem_limit_bytes=62 << 20
        ),
        cost_estimate=pl.CostEstimate(flops=30_000_000_000, bytes_accessed=2_000_000, transcendentals=0),
    )(
        leaving.reshape(8, 8),
        leave_count.reshape(8),
        coriolis,
        winds.reshape(2 * ROWS, CX),
        rays.reshape(NB * 4, 128),
        ray_cell.reshape(NB, 128),
        ray_level.reshape(NB, 128),
        turning.reshape(NB, 128),
    )
    rays_new, arrived, tendency = pl.pallas_call(
        deliver,
        out_shape=tuple(jax.ShapeDtypeStruct(each.shape, F32) for each in (rays_new, arrived, tendency)),
        in_specs=[hbm] * 3,
        out_specs=(hbm,) * 3,
        scratch_shapes=[pltpu.VMEM(each.shape, F32) for each in (rays_new, arrived, tendency)]
        + [pltpu.SemaphoreType.DMA((3,)), pltpu.SemaphoreType.DMA((3,))],
        compiler_params=pltpu.CompilerParams(vmem_limit_bytes=62 << 20),
    )(rays_new, arrived, tendency)
    return (
        rays_new.reshape(rays.shape),
        arrived.reshape(1, 1, 8, 8, 4, 128),
        tendency.reshape(winds.shape),
    )


def solution(mesh):
    placed = (
        P(None, None, "lat", "lon"),
        P("lat"),
        P("lon", "lat", None, None, None),
        P("lon", "lat", None, None),
        P("lon", "lat", None, None),
        P("lon", "lat", None, None),
        P("lon", "lat", None, None),
        P("lon", "lat", None),
    )
    return jax.shard_map(
        on_device,
        mesh=mesh,
        in_specs=placed,
        out_specs=(
            P("lon", "lat", None, None, None),
            P("lon", "lat", None, None, None, None),
            P(None, None, "lat", "lon"),
        ),
        check_vma=False,
    )
```

```python
import jax
import jax.numpy as jnp
from jax import lax
from jax.experimental import pallas as pl
from jax.experimental.pallas import tpu as pltpu
from jax.sharding import PartitionSpec as P

STEP = 0.1
DIRS = ((0, 1), (0, -1), (1, 0), (-1, 0), (1, 1), (1, -1), (-1, 1), (-1, -1))
MESH = pl.DeviceIdType.MESH
LEV, CY, CX, NB = 12, 32, 128, 128
ROWS = LEV * CY
LAG = 8
GREET = 4
GRP = 8
SPAN = GRP * 128
HALF = SPAN // 2
STEPS = NB // GRP
UNIT = 5461.0
F32, BF16 = jnp.float32, jnp.bfloat16


def propagate(wave_k, wave_l, wave_m, action, sample, fcor, turn):
    new_k = wave_k - STEP * (wave_k * sample[0] + wave_l * sample[1])
    new_l = wave_l - STEP * (wave_k * sample[2] + wave_l * sample[3])
    new_m = wave_m - STEP * (wave_k * sample[4] + wave_l * sample[5])
    new_m = jnp.where(turn == 1, -new_m, new_m)
    horiz = new_k * new_k + new_l * new_l
    total = horiz + new_m * new_m + 1.0
    fsq = fcor * fcor
    freq2 = (horiz + fsq * (new_m * new_m + 1.0)) / total
    freq = jnp.sqrt(freq2)
    group_x = new_k * (1.0 - freq2) / (freq * total)
    group_z = new_m * (fsq - freq2) / (freq * total)
    return (
        new_k,
        new_l,
        new_m,
        group_z * new_k * action,
        group_z * new_l * action,
        group_x * new_k * action,
    )


def level_diff(field):
    zero = jnp.zeros((CY, CX), F32)
    upper = jnp.concatenate([field[CY:], zero], axis=0)
    lower = jnp.concatenate([zero, field[:-CY]], axis=0)
    return (upper - lower) * 0.5


def split(value):
    high = value.astype(BF16)
    return high, (value - high.astype(F32)).astype(BF16)


def pack(first, second):
    high = jnp.round(first * UNIT).astype(jnp.int32)
    low = jnp.round(second * UNIT).astype(jnp.int32)
    return high * 65536 + (low + 32768)


def unpack(word):
    high = lax.shift_right_arithmetic(word, 16)
    low = jnp.bitwise_and(word, 65535) - 32768
    return high.astype(F32) * (1.0 / UNIT), low.astype(F32) * (1.0 / UNIT)


def kernel(
    leaving_in, count_in, fcor_in, winds_in, rays_in, cell_in, level_in, turn_in,
    rays_new, arrived, tendency,
    rays_out, tend, leaving, count, fcor, winds, rays, cell, level, turn,
    wind_t, table, words, lat_edge, lon_edge, fresh, hots, found, samples, fluxes, dep,
    lon_out, lon_in, lat_out, lat_in, edge_out, edge_in, box_out,
    load_sem, store_sem, send_sem, recv_sem,
):
    lon, lat = lax.axis_index("lon"), lax.axis_index("lat")
    nlon, nlat = lax.axis_size("lon"), lax.axis_size("lat")

    def at(dlat, dlon):
        return (lax.rem(lon + dlon + nlon, nlon), lax.rem(lat + dlat + nlat, nlat))

    def copy(src, dst, which, where):
        return pltpu.make_async_remote_copy(
            src_ref=src, dst_ref=dst, send_sem=send_sem.at[which], recv_sem=recv_sem.at[which],
            device_id=at(*where), device_id_type=MESH,
        )

    barrier = pltpu.get_barrier_semaphore()
    for where in DIRS:
        pl.semaphore_signal(barrier, inc=1, device_id=at(*where), device_id_type=MESH)

    loads = [
        pltpu.make_async_copy(src, dst, load_sem.at[i])
        for i, (src, dst) in enumerate(
            (
                (winds_in, winds),
                (cell_in, cell),
                (level_in, level),
                (rays_in, rays),
                (turn_in, turn),
                (fcor_in, fcor),
                (leaving_in, leaving),
                (count_in, count),
            )
        )
    ]
    for each in loads:
        each.start()
    dep[...] = jnp.zeros((ROWS, 6 * CX), F32)
    fluxes[:, NB : NB + 2 * GRP, :] = jnp.zeros((6, 2 * GRP, 128), F32)
    loads[0].wait()
    for w in range(2):
        flipped = winds[w * ROWS : (w + 1) * ROWS, :].T
        wind_t[w] = flipped
        lon_out[0, w : w + 1, :] = flipped[CX - 1 : CX, :]
        lon_out[1, w : w + 1, :] = flipped[0:1, :]
    lat_out[0] = winds[pl.ds(CY - 1, 2 * LEV, stride=CY), :]
    lat_out[1] = winds[pl.ds(0, 2 * LEV, stride=CY), :]
    halos = [
        copy(lon_out.at[0], lon_in.at[0], 0, (0, 1)),
        copy(lon_out.at[1], lon_in.at[1], 1, (0, -1)),
        copy(lat_out.at[0], lat_in.at[0], 2, (1, 0)),
        copy(lat_out.at[1], lat_in.at[1], 3, (-1, 0)),
    ]
    def keep(field, flipped):
        high, low = split(flipped)
        table[field * CX : (field + 1) * CX, 0:ROWS] = high
        table[field * CX : (field + 1) * CX, ROWS : 2 * ROWS] = low

    for w in range(2):
        keep(w, level_diff(winds[w * ROWS : (w + 1) * ROWS, :]).T)
    column = lax.broadcasted_iota(jnp.int32, (CX, ROWS), 0)
    row = lax.rem(lax.broadcasted_iota(jnp.int32, (ROWS, CX), 0), CY)
    lane = lax.broadcasted_iota(jnp.int32, (ROWS, CX), 1)
    along, across = [], []
    for w in range(2):
        field = winds[w * ROWS : (w + 1) * ROWS, :]
        east = jnp.where(lane == CX - 1, 0.0, pltpu.roll(field, CX - 1, 1))
        west = jnp.where(lane == 0, 0.0, pltpu.roll(field, 1, 1))
        along.append((east - west) * 0.5)
        north = jnp.where(row == CY - 1, 0.0, pltpu.roll(field, ROWS - 1, 0))
        south = jnp.where(row == 0, 0.0, pltpu.roll(field, 1, 0))
        across.append((north - south) * 0.5)
    words[0] = pack(*along)
    words[1] = pack(*across)
    for each in loads[1:]:
        each.wait()

    x_ids = lax.broadcasted_iota(jnp.int32, (CX, 128), 0)
    r_ids = lax.broadcasted_iota(jnp.int32, (ROWS, 128), 0)

    def blocks_of(c):
        return pl.ds(pl.multiple_of(c * GRP, GRP), GRP)

    def place(c):
        cells = cell[blocks_of(c), :]
        y = lax.shift_right_logical(cells, 7)
        return jnp.bitwise_and(cells, CX - 1), y, level[blocks_of(c), :] * CY + y

    def rise(halves):
        blocks = [h * (GRP // 2) + i for h in halves for i in range(GRP // 2)]
        for i, block in enumerate(blocks):
            cells = cell[pl.ds(block, 1), :]
            rows = level[pl.ds(block, 1), :] * CY + lax.shift_right_logical(cells, 7)
            hot = jnp.where(r_ids == rows, 1.0, 0.0).astype(BF16)
            fresh[:, i * 128 : (i + 1) * 128] = hot
            lanes = slice(i % (GRP // 2) * 128, (i % (GRP // 2) + 1) * 128)
            hots[halves[i // (GRP // 2)], :, lanes] = hot
        hot = fresh[:, : len(halves) * HALF]
        picked = lax.dot_general(
            table[...], jnp.concatenate([hot, hot], axis=0), (((1,), (0,)), ((), ())),
            preferred_element_type=F32,
        )
        for i, block in enumerate(blocks):
            mask = x_ids == jnp.bitwise_and(cell[pl.ds(block, 1), :], CX - 1)
            for f in range(2):
                part = picked[f * CX : (f + 1) * CX, i * 128 : (i + 1) * 128]
                samples[f, pl.ds(block, 1), :] = jnp.sum(
                    jnp.where(mask, part, 0.0), axis=0, keepdims=True
                )

    def pick(c):
        x, _, rows = place(c)
        got = [jnp.zeros((GRP, 128), jnp.int32)] * 2
        for r in range(ROWS):
            here = rows == r
            for w in range(2):
                line = jnp.broadcast_to(words[w, r : r + 1, :], (GRP, CX))
                taken = jnp.take_along_axis(line, x, axis=1, mode="promise_in_bounds")
                got[w] = jnp.where(here, taken, got[w])
        for w in range(2):
            found[w, blocks_of(c), :] = got[w]

    def advance(c):
        x, y, rows = place(c)
        levels = level[blocks_of(c), :]
        sample = [*unpack(found[0, blocks_of(c), :]), *unpack(found[1, blocks_of(c), :])]
        sample += [samples[0, blocks_of(c), :], samples[1, blocks_of(c), :]]
        lanes, tiles = jnp.bitwise_and(rows, 127), lax.shift_right_logical(rows, 7)
        nought = jnp.full((GRP, 128), 32768, jnp.int32)
        for side, end in ((0, 0), (1, CX - 1)):
            word = nought
            for t in range(ROWS // 128):
                line = jnp.broadcast_to(lon_edge[side, t : t + 1, :], (GRP, 128))
                taken = jnp.take_along_axis(line, lanes, axis=1, mode="promise_in_bounds")
                word = jnp.where(jnp.logical_and(tiles == t, x == end), taken, word)
            for f, value in enumerate(unpack(word)):
                sample[f] += value
        for side, end in ((0, 0), (1, CY - 1)):
            word = nought
            for z in range(LEV):
                line = jnp.broadcast_to(lat_edge[side, z : z + 1, :], (GRP, 128))
                taken = jnp.take_along_axis(line, x, axis=1, mode="promise_in_bounds")
                word = jnp.where(jnp.logical_and(levels == z, y == end), taken, word)
            for f, value in enumerate(unpack(word)):
                sample[2 + f] += value
        f_ray = jnp.zeros((GRP, 128), F32)
        for i in range(CY):
            f_ray = jnp.where(y == i, fcor[i], f_ray)
        fields = [rays[pl.ds(c * GRP * 4 + f, GRP, stride=4), :] for f in range(4)]
        out = propagate(*fields, sample, f_ray, turn[blocks_of(c), :])
        for f, value in enumerate((*out[:3], fields[3])):
            rays_out[pl.ds(c * GRP * 4 + f, GRP, stride=4), :] = value
        for j in range(3):
            high = out[3 + j].astype(BF16).astype(F32)
            fluxes[2 * j, blocks_of(c), :] = high
            fluxes[2 * j + 1, blocks_of(c), :] = out[3 + j] - high

    def hot_of(c, steps):
        return [hots[2 * c + i] for i in range(2 * steps)]

    def scatter(js, c, hot, source=None):
        source = c if source is None else source
        parts = []
        for i in range(len(hot) * GRP // 2):
            mask = x_ids == jnp.bitwise_and(cell[pl.ds(c * GRP + i, 1), :], CX - 1)
            parts.append(
                jnp.concatenate(
                    [
                        jnp.where(mask, fluxes[2 * j + p, pl.ds(source * GRP + i, 1), :], 0.0).astype(BF16)
                        for j in js
                        for p in range(2)
                    ],
                    axis=0,
                )
            )
        lanes = slice(js[0] * 2 * CX, (js[-1] + 1) * 2 * CX)
        dep[:, lanes] += lax.dot_general(
            jnp.concatenate(hot, axis=1), jnp.concatenate(parts, axis=1), (((1,), (1,)), ((), ())),
            preferred_element_type=F32,
        )

    def before(c, carry):
        @pl.when(c == GREET)
        def _():
            pl.semaphore_wait(barrier, 8)
            for each in halos:
                each.start()

        rise((2 * c, 2 * c + 1, 2 * LAG + c))
        pick(c)
        return carry

    lax.fori_loop(0, LAG, before, 0)

    for each in halos:
        each.wait()
    for side, sign in ((0, -0.5), (1, 0.5)):
        ends = [lon_in[side, w : w + 1, :] * sign for w in range(2)]
        word = pack(*ends)
        for t in range(ROWS // 128):
            lon_edge[side, t : t + 1, :] = word[:, t * 128 : (t + 1) * 128]
        closed = lat == (0 if side == 0 else nlat - 1)
        lat_edge[side] = pack(
            *[jnp.where(closed, 0.0, lat_in[side, w * LEV : (w + 1) * LEV, :] * sign) for w in range(2)]
        )
    advance(0)
    advance(1)

    def after(i, carry):
        pair = jnp.maximum(2 * i - 2, 0)
        source = jnp.where(i == 0, STEPS, 2 * i - 2)
        scatter((2,), pair, hot_of(pair, 2), source)
        advance(jnp.minimum(2 * i + 2, LAG - 2 + i))
        advance(jnp.minimum(2 * i + 3, LAG - 1 + i))
        rise((3 * LAG + i,))
        pick(LAG + i)
        return carry

    lax.fori_loop(0, STEPS - LAG, after, 0)
    advance(STEPS - 1)

    boxes = []
    for d, where in enumerate(DIRS):
        for slot in range(8):
            block = rays_out[pl.ds(leaving[d, slot] * 4, 4), :]
            box_out[d, slot * 4 : slot * 4 + 4, :] = jnp.where(slot < count[d], block, 0.0)
        boxes.append(copy(box_out.at[d], arrived.at[d], 4 + d, where))
        boxes[-1].start()

    def deposit(j):
        return dep[:, j * 2 * CX : j * 2 * CX + CX] + dep[:, j * 2 * CX + CX : (j + 1) * 2 * CX]


    def last(js, first, count):
        def step(c, carry):
            scatter(js, first + 2 * c, hot_of(first + 2 * c, 2))
            return carry

        lax.fori_loop(0, count // 2, step, 0)

    stores = [pltpu.make_async_copy(rays_out, rays_new, store_sem.at[0])]
    stores[0].start()
    last((2,), STEPS - 2, 2)
    zonal = deposit(2).T
    edge_out[0, 0:1, :] = zonal[CX - 1 : CX, :]
    edge_out[1, 0:1, :] = zonal[0:1, :]
    edges = [
        copy(edge_out.at[0], edge_in.at[0], 12, (0, 1)),
        copy(edge_out.at[1], edge_in.at[1], 13, (0, -1)),
    ]
    for each in edges:
        each.start()
    last((0, 1), 0, STEPS)
    tend[ROWS : 2 * ROWS, :] = -level_diff(deposit(1))
    half = pl.ds(ROWS, ROWS)
    stores.append(pltpu.make_async_copy(tend.at[half], tendency.at[half], store_sem.at[1]))
    stores[1].start()
    zonal = deposit(2)
    east = jnp.where(lane == CX - 1, 0.0, pltpu.roll(zonal, CX - 1, 1))
    west = jnp.where(lane == 0, 0.0, pltpu.roll(zonal, 1, 1))
    tend[0:ROWS, :] = -level_diff(deposit(0)) - (east - west) * 0.5
    for each in edges:
        each.wait()
    beyond = jnp.where(column == CX - 1, edge_in[1, 0:1, :] * -0.5, 0.0)
    tend[0:ROWS, :] += jnp.where(column == 0, edge_in[0, 0:1, :] * 0.5, beyond).T
    half = pl.ds(0, ROWS)
    stores.append(pltpu.make_async_copy(tend.at[half], tendency.at[half], store_sem.at[2]))
    stores[2].start()
    for each in (*boxes, *stores):
        each.wait()


def deliver(*refs):
    ins, outs, held, sem_in, sem_out = refs[:3], refs[3:6], refs[6:9], refs[9], refs[10]
    loads = [pltpu.make_async_copy(ins[i], held[i], sem_in.at[i]) for i in range(3)]
    stores = [pltpu.make_async_copy(held[i], outs[i], sem_out.at[i]) for i in range(3)]
    for each in loads:
        each.start()
    for load, store in zip(loads, stores):
        load.wait()
        store.start()
    for each in stores:
        each.wait()


def on_device(winds, coriolis, rays, ray_cell, ray_level, turning, leaving, leave_count):
    hbm = pl.BlockSpec(memory_space=pltpu.HBM)
    rays_new, arrived, tendency = pl.pallas_call(
        kernel,
        out_shape=(
            jax.ShapeDtypeStruct((NB * 4, 128), F32),
            jax.ShapeDtypeStruct((8, 32, 128), F32),
            jax.ShapeDtypeStruct((2 * ROWS, CX), F32),
        ),
        in_specs=[hbm] * 8,
        out_specs=(hbm,) * 3,
        scratch_shapes=[
            pltpu.VMEM((NB * 4, 128), F32),
            pltpu.VMEM((2 * ROWS, CX), F32),
            pltpu.SMEM((8, 8), jnp.int32),
            pltpu.SMEM((8,), jnp.int32),
            pltpu.SMEM((32,), F32),
            pltpu.VMEM((2 * ROWS, CX), F32),
            pltpu.VMEM((NB * 4, 128), F32),
            pltpu.VMEM((NB, 128), jnp.int32),
            pltpu.VMEM((NB, 128), jnp.int32),
            pltpu.VMEM((NB, 128), jnp.int32),
            pltpu.VMEM((2, CX, ROWS), F32),
            pltpu.VMEM((2 * CX, 2 * ROWS), BF16),
            pltpu.VMEM((2, ROWS, CX), jnp.int32),
            pltpu.VMEM((2, LEV, CX), jnp.int32),
            pltpu.VMEM((2, ROWS // 128, 128), jnp.int32),
            pltpu.VMEM((ROWS, 3 * HALF), BF16),
            pltpu.VMEM((2 * STEPS, ROWS, HALF), BF16),
            pltpu.VMEM((2, NB, 128), jnp.int32),
            pltpu.VMEM((2, NB, 128), F32),
            pltpu.VMEM((6, NB + 2 * GRP, 128), F32),
            pltpu.VMEM((ROWS, 6 * CX), F32),
            pltpu.VMEM((2, 2, ROWS), F32),
            pltpu.VMEM((2, 2, ROWS), F32),
            pltpu.VMEM((2, 2 * LEV, CX), F32),
            pltpu.VMEM((2, 2 * LEV, CX), F32),
            pltpu.VMEM((2, 1, ROWS), F32),
            pltpu.VMEM((2, 1, ROWS), F32),
            pltpu.VMEM((8, 32, 128), F32),
            pltpu.SemaphoreType.DMA((8,)),
            pltpu.SemaphoreType.DMA((3,)),
            pltpu.SemaphoreType.DMA((14,)),
            pltpu.SemaphoreType.DMA((14,)),
        ],
        compiler_params=pltpu.CompilerParams(
            collective_id=0, has_side_effects=True, vmem_limit_bytes=62 << 20
        ),
        cost_estimate=pl.CostEstimate(flops=30_000_000_000, bytes_accessed=2_000_000, transcendentals=0),
    )(
        leaving.reshape(8, 8),
        leave_count.reshape(8),
        coriolis,
        winds.reshape(2 * ROWS, CX),
        rays.reshape(NB * 4, 128),
        ray_cell.reshape(NB, 128),
        ray_level.reshape(NB, 128),
        turning.reshape(NB, 128),
    )
    rays_new, arrived, tendency = pl.pallas_call(
        deliver,
        out_shape=tuple(jax.ShapeDtypeStruct(each.shape, F32) for each in (rays_new, arrived, tendency)),
        in_specs=[hbm] * 3,
        out_specs=(hbm,) * 3,
        scratch_shapes=[pltpu.VMEM(each.shape, F32) for each in (rays_new, arrived, tendency)]
        + [pltpu.SemaphoreType.DMA((3,)), pltpu.SemaphoreType.DMA((3,))],
        compiler_params=pltpu.CompilerParams(vmem_limit_bytes=62 << 20),
    )(rays_new, arrived, tendency)
    return (
        rays_new.reshape(rays.shape),
        arrived.reshape(1, 1, 8, 8, 4, 128),
        tendency.reshape(winds.shape),
    )


def solution(mesh):
    placed = (
        P(None, None, "lat", "lon"),
        P("lat"),
        P("lon", "lat", None, None, None),
        P("lon", "lat", None, None),
        P("lon", "lat", None, None),
        P("lon", "lat", None, None),
        P("lon", "lat", None, None),
        P("lon", "lat", None),
    )
    return jax.shard_map(
        on_device,
        mesh=mesh,
        in_specs=placed,
        out_specs=(
            P("lon", "lat", None, None, None),
            P("lon", "lat", None, None, None, None),
            P(None, None, "lat", "lon"),
        ),
        check_vma=False,
    )
```

```python
import jax
import jax.numpy as jnp
from jax import lax
from jax.experimental import pallas as pl
from jax.experimental.pallas import tpu as pltpu
from jax.sharding import PartitionSpec as P

STEP = 0.1
DIRS = ((0, 1), (0, -1), (1, 0), (-1, 0), (1, 1), (1, -1), (-1, 1), (-1, -1))
MESH = pl.DeviceIdType.MESH
LEV, CY, CX, NB = 12, 32, 128, 128
ROWS = LEV * CY
LAG = 8
GREET = 2
GRP = 8
SPAN = GRP * 128
HALF = SPAN // 2
STEPS = NB // GRP
UNIT = 5461.0
F32, BF16 = jnp.float32, jnp.bfloat16


def propagate(wave_k, wave_l, wave_m, action, sample, fcor, turn):
    new_k = wave_k - STEP * (wave_k * sample[0] + wave_l * sample[1])
    new_l = wave_l - STEP * (wave_k * sample[2] + wave_l * sample[3])
    new_m = wave_m - STEP * (wave_k * sample[4] + wave_l * sample[5])
    new_m = jnp.where(turn == 1, -new_m, new_m)
    horiz = new_k * new_k + new_l * new_l
    total = horiz + new_m * new_m + 1.0
    fsq = fcor * fcor
    freq2 = (horiz + fsq * (new_m * new_m + 1.0)) / total
    freq = jnp.sqrt(freq2)
    group_x = new_k * (1.0 - freq2) / (freq * total)
    group_z = new_m * (fsq - freq2) / (freq * total)
    return (
        new_k,
        new_l,
        new_m,
        group_z * new_k * action,
        group_z * new_l * action,
        group_x * new_k * action,
    )


def level_diff(field):
    zero = jnp.zeros((CY, CX), F32)
    upper = jnp.concatenate([field[CY:], zero], axis=0)
    lower = jnp.concatenate([zero, field[:-CY]], axis=0)
    return (upper - lower) * 0.5


def split(value):
    high = value.astype(BF16)
    return high, (value - high.astype(F32)).astype(BF16)


def pack(first, second):
    high = jnp.round(first * UNIT).astype(jnp.int32)
    low = jnp.round(second * UNIT).astype(jnp.int32)
    return high * 65536 + (low + 32768)


def unpack(word):
    high = lax.shift_right_arithmetic(word, 16)
    low = jnp.bitwise_and(word, 65535) - 32768
    return high.astype(F32) * (1.0 / UNIT), low.astype(F32) * (1.0 / UNIT)


def kernel(
    leaving_in, count_in, fcor_in, winds_in, rays_in, cell_in, level_in, turn_in,
    rays_new, arrived, tendency,
    rays_out, tend, leaving, count, fcor, winds, rays, cell, level, turn,
    wind_t, table, words, lat_edge, lon_edge, fresh, hots, found, samples, fluxes, dep,
    lon_out, lon_in, lat_out, lat_in, edge_out, edge_in, box_out,
    load_sem, store_sem, send_sem, recv_sem,
):
    lon, lat = lax.axis_index("lon"), lax.axis_index("lat")
    nlon, nlat = lax.axis_size("lon"), lax.axis_size("lat")

    def at(dlat, dlon):
        return (lax.rem(lon + dlon + nlon, nlon), lax.rem(lat + dlat + nlat, nlat))

    def copy(src, dst, which, where):
        return pltpu.make_async_remote_copy(
            src_ref=src, dst_ref=dst, send_sem=send_sem.at[which], recv_sem=recv_sem.at[which],
            device_id=at(*where), device_id_type=MESH,
        )

    barrier = pltpu.get_barrier_semaphore()
    for where in DIRS:
        pl.semaphore_signal(barrier, inc=1, device_id=at(*where), device_id_type=MESH)

    loads = [
        pltpu.make_async_copy(src, dst, load_sem.at[i])
        for i, (src, dst) in enumerate(
            (
                (winds_in, winds),
                (cell_in, cell),
                (level_in, level),
                (rays_in, rays),
                (turn_in, turn),
                (fcor_in, fcor),
                (leaving_in, leaving),
                (count_in, count),
            )
        )
    ]
    for each in loads:
        each.start()
    dep[...] = jnp.zeros((ROWS, 6 * CX), F32)
    fluxes[:, NB : NB + 2 * GRP, :] = jnp.zeros((6, 2 * GRP, 128), F32)
    loads[0].wait()
    for w in range(2):
        flipped = winds[w * ROWS : (w + 1) * ROWS, :].T
        wind_t[w] = flipped
        lon_out[0, w : w + 1, :] = flipped[CX - 1 : CX, :]
        lon_out[1, w : w + 1, :] = flipped[0:1, :]
    lat_out[0] = winds[pl.ds(CY - 1, 2 * LEV, stride=CY), :]
    lat_out[1] = winds[pl.ds(0, 2 * LEV, stride=CY), :]
    halos = [
        copy(lon_out.at[0], lon_in.at[0], 0, (0, 1)),
        copy(lon_out.at[1], lon_in.at[1], 1, (0, -1)),
        copy(lat_out.at[0], lat_in.at[0], 2, (1, 0)),
        copy(lat_out.at[1], lat_in.at[1], 3, (-1, 0)),
    ]
    def keep(field, flipped):
        high, low = split(flipped)
        table[field * CX : (field + 1) * CX, 0:ROWS] = high
        table[field * CX : (field + 1) * CX, ROWS : 2 * ROWS] = low

    for w in range(2):
        keep(w, level_diff(winds[w * ROWS : (w + 1) * ROWS, :]).T)
    column = lax.broadcasted_iota(jnp.int32, (CX, ROWS), 0)
    row = lax.rem(lax.broadcasted_iota(jnp.int32, (ROWS, CX), 0), CY)
    lane = lax.broadcasted_iota(jnp.int32, (ROWS, CX), 1)
    along, across = [], []
    for w in range(2):
        field = winds[w * ROWS : (w + 1) * ROWS, :]
        east = jnp.where(lane == CX - 1, 0.0, pltpu.roll(field, CX - 1, 1))
        west = jnp.where(lane == 0, 0.0, pltpu.roll(field, 1, 1))
        along.append((east - west) * 0.5)
        north = jnp.where(row == CY - 1, 0.0, pltpu.roll(field, ROWS - 1, 0))
        south = jnp.where(row == 0, 0.0, pltpu.roll(field, 1, 0))
        across.append((north - south) * 0.5)
    words[0] = pack(*along)
    words[1] = pack(*across)
    for each in loads[1:]:
        each.wait()

    x_ids = lax.broadcasted_iota(jnp.int32, (CX, 128), 0)
    r_ids = lax.broadcasted_iota(jnp.int32, (ROWS, 128), 0)

    def blocks_of(c):
        return pl.ds(pl.multiple_of(c * GRP, GRP), GRP)

    def place(c):
        cells = cell[blocks_of(c), :]
        y = lax.shift_right_logical(cells, 7)
        return jnp.bitwise_and(cells, CX - 1), y, level[blocks_of(c), :] * CY + y

    def rise(halves):
        blocks = [h * (GRP // 2) + i for h in halves for i in range(GRP // 2)]
        for i, block in enumerate(blocks):
            cells = cell[pl.ds(block, 1), :]
            rows = level[pl.ds(block, 1), :] * CY + lax.shift_right_logical(cells, 7)
            hot = jnp.where(r_ids == rows, 1.0, 0.0).astype(BF16)
            fresh[:, i * 128 : (i + 1) * 128] = hot
            lanes = slice(i % (GRP // 2) * 128, (i % (GRP // 2) + 1) * 128)
            hots[halves[i // (GRP // 2)], :, lanes] = hot
        hot = fresh[:, : len(halves) * HALF]
        picked = lax.dot_general(
            table[...], jnp.concatenate([hot, hot], axis=0), (((1,), (0,)), ((), ())),
            preferred_element_type=F32,
        )
        for i, block in enumerate(blocks):
            mask = x_ids == jnp.bitwise_and(cell[pl.ds(block, 1), :], CX - 1)
            for f in range(2):
                part = picked[f * CX : (f + 1) * CX, i * 128 : (i + 1) * 128]
                samples[f, pl.ds(block, 1), :] = jnp.sum(
                    jnp.where(mask, part, 0.0), axis=0, keepdims=True
                )

    def pick(c):
        x, _, rows = place(c)
        got = [jnp.zeros((GRP, 128), jnp.int32)] * 2
        for r in range(ROWS):
            here = rows == r
            for w in range(2):
                line = jnp.broadcast_to(words[w, r : r + 1, :], (GRP, CX))
                taken = jnp.take_along_axis(line, x, axis=1, mode="promise_in_bounds")
                got[w] = jnp.where(here, taken, got[w])
        for w in range(2):
            found[w, blocks_of(c), :] = got[w]

    def advance(c):
        x, y, rows = place(c)
        levels = level[blocks_of(c), :]
        sample = [*unpack(found[0, blocks_of(c), :]), *unpack(found[1, blocks_of(c), :])]
        sample += [samples[0, blocks_of(c), :], samples[1, blocks_of(c), :]]
        lanes, tiles = jnp.bitwise_and(rows, 127), lax.shift_right_logical(rows, 7)
        nought = jnp.full((GRP, 128), 32768, jnp.int32)
        for side, end in ((0, 0), (1, CX - 1)):
            word = nought
            for t in range(ROWS // 128):
                line = jnp.broadcast_to(lon_edge[side, t : t + 1, :], (GRP, 128))
                taken = jnp.take_along_axis(line, lanes, axis=1, mode="promise_in_bounds")
                word = jnp.where(jnp.logical_and(tiles == t, x == end), taken, word)
            for f, value in enumerate(unpack(word)):
                sample[f] += value
        for side, end in ((0, 0), (1, CY - 1)):
            word = nought
            for z in range(LEV):
                line = jnp.broadcast_to(lat_edge[side, z : z + 1, :], (GRP, 128))
                taken = jnp.take_along_axis(line, x, axis=1, mode="promise_in_bounds")
                word = jnp.where(jnp.logical_and(levels == z, y == end), taken, word)
            for f, value in enumerate(unpack(word)):
                sample[2 + f] += value
        f_ray = jnp.zeros((GRP, 128), F32)
        for i in range(CY):
            f_ray = jnp.where(y == i, fcor[i], f_ray)
        fields = [rays[pl.ds(c * GRP * 4 + f, GRP, stride=4), :] for f in range(4)]
        out = propagate(*fields, sample, f_ray, turn[blocks_of(c), :])
        for f, value in enumerate((*out[:3], fields[3])):
            rays_out[pl.ds(c * GRP * 4 + f, GRP, stride=4), :] = value
        for j in range(3):
            high = out[3 + j].astype(BF16).astype(F32)
            fluxes[2 * j, blocks_of(c), :] = high
            fluxes[2 * j + 1, blocks_of(c), :] = out[3 + j] - high

    def hot_of(c, steps):
        return [hots[2 * c + i] for i in range(2 * steps)]

    def scatter(js, c, hot, source=None):
        source = c if source is None else source
        parts = []
        for i in range(len(hot) * GRP // 2):
            mask = x_ids == jnp.bitwise_and(cell[pl.ds(c * GRP + i, 1), :], CX - 1)
            parts.append(
                jnp.concatenate(
                    [
                        jnp.where(mask, fluxes[2 * j + p, pl.ds(source * GRP + i, 1), :], 0.0).astype(BF16)
                        for j in js
                        for p in range(2)
                    ],
                    axis=0,
                )
            )
        lanes = slice(js[0] * 2 * CX, (js[-1] + 1) * 2 * CX)
        dep[:, lanes] += lax.dot_general(
            jnp.concatenate(hot, axis=1), jnp.concatenate(parts, axis=1), (((1,), (1,)), ((), ())),
            preferred_element_type=F32,
        )

    greet = jnp.where(lax.rem(lon, 4) == 0, GREET + 2, GREET)

    def before(c, carry):
        @pl.when(c == greet)
        def _():
            pl.semaphore_wait(barrier, 8)
            for each in halos:
                each.start()

        rise((2 * c, 2 * c + 1, 2 * LAG + c))
        pick(c)
        return carry

    lax.fori_loop(0, LAG, before, 0)

    for each in halos:
        each.wait()
    for side, sign in ((0, -0.5), (1, 0.5)):
        ends = [lon_in[side, w : w + 1, :] * sign for w in range(2)]
        word = pack(*ends)
        for t in range(ROWS // 128):
            lon_edge[side, t : t + 1, :] = word[:, t * 128 : (t + 1) * 128]
        closed = lat == (0 if side == 0 else nlat - 1)
        lat_edge[side] = pack(
            *[jnp.where(closed, 0.0, lat_in[side, w * LEV : (w + 1) * LEV, :] * sign) for w in range(2)]
        )
    advance(0)
    advance(1)

    def after(i, carry):
        pair = jnp.maximum(2 * i - 2, 0)
        source = jnp.where(i == 0, STEPS, 2 * i - 2)
        scatter((2,), pair, hot_of(pair, 2), source)
        advance(jnp.minimum(2 * i + 2, LAG - 2 + i))
        advance(jnp.minimum(2 * i + 3, LAG - 1 + i))
        rise((3 * LAG + i,))
        pick(LAG + i)
        return carry

    lax.fori_loop(0, STEPS - LAG, after, 0)
    advance(STEPS - 1)

    boxes = []
    for d, where in enumerate(DIRS):
        for slot in range(8):
            block = rays_out[pl.ds(leaving[d, slot] * 4, 4), :]
            box_out[d, slot * 4 : slot * 4 + 4, :] = jnp.where(slot < count[d], block, 0.0)
        boxes.append(copy(box_out.at[d], arrived.at[d], 4 + d, where))
        boxes[-1].start()

    def deposit(j):
        return dep[:, j * 2 * CX : j * 2 * CX + CX] + dep[:, j * 2 * CX + CX : (j + 1) * 2 * CX]


    def last(js, first, count, each=2):
        def step(c, carry):
            scatter(js, first + each * c, hot_of(first + each * c, each))
            return carry

        lax.fori_loop(0, count // each, step, 0)

    stores = [pltpu.make_async_copy(rays_out, rays_new, store_sem.at[0])]
    stores[0].start()
    last((2,), STEPS - 2, 2)
    zonal = deposit(2).T
    edge_out[0, 0:1, :] = zonal[CX - 1 : CX, :]
    edge_out[1, 0:1, :] = zonal[0:1, :]
    edges = [
        copy(edge_out.at[0], edge_in.at[0], 12, (0, 1)),
        copy(edge_out.at[1], edge_in.at[1], 13, (0, -1)),
    ]
    for each in edges:
        each.start()
    last((0, 1), 0, STEPS, 4)
    tend[ROWS : 2 * ROWS, :] = -level_diff(deposit(1))
    half = pl.ds(ROWS, ROWS)
    stores.append(pltpu.make_async_copy(tend.at[half], tendency.at[half], store_sem.at[1]))
    stores[1].start()
    zonal = deposit(2)
    east = jnp.where(lane == CX - 1, 0.0, pltpu.roll(zonal, CX - 1, 1))
    west = jnp.where(lane == 0, 0.0, pltpu.roll(zonal, 1, 1))
    tend[0:ROWS, :] = -level_diff(deposit(0)) - (east - west) * 0.5
    for each in edges:
        each.wait()
    beyond = jnp.where(column == CX - 1, edge_in[1, 0:1, :] * -0.5, 0.0)
    tend[0:ROWS, :] += jnp.where(column == 0, edge_in[0, 0:1, :] * 0.5, beyond).T
    half = pl.ds(0, ROWS)
    stores.append(pltpu.make_async_copy(tend.at[half], tendency.at[half], store_sem.at[2]))
    stores[2].start()
    for each in (*boxes, *stores):
        each.wait()


def deliver(*refs):
    ins, outs, held, sem_in, sem_out = refs[:3], refs[3:6], refs[6:9], refs[9], refs[10]
    loads = [pltpu.make_async_copy(ins[i], held[i], sem_in.at[i]) for i in range(3)]
    stores = [pltpu.make_async_copy(held[i], outs[i], sem_out.at[i]) for i in range(3)]
    for each in loads:
        each.start()
    for load, store in zip(loads, stores):
        load.wait()
        store.start()
    for each in stores:
        each.wait()


def on_device(winds, coriolis, rays, ray_cell, ray_level, turning, leaving, leave_count):
    hbm = pl.BlockSpec(memory_space=pltpu.HBM)
    rays_new, arrived, tendency = pl.pallas_call(
        kernel,
        out_shape=(
            jax.ShapeDtypeStruct((NB * 4, 128), F32),
            jax.ShapeDtypeStruct((8, 32, 128), F32),
            jax.ShapeDtypeStruct((2 * ROWS, CX), F32),
        ),
        in_specs=[hbm] * 8,
        out_specs=(hbm,) * 3,
        scratch_shapes=[
            pltpu.VMEM((NB * 4, 128), F32),
            pltpu.VMEM((2 * ROWS, CX), F32),
            pltpu.SMEM((8, 8), jnp.int32),
            pltpu.SMEM((8,), jnp.int32),
            pltpu.SMEM((32,), F32),
            pltpu.VMEM((2 * ROWS, CX), F32),
            pltpu.VMEM((NB * 4, 128), F32),
            pltpu.VMEM((NB, 128), jnp.int32),
            pltpu.VMEM((NB, 128), jnp.int32),
            pltpu.VMEM((NB, 128), jnp.int32),
            pltpu.VMEM((2, CX, ROWS), F32),
            pltpu.VMEM((2 * CX, 2 * ROWS), BF16),
            pltpu.VMEM((2, ROWS, CX), jnp.int32),
            pltpu.VMEM((2, LEV, CX), jnp.int32),
            pltpu.VMEM((2, ROWS // 128, 128), jnp.int32),
            pltpu.VMEM((ROWS, 3 * HALF), BF16),
            pltpu.VMEM((2 * STEPS, ROWS, HALF), BF16),
            pltpu.VMEM((2, NB, 128), jnp.int32),
            pltpu.VMEM((2, NB, 128), F32),
            pltpu.VMEM((6, NB + 2 * GRP, 128), F32),
            pltpu.VMEM((ROWS, 6 * CX), F32),
            pltpu.VMEM((2, 2, ROWS), F32),
            pltpu.VMEM((2, 2, ROWS), F32),
            pltpu.VMEM((2, 2 * LEV, CX), F32),
            pltpu.VMEM((2, 2 * LEV, CX), F32),
            pltpu.VMEM((2, 1, ROWS), F32),
            pltpu.VMEM((2, 1, ROWS), F32),
            pltpu.VMEM((8, 32, 128), F32),
            pltpu.SemaphoreType.DMA((8,)),
            pltpu.SemaphoreType.DMA((3,)),
            pltpu.SemaphoreType.DMA((14,)),
            pltpu.SemaphoreType.DMA((14,)),
        ],
        compiler_params=pltpu.CompilerParams(
            collective_id=0, has_side_effects=True, vmem_limit_bytes=62 << 20
        ),
        cost_estimate=pl.CostEstimate(flops=30_000_000_000, bytes_accessed=2_000_000, transcendentals=0),
    )(
        leaving.reshape(8, 8),
        leave_count.reshape(8),
        coriolis,
        winds.reshape(2 * ROWS, CX),
        rays.reshape(NB * 4, 128),
        ray_cell.reshape(NB, 128),
        ray_level.reshape(NB, 128),
        turning.reshape(NB, 128),
    )
    rays_new, arrived, tendency = pl.pallas_call(
        deliver,
        out_shape=tuple(jax.ShapeDtypeStruct(each.shape, F32) for each in (rays_new, arrived, tendency)),
        in_specs=[hbm] * 3,
        out_specs=(hbm,) * 3,
        scratch_shapes=[pltpu.VMEM(each.shape, F32) for each in (rays_new, arrived, tendency)]
        + [pltpu.SemaphoreType.DMA((3,)), pltpu.SemaphoreType.DMA((3,))],
        compiler_params=pltpu.CompilerParams(vmem_limit_bytes=62 << 20),
    )(rays_new, arrived, tendency)
    return (
        rays_new.reshape(rays.shape),
        arrived.reshape(1, 1, 8, 8, 4, 128),
        tendency.reshape(winds.shape),
    )


def solution(mesh):
    placed = (
        P(None, None, "lat", "lon"),
        P("lat"),
        P("lon", "lat", None, None, None),
        P("lon", "lat", None, None),
        P("lon", "lat", None, None),
        P("lon", "lat", None, None),
        P("lon", "lat", None, None),
        P("lon", "lat", None),
    )
    return jax.shard_map(
        on_device,
        mesh=mesh,
        in_specs=placed,
        out_specs=(
            P("lon", "lat", None, None, None),
            P("lon", "lat", None, None, None, None),
            P(None, None, "lat", "lon"),
        ),
        check_vma=False,
    )
```

```python
import jax
import jax.numpy as jnp
from jax import lax
from jax.experimental import pallas as pl
from jax.experimental.pallas import tpu as pltpu
from jax.sharding import PartitionSpec as P

STEP = 0.1
DIRS = ((0, 1), (0, -1), (1, 0), (-1, 0), (1, 1), (1, -1), (-1, 1), (-1, -1))
MESH = pl.DeviceIdType.MESH
LEV, CY, CX, NB = 12, 32, 128, 128
ROWS = LEV * CY
LAG = 8
GREET = 2
GRP = 8
SPAN = GRP * 128
HALF = SPAN // 2
STEPS = NB // GRP
UNIT = 5461.0
F32, BF16 = jnp.float32, jnp.bfloat16


def propagate(wave_k, wave_l, wave_m, action, sample, fcor, turn):
    new_k = wave_k - STEP * (wave_k * sample[0] + wave_l * sample[1])
    new_l = wave_l - STEP * (wave_k * sample[2] + wave_l * sample[3])
    new_m = wave_m - STEP * (wave_k * sample[4] + wave_l * sample[5])
    new_m = jnp.where(turn == 1, -new_m, new_m)
    horiz = new_k * new_k + new_l * new_l
    total = horiz + new_m * new_m + 1.0
    fsq = fcor * fcor
    freq2 = (horiz + fsq * (new_m * new_m + 1.0)) / total
    freq = jnp.sqrt(freq2)
    group_x = new_k * (1.0 - freq2) / (freq * total)
    group_z = new_m * (fsq - freq2) / (freq * total)
    return (
        new_k,
        new_l,
        new_m,
        group_z * new_k * action,
        group_z * new_l * action,
        group_x * new_k * action,
    )


def level_diff(field):
    zero = jnp.zeros((CY, CX), F32)
    upper = jnp.concatenate([field[CY:], zero], axis=0)
    lower = jnp.concatenate([zero, field[:-CY]], axis=0)
    return (upper - lower) * 0.5


def split(value):
    high = value.astype(BF16)
    return high, (value - high.astype(F32)).astype(BF16)


def pack(first, second):
    high = jnp.round(first * UNIT).astype(jnp.int32)
    low = jnp.round(second * UNIT).astype(jnp.int32)
    return high * 65536 + (low + 32768)


def unpack(word):
    high = lax.shift_right_arithmetic(word, 16)
    low = jnp.bitwise_and(word, 65535) - 32768
    return high.astype(F32) * (1.0 / UNIT), low.astype(F32) * (1.0 / UNIT)


def kernel(
    leaving_in, count_in, fcor_in, winds_in, rays_in, cell_in, level_in, turn_in,
    rays_new, arrived, tendency,
    rays_out, tend, leaving, count, fcor, winds, rays, cell, level, turn,
    wind_t, table, words, lat_edge, lon_edge, fresh, hots, found, samples, fluxes, dep,
    lon_out, lon_in, lat_out, lat_in, edge_out, edge_in, box_out,
    load_sem, store_sem, send_sem, recv_sem,
):
    lon, lat = lax.axis_index("lon"), lax.axis_index("lat")
    nlon, nlat = lax.axis_size("lon"), lax.axis_size("lat")

    def at(dlat, dlon):
        return (lax.rem(lon + dlon + nlon, nlon), lax.rem(lat + dlat + nlat, nlat))

    def copy(src, dst, which, where):
        return pltpu.make_async_remote_copy(
            src_ref=src, dst_ref=dst, send_sem=send_sem.at[which], recv_sem=recv_sem.at[which],
            device_id=at(*where), device_id_type=MESH,
        )

    barrier = pltpu.get_barrier_semaphore()
    for where in DIRS:
        pl.semaphore_signal(barrier, inc=1, device_id=at(*where), device_id_type=MESH)

    loads = [
        pltpu.make_async_copy(src, dst, load_sem.at[i])
        for i, (src, dst) in enumerate(
            (
                (winds_in, winds),
                (cell_in, cell),
                (level_in, level),
                (rays_in, rays),
                (turn_in, turn),
                (fcor_in, fcor),
                (leaving_in, leaving),
                (count_in, count),
            )
        )
    ]
    for each in loads:
        each.start()
    dep[...] = jnp.zeros((ROWS, 6 * CX), F32)
    fluxes[:, NB : NB + 2 * GRP, :] = jnp.zeros((6, 2 * GRP, 128), F32)
    loads[0].wait()
    for w in range(2):
        flipped = winds[w * ROWS : (w + 1) * ROWS, :].T
        wind_t[w] = flipped
        lon_out[0, w : w + 1, :] = flipped[CX - 1 : CX, :]
        lon_out[1, w : w + 1, :] = flipped[0:1, :]
    lat_out[0] = winds[pl.ds(CY - 1, 2 * LEV, stride=CY), :]
    lat_out[1] = winds[pl.ds(0, 2 * LEV, stride=CY), :]
    halos = [
        copy(lon_out.at[0], lon_in.at[0], 0, (0, 1)),
        copy(lon_out.at[1], lon_in.at[1], 1, (0, -1)),
        copy(lat_out.at[0], lat_in.at[0], 2, (1, 0)),
        copy(lat_out.at[1], lat_in.at[1], 3, (-1, 0)),
    ]
    def keep(field, flipped):
        high, low = split(flipped)
        table[field * CX : (field + 1) * CX, 0:ROWS] = high
        table[field * CX : (field + 1) * CX, ROWS : 2 * ROWS] = low

    for w in range(2):
        keep(w, level_diff(winds[w * ROWS : (w + 1) * ROWS, :]).T)
    column = lax.broadcasted_iota(jnp.int32, (CX, ROWS), 0)
    row = lax.rem(lax.broadcasted_iota(jnp.int32, (ROWS, CX), 0), CY)
    lane = lax.broadcasted_iota(jnp.int32, (ROWS, CX), 1)
    along, across = [], []
    for w in range(2):
        field = winds[w * ROWS : (w + 1) * ROWS, :]
        east = jnp.where(lane == CX - 1, 0.0, pltpu.roll(field, CX - 1, 1))
        west = jnp.where(lane == 0, 0.0, pltpu.roll(field, 1, 1))
        along.append((east - west) * 0.5)
        north = jnp.where(row == CY - 1, 0.0, pltpu.roll(field, ROWS - 1, 0))
        south = jnp.where(row == 0, 0.0, pltpu.roll(field, 1, 0))
        across.append((north - south) * 0.5)
    words[0] = pack(*along)
    words[1] = pack(*across)
    for each in loads[1:]:
        each.wait()

    x_ids = lax.broadcasted_iota(jnp.int32, (CX, 128), 0)
    r_ids = lax.broadcasted_iota(jnp.int32, (ROWS, 128), 0)

    def blocks_of(c):
        return pl.ds(pl.multiple_of(c * GRP, GRP), GRP)

    def place(c):
        cells = cell[blocks_of(c), :]
        y = lax.shift_right_logical(cells, 7)
        return jnp.bitwise_and(cells, CX - 1), y, level[blocks_of(c), :] * CY + y

    def rise(halves):
        blocks = [h * (GRP // 2) + i for h in halves for i in range(GRP // 2)]
        for i, block in enumerate(blocks):
            cells = cell[pl.ds(block, 1), :]
            rows = level[pl.ds(block, 1), :] * CY + lax.shift_right_logical(cells, 7)
            hot = jnp.where(r_ids == rows, 1.0, 0.0).astype(BF16)
            fresh[:, i * 128 : (i + 1) * 128] = hot
            lanes = slice(i % (GRP // 2) * 128, (i % (GRP // 2) + 1) * 128)
            hots[halves[i // (GRP // 2)], :, lanes] = hot
        hot = fresh[:, : len(halves) * HALF]
        picked = lax.dot_general(
            table[...], jnp.concatenate([hot, hot], axis=0), (((1,), (0,)), ((), ())),
            preferred_element_type=F32,
        )
        for i, block in enumerate(blocks):
            mask = x_ids == jnp.bitwise_and(cell[pl.ds(block, 1), :], CX - 1)
            for f in range(2):
                part = picked[f * CX : (f + 1) * CX, i * 128 : (i + 1) * 128]
                samples[f, pl.ds(block, 1), :] = jnp.sum(
                    jnp.where(mask, part, 0.0), axis=0, keepdims=True
                )

    def pick(c):
        x, _, rows = place(c)
        got = [jnp.zeros((GRP, 128), jnp.int32)] * 2
        for r in range(ROWS):
            here = rows == r
            for w in range(2):
                line = jnp.broadcast_to(words[w, r : r + 1, :], (GRP, CX))
                taken = jnp.take_along_axis(line, x, axis=1, mode="promise_in_bounds")
                got[w] = jnp.where(here, taken, got[w])
        for w in range(2):
            found[w, blocks_of(c), :] = got[w]

    def advance(c):
        x, y, rows = place(c)
        levels = level[blocks_of(c), :]
        sample = [*unpack(found[0, blocks_of(c), :]), *unpack(found[1, blocks_of(c), :])]
        sample += [samples[0, blocks_of(c), :], samples[1, blocks_of(c), :]]
        lanes, tiles = jnp.bitwise_and(rows, 127), lax.shift_right_logical(rows, 7)
        nought = jnp.full((GRP, 128), 32768, jnp.int32)
        for side, end in ((0, 0), (1, CX - 1)):
            word = nought
            for t in range(ROWS // 128):
                line = jnp.broadcast_to(lon_edge[side, t : t + 1, :], (GRP, 128))
                taken = jnp.take_along_axis(line, lanes, axis=1, mode="promise_in_bounds")
                word = jnp.where(jnp.logical_and(tiles == t, x == end), taken, word)
            for f, value in enumerate(unpack(word)):
                sample[f] += value
        for side, end in ((0, 0), (1, CY - 1)):
            word = nought
            for z in range(LEV):
                line = jnp.broadcast_to(lat_edge[side, z : z + 1, :], (GRP, 128))
                taken = jnp.take_along_axis(line, x, axis=1, mode="promise_in_bounds")
                word = jnp.where(jnp.logical_and(levels == z, y == end), taken, word)
            for f, value in enumerate(unpack(word)):
                sample[2 + f] += value
        f_ray = jnp.zeros((GRP, 128), F32)
        for i in range(CY):
            f_ray = jnp.where(y == i, fcor[i], f_ray)
        fields = [rays[pl.ds(c * GRP * 4 + f, GRP, stride=4), :] for f in range(4)]
        out = propagate(*fields, sample, f_ray, turn[blocks_of(c), :])
        for f, value in enumerate((*out[:3], fields[3])):
            rays_out[pl.ds(c * GRP * 4 + f, GRP, stride=4), :] = value
        for j in range(3):
            high = out[3 + j].astype(BF16).astype(F32)
            fluxes[2 * j, blocks_of(c), :] = high
            fluxes[2 * j + 1, blocks_of(c), :] = out[3 + j] - high

    def hot_of(c, steps):
        return [hots[2 * c + i] for i in range(2 * steps)]

    def scatter(js, c, hot, source=None):
        source = c if source is None else source
        parts = []
        for i in range(len(hot) * GRP // 2):
            mask = x_ids == jnp.bitwise_and(cell[pl.ds(c * GRP + i, 1), :], CX - 1)
            parts.append(
                jnp.concatenate(
                    [
                        jnp.where(mask, fluxes[2 * j + p, pl.ds(source * GRP + i, 1), :], 0.0).astype(BF16)
                        for j in js
                        for p in range(2)
                    ],
                    axis=0,
                )
            )
        lanes = slice(js[0] * 2 * CX, (js[-1] + 1) * 2 * CX)
        dep[:, lanes] += lax.dot_general(
            jnp.concatenate(hot, axis=1), jnp.concatenate(parts, axis=1), (((1,), (1,)), ((), ())),
            preferred_element_type=F32,
        )

    greet = jnp.where(lon == 0, GREET + 3, jnp.where(lax.rem(lon, 4) == 0, GREET + 2, GREET))

    def before(c, carry):
        @pl.when(c == greet)
        def _():
            pl.semaphore_wait(barrier, 8)
            for each in halos:
                each.start()

        rise((2 * c, 2 * c + 1, 2 * LAG + c))
        pick(c)
        return carry

    lax.fori_loop(0, LAG, before, 0)

    for each in halos:
        each.wait()
    for side, sign in ((0, -0.5), (1, 0.5)):
        ends = [lon_in[side, w : w + 1, :] * sign for w in range(2)]
        word = pack(*ends)
        for t in range(ROWS // 128):
            lon_edge[side, t : t + 1, :] = word[:, t * 128 : (t + 1) * 128]
        closed = lat == (0 if side == 0 else nlat - 1)
        lat_edge[side] = pack(
            *[jnp.where(closed, 0.0, lat_in[side, w * LEV : (w + 1) * LEV, :] * sign) for w in range(2)]
        )
    advance(0)
    advance(1)

    def after(i, carry):
        pair = jnp.maximum(2 * i - 2, 0)
        source = jnp.where(i == 0, STEPS, 2 * i - 2)
        scatter((2,), pair, hot_of(pair, 2), source)
        advance(jnp.minimum(2 * i + 2, LAG - 2 + i))
        advance(jnp.minimum(2 * i + 3, LAG - 1 + i))
        rise((3 * LAG + i,))
        pick(LAG + i)
        return carry

    lax.fori_loop(0, STEPS - LAG, after, 0)
    advance(STEPS - 1)

    boxes = []
    for d, where in enumerate(DIRS):
        for slot in range(8):
            block = rays_out[pl.ds(leaving[d, slot] * 4, 4), :]
            box_out[d, slot * 4 : slot * 4 + 4, :] = jnp.where(slot < count[d], block, 0.0)
        boxes.append(copy(box_out.at[d], arrived.at[d], 4 + d, where))
        boxes[-1].start()

    def deposit(j):
        return dep[:, j * 2 * CX : j * 2 * CX + CX] + dep[:, j * 2 * CX + CX : (j + 1) * 2 * CX]


    def last(js, first, count, each=2):
        def step(c, carry):
            scatter(js, first + each * c, hot_of(first + each * c, each))
            return carry

        lax.fori_loop(0, count // each, step, 0)

    stores = [pltpu.make_async_copy(rays_out, rays_new, store_sem.at[0])]
    stores[0].start()
    last((2,), STEPS - 2, 2)
    zonal = deposit(2).T
    edge_out[0, 0:1, :] = zonal[CX - 1 : CX, :]
    edge_out[1, 0:1, :] = zonal[0:1, :]
    edges = [
        copy(edge_out.at[0], edge_in.at[0], 12, (0, 1)),
        copy(edge_out.at[1], edge_in.at[1], 13, (0, -1)),
    ]
    for each in edges:
        each.start()
    last((0, 1), 0, STEPS, 4)
    tend[ROWS : 2 * ROWS, :] = -level_diff(deposit(1))
    half = pl.ds(ROWS, ROWS)
    stores.append(pltpu.make_async_copy(tend.at[half], tendency.at[half], store_sem.at[1]))
    stores[1].start()
    zonal = deposit(2)
    east = jnp.where(lane == CX - 1, 0.0, pltpu.roll(zonal, CX - 1, 1))
    west = jnp.where(lane == 0, 0.0, pltpu.roll(zonal, 1, 1))
    tend[0:ROWS, :] = -level_diff(deposit(0)) - (east - west) * 0.5
    for each in edges:
        each.wait()
    beyond = jnp.where(column == CX - 1, edge_in[1, 0:1, :] * -0.5, 0.0)
    tend[0:ROWS, :] += jnp.where(column == 0, edge_in[0, 0:1, :] * 0.5, beyond).T
    half = pl.ds(0, ROWS)
    stores.append(pltpu.make_async_copy(tend.at[half], tendency.at[half], store_sem.at[2]))
    stores[2].start()
    for each in (*boxes, *stores):
        each.wait()


def deliver(*refs):
    ins, outs, held, sem_in, sem_out = refs[:3], refs[3:6], refs[6:9], refs[9], refs[10]
    loads = [pltpu.make_async_copy(ins[i], held[i], sem_in.at[i]) for i in range(3)]
    stores = [pltpu.make_async_copy(held[i], outs[i], sem_out.at[i]) for i in range(3)]
    for each in loads:
        each.start()
    for load, store in zip(loads, stores):
        load.wait()
        store.start()
    for each in stores:
        each.wait()


def on_device(winds, coriolis, rays, ray_cell, ray_level, turning, leaving, leave_count):
    hbm = pl.BlockSpec(memory_space=pltpu.HBM)
    rays_new, arrived, tendency = pl.pallas_call(
        kernel,
        out_shape=(
            jax.ShapeDtypeStruct((NB * 4, 128), F32),
            jax.ShapeDtypeStruct((8, 32, 128), F32),
            jax.ShapeDtypeStruct((2 * ROWS, CX), F32),
        ),
        in_specs=[hbm] * 8,
        out_specs=(hbm,) * 3,
        scratch_shapes=[
            pltpu.VMEM((NB * 4, 128), F32),
            pltpu.VMEM((2 * ROWS, CX), F32),
            pltpu.SMEM((8, 8), jnp.int32),
            pltpu.SMEM((8,), jnp.int32),
            pltpu.SMEM((32,), F32),
            pltpu.VMEM((2 * ROWS, CX), F32),
            pltpu.VMEM((NB * 4, 128), F32),
            pltpu.VMEM((NB, 128), jnp.int32),
            pltpu.VMEM((NB, 128), jnp.int32),
            pltpu.VMEM((NB, 128), jnp.int32),
            pltpu.VMEM((2, CX, ROWS), F32),
            pltpu.VMEM((2 * CX, 2 * ROWS), BF16),
            pltpu.VMEM((2, ROWS, CX), jnp.int32),
            pltpu.VMEM((2, LEV, CX), jnp.int32),
            pltpu.VMEM((2, ROWS // 128, 128), jnp.int32),
            pltpu.VMEM((ROWS, 3 * HALF), BF16),
            pltpu.VMEM((2 * STEPS, ROWS, HALF), BF16),
            pltpu.VMEM((2, NB, 128), jnp.int32),
            pltpu.VMEM((2, NB, 128), F32),
            pltpu.VMEM((6, NB + 2 * GRP, 128), F32),
            pltpu.VMEM((ROWS, 6 * CX), F32),
            pltpu.VMEM((2, 2, ROWS), F32),
            pltpu.VMEM((2, 2, ROWS), F32),
            pltpu.VMEM((2, 2 * LEV, CX), F32),
            pltpu.VMEM((2, 2 * LEV, CX), F32),
            pltpu.VMEM((2, 1, ROWS), F32),
            pltpu.VMEM((2, 1, ROWS), F32),
            pltpu.VMEM((8, 32, 128), F32),
            pltpu.SemaphoreType.DMA((8,)),
            pltpu.SemaphoreType.DMA((3,)),
            pltpu.SemaphoreType.DMA((14,)),
            pltpu.SemaphoreType.DMA((14,)),
        ],
        compiler_params=pltpu.CompilerParams(
            collective_id=0, has_side_effects=True, vmem_limit_bytes=62 << 20
        ),
        cost_estimate=pl.CostEstimate(flops=30_000_000_000, bytes_accessed=2_000_000, transcendentals=0),
    )(
        leaving.reshape(8, 8),
        leave_count.reshape(8),
        coriolis,
        winds.reshape(2 * ROWS, CX),
        rays.reshape(NB * 4, 128),
        ray_cell.reshape(NB, 128),
        ray_level.reshape(NB, 128),
        turning.reshape(NB, 128),
    )
    rays_new, arrived, tendency = pl.pallas_call(
        deliver,
        out_shape=tuple(jax.ShapeDtypeStruct(each.shape, F32) for each in (rays_new, arrived, tendency)),
        in_specs=[hbm] * 3,
        out_specs=(hbm,) * 3,
        scratch_shapes=[pltpu.VMEM(each.shape, F32) for each in (rays_new, arrived, tendency)]
        + [pltpu.SemaphoreType.DMA((3,)), pltpu.SemaphoreType.DMA((3,))],
        compiler_params=pltpu.CompilerParams(vmem_limit_bytes=62 << 20),
    )(rays_new, arrived, tendency)
    return (
        rays_new.reshape(rays.shape),
        arrived.reshape(1, 1, 8, 8, 4, 128),
        tendency.reshape(winds.shape),
    )


def solution(mesh):
    placed = (
        P(None, None, "lat", "lon"),
        P("lat"),
        P("lon", "lat", None, None, None),
        P("lon", "lat", None, None),
        P("lon", "lat", None, None),
        P("lon", "lat", None, None),
        P("lon", "lat", None, None),
        P("lon", "lat", None),
    )
    return jax.shard_map(
        on_device,
        mesh=mesh,
        in_specs=placed,
        out_specs=(
            P("lon", "lat", None, None, None),
            P("lon", "lat", None, None, None, None),
            P(None, None, "lat", "lon"),
        ),
        check_vma=False,
    )
```

```python
import jax
import jax.numpy as jnp
from jax import lax
from jax.experimental import pallas as pl
from jax.experimental.pallas import tpu as pltpu
from jax.sharding import PartitionSpec as P

STEP = 0.1
DIRS = ((0, 1), (0, -1), (1, 0), (-1, 0), (1, 1), (1, -1), (-1, 1), (-1, -1))
MESH = pl.DeviceIdType.MESH
LEV, CY, CX, NB = 12, 32, 128, 128
ROWS = LEV * CY
LAG = 8
GREET = 2
GRP = 8
SPAN = GRP * 128
HALF = SPAN // 2
STEPS = NB // GRP
UNIT = 5461.0
F32, BF16 = jnp.float32, jnp.bfloat16


def propagate(wave_k, wave_l, wave_m, action, sample, fcor, turn):
    new_k = wave_k - STEP * (wave_k * sample[0] + wave_l * sample[1])
    new_l = wave_l - STEP * (wave_k * sample[2] + wave_l * sample[3])
    new_m = wave_m - STEP * (wave_k * sample[4] + wave_l * sample[5])
    new_m = jnp.where(turn == 1, -new_m, new_m)
    horiz = new_k * new_k + new_l * new_l
    total = horiz + new_m * new_m + 1.0
    fsq = fcor * fcor
    freq2 = (horiz + fsq * (new_m * new_m + 1.0)) / total
    freq = jnp.sqrt(freq2)
    group_x = new_k * (1.0 - freq2) / (freq * total)
    group_z = new_m * (fsq - freq2) / (freq * total)
    return (
        new_k,
        new_l,
        new_m,
        group_z * new_k * action,
        group_z * new_l * action,
        group_x * new_k * action,
    )


def level_diff(field):
    zero = jnp.zeros((CY, CX), F32)
    upper = jnp.concatenate([field[CY:], zero], axis=0)
    lower = jnp.concatenate([zero, field[:-CY]], axis=0)
    return (upper - lower) * 0.5


def split(value):
    high = value.astype(BF16)
    return high, (value - high.astype(F32)).astype(BF16)


def pack(first, second):
    high = jnp.round(first * UNIT).astype(jnp.int32)
    low = jnp.round(second * UNIT).astype(jnp.int32)
    return high * 65536 + (low + 32768)


def unpack(word):
    high = lax.shift_right_arithmetic(word, 16)
    low = jnp.bitwise_and(word, 65535) - 32768
    return high.astype(F32) * (1.0 / UNIT), low.astype(F32) * (1.0 / UNIT)


def kernel(
    leaving_in, count_in, fcor_in, winds_in, rays_in, cell_in, level_in, turn_in,
    rays_new, arrived, tendency,
    rays_out, tend, leaving, count, fcor, winds, rays, cell, level, turn,
    wind_t, table, words, lat_edge, lon_edge, fresh, hots, found, samples, fluxes, dep,
    lon_out, lon_in, lat_out, lat_in, edge_out, edge_in, box_out,
    load_sem, store_sem, send_sem, recv_sem,
):
    lon, lat = lax.axis_index("lon"), lax.axis_index("lat")
    nlon, nlat = lax.axis_size("lon"), lax.axis_size("lat")

    def at(dlat, dlon):
        return (lax.rem(lon + dlon + nlon, nlon), lax.rem(lat + dlat + nlat, nlat))

    def copy(src, dst, which, where):
        return pltpu.make_async_remote_copy(
            src_ref=src, dst_ref=dst, send_sem=send_sem.at[which], recv_sem=recv_sem.at[which],
            device_id=at(*where), device_id_type=MESH,
        )

    barrier = pltpu.get_barrier_semaphore()
    for where in DIRS:
        pl.semaphore_signal(barrier, inc=1, device_id=at(*where), device_id_type=MESH)

    loads = [
        pltpu.make_async_copy(src, dst, load_sem.at[i])
        for i, (src, dst) in enumerate(
            (
                (winds_in, winds),
                (cell_in, cell),
                (level_in, level),
                (rays_in, rays),
                (turn_in, turn),
                (fcor_in, fcor),
                (leaving_in, leaving),
                (count_in, count),
            )
        )
    ]
    for each in loads:
        each.start()
    dep[...] = jnp.zeros((ROWS, 6 * CX), F32)
    fluxes[:, NB : NB + 2 * GRP, :] = jnp.zeros((6, 2 * GRP, 128), F32)
    loads[0].wait()
    for w in range(2):
        flipped = winds[w * ROWS : (w + 1) * ROWS, :].T
        wind_t[w] = flipped
        lon_out[0, w : w + 1, :] = flipped[CX - 1 : CX, :]
        lon_out[1, w : w + 1, :] = flipped[0:1, :]
    lat_out[0] = winds[pl.ds(CY - 1, 2 * LEV, stride=CY), :]
    lat_out[1] = winds[pl.ds(0, 2 * LEV, stride=CY), :]
    halos = [
        copy(lon_out.at[0], lon_in.at[0], 0, (0, 1)),
        copy(lon_out.at[1], lon_in.at[1], 1, (0, -1)),
        copy(lat_out.at[0], lat_in.at[0], 2, (1, 0)),
        copy(lat_out.at[1], lat_in.at[1], 3, (-1, 0)),
    ]
    def keep(field, flipped):
        high, low = split(flipped)
        table[field * CX : (field + 1) * CX, 0:ROWS] = high
        table[field * CX : (field + 1) * CX, ROWS : 2 * ROWS] = low

    for w in range(2):
        keep(w, level_diff(winds[w * ROWS : (w + 1) * ROWS, :]).T)
    column = lax.broadcasted_iota(jnp.int32, (CX, ROWS), 0)
    row = lax.rem(lax.broadcasted_iota(jnp.int32, (ROWS, CX), 0), CY)
    lane = lax.broadcasted_iota(jnp.int32, (ROWS, CX), 1)
    along, across = [], []
    for w in range(2):
        field = winds[w * ROWS : (w + 1) * ROWS, :]
        east = jnp.where(lane == CX - 1, 0.0, pltpu.roll(field, CX - 1, 1))
        west = jnp.where(lane == 0, 0.0, pltpu.roll(field, 1, 1))
        along.append((east - west) * 0.5)
        north = jnp.where(row == CY - 1, 0.0, pltpu.roll(field, ROWS - 1, 0))
        south = jnp.where(row == 0, 0.0, pltpu.roll(field, 1, 0))
        across.append((north - south) * 0.5)
    words[0] = pack(*along)
    words[1] = pack(*across)
    for each in loads[1:]:
        each.wait()

    x_ids = lax.broadcasted_iota(jnp.int32, (CX, 128), 0)
    r_ids = lax.broadcasted_iota(jnp.int32, (ROWS, 128), 0)

    def blocks_of(c):
        return pl.ds(pl.multiple_of(c * GRP, GRP), GRP)

    def place(c):
        cells = cell[blocks_of(c), :]
        y = lax.shift_right_logical(cells, 7)
        return jnp.bitwise_and(cells, CX - 1), y, level[blocks_of(c), :] * CY + y

    def rise(halves):
        blocks = [h * (GRP // 2) + i for h in halves for i in range(GRP // 2)]
        for i, block in enumerate(blocks):
            cells = cell[pl.ds(block, 1), :]
            rows = level[pl.ds(block, 1), :] * CY + lax.shift_right_logical(cells, 7)
            hot = jnp.where(r_ids == rows, 1.0, 0.0).astype(BF16)
            fresh[:, i * 128 : (i + 1) * 128] = hot
            lanes = slice(i % (GRP // 2) * 128, (i % (GRP // 2) + 1) * 128)
            hots[halves[i // (GRP // 2)], :, lanes] = hot
        hot = fresh[:, : len(halves) * HALF]
        picked = lax.dot_general(
            table[...], jnp.concatenate([hot, hot], axis=0), (((1,), (0,)), ((), ())),
            preferred_element_type=F32,
        )
        for i, block in enumerate(blocks):
            mask = x_ids == jnp.bitwise_and(cell[pl.ds(block, 1), :], CX - 1)
            for f in range(2):
                part = picked[f * CX : (f + 1) * CX, i * 128 : (i + 1) * 128]
                samples[f, pl.ds(block, 1), :] = jnp.sum(
                    jnp.where(mask, part, 0.0), axis=0, keepdims=True
                )

    def pick(c):
        x, _, rows = place(c)
        got = [jnp.zeros((GRP, 128), jnp.int32)] * 2
        for r in range(ROWS):
            here = rows == r
            for w in range(2):
                line = jnp.broadcast_to(words[w, r : r + 1, :], (GRP, CX))
                taken = jnp.take_along_axis(line, x, axis=1, mode="promise_in_bounds")
                got[w] = jnp.where(here, taken, got[w])
        for w in range(2):
            found[w, blocks_of(c), :] = got[w]

    def advance(c):
        x, y, rows = place(c)
        levels = level[blocks_of(c), :]
        sample = [*unpack(found[0, blocks_of(c), :]), *unpack(found[1, blocks_of(c), :])]
        sample += [samples[0, blocks_of(c), :], samples[1, blocks_of(c), :]]
        lanes, tiles = jnp.bitwise_and(rows, 127), lax.shift_right_logical(rows, 7)
        nought = jnp.full((GRP, 128), 32768, jnp.int32)
        for side, end in ((0, 0), (1, CX - 1)):
            word = nought
            for t in range(ROWS // 128):
                line = jnp.broadcast_to(lon_edge[side, t : t + 1, :], (GRP, 128))
                taken = jnp.take_along_axis(line, lanes, axis=1, mode="promise_in_bounds")
                word = jnp.where(jnp.logical_and(tiles == t, x == end), taken, word)
            for f, value in enumerate(unpack(word)):
                sample[f] += value
        for side, end in ((0, 0), (1, CY - 1)):
            word = nought
            for z in range(LEV):
                line = jnp.broadcast_to(lat_edge[side, z : z + 1, :], (GRP, 128))
                taken = jnp.take_along_axis(line, x, axis=1, mode="promise_in_bounds")
                word = jnp.where(jnp.logical_and(levels == z, y == end), taken, word)
            for f, value in enumerate(unpack(word)):
                sample[2 + f] += value
        f_ray = jnp.zeros((GRP, 128), F32)
        for i in range(CY):
            f_ray = jnp.where(y == i, fcor[i], f_ray)
        fields = [rays[pl.ds(c * GRP * 4 + f, GRP, stride=4), :] for f in range(4)]
        out = propagate(*fields, sample, f_ray, turn[blocks_of(c), :])
        for f, value in enumerate((*out[:3], fields[3])):
            rays_out[pl.ds(c * GRP * 4 + f, GRP, stride=4), :] = value
        for j in range(3):
            high = out[3 + j].astype(BF16).astype(F32)
            fluxes[2 * j, blocks_of(c), :] = high
            fluxes[2 * j + 1, blocks_of(c), :] = out[3 + j] - high

    def hot_of(c, steps):
        return [hots[2 * c + i] for i in range(2 * steps)]

    def scatter(js, c, hot, source=None):
        source = c if source is None else source
        parts = []
        for i in range(len(hot) * GRP // 2):
            mask = x_ids == jnp.bitwise_and(cell[pl.ds(c * GRP + i, 1), :], CX - 1)
            parts.append(
                jnp.concatenate(
                    [
                        jnp.where(mask, fluxes[2 * j + p, pl.ds(source * GRP + i, 1), :], 0.0).astype(BF16)
                        for j in js
                        for p in range(2)
                    ],
                    axis=0,
                )
            )
        lanes = slice(js[0] * 2 * CX, (js[-1] + 1) * 2 * CX)
        dep[:, lanes] += lax.dot_general(
            jnp.concatenate(hot, axis=1), jnp.concatenate(parts, axis=1), (((1,), (1,)), ((), ())),
            preferred_element_type=F32,
        )

    greet = jnp.where(lon == 0, GREET + 3, jnp.where(lax.rem(lon, 4) == 0, GREET + 2, GREET))

    def before(c, carry):
        @pl.when(c == greet)
        def _():
            pl.semaphore_wait(barrier, 8)
            for each in halos:
                each.start()

        rise((2 * c, 2 * c + 1, 2 * LAG + c))
        pick(c)
        return carry

    lax.fori_loop(0, LAG, before, 0)

    for each in halos:
        each.wait()
    for side, sign in ((0, -0.5), (1, 0.5)):
        ends = [lon_in[side, w : w + 1, :] * sign for w in range(2)]
        word = pack(*ends)
        for t in range(ROWS // 128):
            lon_edge[side, t : t + 1, :] = word[:, t * 128 : (t + 1) * 128]
        closed = lat == (0 if side == 0 else nlat - 1)
        lat_edge[side] = pack(
            *[jnp.where(closed, 0.0, lat_in[side, w * LEV : (w + 1) * LEV, :] * sign) for w in range(2)]
        )
    advance(0)
    advance(1)

    def after(i, carry):
        pair = jnp.maximum(2 * i - 2, 0)
        source = jnp.where(i == 0, STEPS, 2 * i - 2)
        scatter((2,), pair, hot_of(pair, 2), source)
        scatter((1,), i, hot_of(i, 1))
        advance(jnp.minimum(2 * i + 2, LAG - 2 + i))
        advance(jnp.minimum(2 * i + 3, LAG - 1 + i))
        rise((3 * LAG + i,))
        pick(LAG + i)
        return carry

    lax.fori_loop(0, STEPS - LAG, after, 0)
    advance(STEPS - 1)

    boxes = []
    for d, where in enumerate(DIRS):
        for slot in range(8):
            block = rays_out[pl.ds(leaving[d, slot] * 4, 4), :]
            box_out[d, slot * 4 : slot * 4 + 4, :] = jnp.where(slot < count[d], block, 0.0)
        boxes.append(copy(box_out.at[d], arrived.at[d], 4 + d, where))
        boxes[-1].start()

    def deposit(j):
        return dep[:, j * 2 * CX : j * 2 * CX + CX] + dep[:, j * 2 * CX + CX : (j + 1) * 2 * CX]


    def last(js, first, count, each=2):
        def step(c, carry):
            scatter(js, first + each * c, hot_of(first + each * c, each))
            return carry

        lax.fori_loop(0, count // each, step, 0)

    stores = [pltpu.make_async_copy(rays_out, rays_new, store_sem.at[0])]
    stores[0].start()
    last((2,), STEPS - 2, 2)
    zonal = deposit(2).T
    edge_out[0, 0:1, :] = zonal[CX - 1 : CX, :]
    edge_out[1, 0:1, :] = zonal[0:1, :]
    edges = [
        copy(edge_out.at[0], edge_in.at[0], 12, (0, 1)),
        copy(edge_out.at[1], edge_in.at[1], 13, (0, -1)),
    ]
    for each in edges:
        each.start()
    last((0, 1), LAG, STEPS - LAG, 8)
    last((0,), 0, LAG, 8)
    tend[ROWS : 2 * ROWS, :] = -level_diff(deposit(1))
    half = pl.ds(ROWS, ROWS)
    stores.append(pltpu.make_async_copy(tend.at[half], tendency.at[half], store_sem.at[1]))
    stores[1].start()
    zonal = deposit(2)
    east = jnp.where(lane == CX - 1, 0.0, pltpu.roll(zonal, CX - 1, 1))
    west = jnp.where(lane == 0, 0.0, pltpu.roll(zonal, 1, 1))
    tend[0:ROWS, :] = -level_diff(deposit(0)) - (east - west) * 0.5
    for each in edges:
        each.wait()
    beyond = jnp.where(column == CX - 1, edge_in[1, 0:1, :] * -0.5, 0.0)
    tend[0:ROWS, :] += jnp.where(column == 0, edge_in[0, 0:1, :] * 0.5, beyond).T
    half = pl.ds(0, ROWS)
    stores.append(pltpu.make_async_copy(tend.at[half], tendency.at[half], store_sem.at[2]))
    stores[2].start()
    for each in (*boxes, *stores):
        each.wait()


def deliver(*refs):
    ins, outs, held, sem_in, sem_out = refs[:3], refs[3:6], refs[6:9], refs[9], refs[10]
    loads = [pltpu.make_async_copy(ins[i], held[i], sem_in.at[i]) for i in range(3)]
    stores = [pltpu.make_async_copy(held[i], outs[i], sem_out.at[i]) for i in range(3)]
    for each in loads:
        each.start()
    for load, store in zip(loads, stores):
        load.wait()
        store.start()
    for each in stores:
        each.wait()


def on_device(winds, coriolis, rays, ray_cell, ray_level, turning, leaving, leave_count):
    hbm = pl.BlockSpec(memory_space=pltpu.HBM)
    rays_new, arrived, tendency = pl.pallas_call(
        kernel,
        out_shape=(
            jax.ShapeDtypeStruct((NB * 4, 128), F32),
            jax.ShapeDtypeStruct((8, 32, 128), F32),
            jax.ShapeDtypeStruct((2 * ROWS, CX), F32),
        ),
        in_specs=[hbm] * 8,
        out_specs=(hbm,) * 3,
        scratch_shapes=[
            pltpu.VMEM((NB * 4, 128), F32),
            pltpu.VMEM((2 * ROWS, CX), F32),
            pltpu.SMEM((8, 8), jnp.int32),
            pltpu.SMEM((8,), jnp.int32),
            pltpu.SMEM((32,), F32),
            pltpu.VMEM((2 * ROWS, CX), F32),
            pltpu.VMEM((NB * 4, 128), F32),
            pltpu.VMEM((NB, 128), jnp.int32),
            pltpu.VMEM((NB, 128), jnp.int32),
            pltpu.VMEM((NB, 128), jnp.int32),
            pltpu.VMEM((2, CX, ROWS), F32),
            pltpu.VMEM((2 * CX, 2 * ROWS), BF16),
            pltpu.VMEM((2, ROWS, CX), jnp.int32),
            pltpu.VMEM((2, LEV, CX), jnp.int32),
            pltpu.VMEM((2, ROWS // 128, 128), jnp.int32),
            pltpu.VMEM((ROWS, 3 * HALF), BF16),
            pltpu.VMEM((2 * STEPS, ROWS, HALF), BF16),
            pltpu.VMEM((2, NB, 128), jnp.int32),
            pltpu.VMEM((2, NB, 128), F32),
            pltpu.VMEM((6, NB + 2 * GRP, 128), F32),
            pltpu.VMEM((ROWS, 6 * CX), F32),
            pltpu.VMEM((2, 2, ROWS), F32),
            pltpu.VMEM((2, 2, ROWS), F32),
            pltpu.VMEM((2, 2 * LEV, CX), F32),
            pltpu.VMEM((2, 2 * LEV, CX), F32),
            pltpu.VMEM((2, 1, ROWS), F32),
            pltpu.VMEM((2, 1, ROWS), F32),
            pltpu.VMEM((8, 32, 128), F32),
            pltpu.SemaphoreType.DMA((8,)),
            pltpu.SemaphoreType.DMA((3,)),
            pltpu.SemaphoreType.DMA((14,)),
            pltpu.SemaphoreType.DMA((14,)),
        ],
        compiler_params=pltpu.CompilerParams(
            collective_id=0, has_side_effects=True, vmem_limit_bytes=62 << 20
        ),
        cost_estimate=pl.CostEstimate(flops=30_000_000_000, bytes_accessed=2_000_000, transcendentals=0),
    )(
        leaving.reshape(8, 8),
        leave_count.reshape(8),
        coriolis,
        winds.reshape(2 * ROWS, CX),
        rays.reshape(NB * 4, 128),
        ray_cell.reshape(NB, 128),
        ray_level.reshape(NB, 128),
        turning.reshape(NB, 128),
    )
    rays_new, arrived, tendency = pl.pallas_call(
        deliver,
        out_shape=tuple(jax.ShapeDtypeStruct(each.shape, F32) for each in (rays_new, arrived, tendency)),
        in_specs=[hbm] * 3,
        out_specs=(hbm,) * 3,
        scratch_shapes=[pltpu.VMEM(each.shape, F32) for each in (rays_new, arrived, tendency)]
        + [pltpu.SemaphoreType.DMA((3,)), pltpu.SemaphoreType.DMA((3,))],
        compiler_params=pltpu.CompilerParams(vmem_limit_bytes=62 << 20),
    )(rays_new, arrived, tendency)
    return (
        rays_new.reshape(rays.shape),
        arrived.reshape(1, 1, 8, 8, 4, 128),
        tendency.reshape(winds.shape),
    )


def solution(mesh):
    placed = (
        P(None, None, "lat", "lon"),
        P("lat"),
        P("lon", "lat", None, None, None),
        P("lon", "lat", None, None),
        P("lon", "lat", None, None),
        P("lon", "lat", None, None),
        P("lon", "lat", None, None),
        P("lon", "lat", None),
    )
    return jax.shard_map(
        on_device,
        mesh=mesh,
        in_specs=placed,
        out_specs=(
            P("lon", "lat", None, None, None),
            P("lon", "lat", None, None, None, None),
            P(None, None, "lat", "lon"),
        ),
        check_vma=False,
    )
```

```python
import jax
import jax.numpy as jnp
from jax import lax
from jax.experimental import pallas as pl
from jax.experimental.pallas import tpu as pltpu
from jax.sharding import PartitionSpec as P

STEP = 0.1
DIRS = ((0, 1), (0, -1), (1, 0), (-1, 0), (1, 1), (1, -1), (-1, 1), (-1, -1))
MESH = pl.DeviceIdType.MESH
LEV, CY, CX, NB = 12, 32, 128, 128
ROWS = LEV * CY
LAG = 8
GREET = 2
GRP = 8
SPAN = GRP * 128
HALF = SPAN // 2
STEPS = NB // GRP
UNIT = 5461.0
F32, BF16 = jnp.float32, jnp.bfloat16


def propagate(wave_k, wave_l, wave_m, action, sample, fcor, turn):
    new_k = wave_k - STEP * (wave_k * sample[0] + wave_l * sample[1])
    new_l = wave_l - STEP * (wave_k * sample[2] + wave_l * sample[3])
    new_m = wave_m - STEP * (wave_k * sample[4] + wave_l * sample[5])
    new_m = jnp.where(turn == 1, -new_m, new_m)
    horiz = new_k * new_k + new_l * new_l
    total = horiz + new_m * new_m + 1.0
    fsq = fcor * fcor
    freq2 = (horiz + fsq * (new_m * new_m + 1.0)) / total
    freq = jnp.sqrt(freq2)
    group_x = new_k * (1.0 - freq2) / (freq * total)
    group_z = new_m * (fsq - freq2) / (freq * total)
    return (
        new_k,
        new_l,
        new_m,
        group_z * new_k * action,
        group_z * new_l * action,
        group_x * new_k * action,
    )


def level_diff(field):
    zero = jnp.zeros((CY, CX), F32)
    upper = jnp.concatenate([field[CY:], zero], axis=0)
    lower = jnp.concatenate([zero, field[:-CY]], axis=0)
    return (upper - lower) * 0.5


def split(value):
    high = value.astype(BF16)
    return high, (value - high.astype(F32)).astype(BF16)


def pack(first, second):
    high = jnp.round(first * UNIT).astype(jnp.int32)
    low = jnp.round(second * UNIT).astype(jnp.int32)
    return high * 65536 + (low + 32768)


def unpack(word):
    high = lax.shift_right_arithmetic(word, 16)
    low = jnp.bitwise_and(word, 65535) - 32768
    return high.astype(F32) * (1.0 / UNIT), low.astype(F32) * (1.0 / UNIT)


def kernel(
    leaving_in, count_in, fcor_in, winds_in, rays_in, cell_in, level_in, turn_in,
    rays_new, arrived, tendency,
    rays_out, tend, leaving, count, fcor, winds, rays, cell, level, turn,
    wind_t, table, words, lat_edge, lon_edge, fresh, hots, found, samples, fluxes, dep,
    lon_out, lon_in, lat_out, lat_in, edge_out, edge_in, box_out,
    load_sem, store_sem, send_sem, recv_sem,
):
    lon, lat = lax.axis_index("lon"), lax.axis_index("lat")
    nlon, nlat = lax.axis_size("lon"), lax.axis_size("lat")

    def at(dlat, dlon):
        return (lax.rem(lon + dlon + nlon, nlon), lax.rem(lat + dlat + nlat, nlat))

    def copy(src, dst, which, where):
        return pltpu.make_async_remote_copy(
            src_ref=src, dst_ref=dst, send_sem=send_sem.at[which], recv_sem=recv_sem.at[which],
            device_id=at(*where), device_id_type=MESH,
        )

    barrier = pltpu.get_barrier_semaphore()
    for where in DIRS:
        pl.semaphore_signal(barrier, inc=1, device_id=at(*where), device_id_type=MESH)

    loads = [
        pltpu.make_async_copy(src, dst, load_sem.at[i])
        for i, (src, dst) in enumerate(
            (
                (winds_in, winds),
                (cell_in, cell),
                (level_in, level),
                (rays_in, rays),
                (turn_in, turn),
                (fcor_in, fcor),
                (leaving_in, leaving),
                (count_in, count),
            )
        )
    ]
    for each in loads:
        each.start()
    dep[...] = jnp.zeros((ROWS, 6 * CX), F32)
    fluxes[:, NB : NB + 2 * GRP, :] = jnp.zeros((6, 2 * GRP, 128), F32)
    loads[0].wait()
    for w in range(2):
        flipped = winds[w * ROWS : (w + 1) * ROWS, :].T
        wind_t[w] = flipped
        lon_out[0, w : w + 1, :] = flipped[CX - 1 : CX, :]
        lon_out[1, w : w + 1, :] = flipped[0:1, :]
    lat_out[0] = winds[pl.ds(CY - 1, 2 * LEV, stride=CY), :]
    lat_out[1] = winds[pl.ds(0, 2 * LEV, stride=CY), :]
    halos = [
        copy(lon_out.at[0], lon_in.at[0], 0, (0, 1)),
        copy(lon_out.at[1], lon_in.at[1], 1, (0, -1)),
        copy(lat_out.at[0], lat_in.at[0], 2, (1, 0)),
        copy(lat_out.at[1], lat_in.at[1], 3, (-1, 0)),
    ]
    def keep(field, flipped):
        high, low = split(flipped)
        table[field * CX : (field + 1) * CX, 0:ROWS] = high
        table[field * CX : (field + 1) * CX, ROWS : 2 * ROWS] = low

    for w in range(2):
        keep(w, level_diff(winds[w * ROWS : (w + 1) * ROWS, :]).T)
    column = lax.broadcasted_iota(jnp.int32, (CX, ROWS), 0)
    row = lax.rem(lax.broadcasted_iota(jnp.int32, (ROWS, CX), 0), CY)
    lane = lax.broadcasted_iota(jnp.int32, (ROWS, CX), 1)
    along, across = [], []
    for w in range(2):
        field = winds[w * ROWS : (w + 1) * ROWS, :]
        east = jnp.where(lane == CX - 1, 0.0, pltpu.roll(field, CX - 1, 1))
        west = jnp.where(lane == 0, 0.0, pltpu.roll(field, 1, 1))
        along.append((east - west) * 0.5)
        north = jnp.where(row == CY - 1, 0.0, pltpu.roll(field, ROWS - 1, 0))
        south = jnp.where(row == 0, 0.0, pltpu.roll(field, 1, 0))
        across.append((north - south) * 0.5)
    words[0] = pack(*along)
    words[1] = pack(*across)
    for each in loads[1:]:
        each.wait()

    x_ids = lax.broadcasted_iota(jnp.int32, (CX, 128), 0)
    r_ids = lax.broadcasted_iota(jnp.int32, (ROWS, 128), 0)

    def blocks_of(c):
        return pl.ds(pl.multiple_of(c * GRP, GRP), GRP)

    def place(c):
        cells = cell[blocks_of(c), :]
        y = lax.shift_right_logical(cells, 7)
        return jnp.bitwise_and(cells, CX - 1), y, level[blocks_of(c), :] * CY + y

    def rise(halves):
        blocks = [h * (GRP // 2) + i for h in halves for i in range(GRP // 2)]
        for i, block in enumerate(blocks):
            cells = cell[pl.ds(block, 1), :]
            rows = level[pl.ds(block, 1), :] * CY + lax.shift_right_logical(cells, 7)
            hot = jnp.where(r_ids == rows, 1.0, 0.0).astype(BF16)
            fresh[:, i * 128 : (i + 1) * 128] = hot
            lanes = slice(i % (GRP // 2) * 128, (i % (GRP // 2) + 1) * 128)
            hots[halves[i // (GRP // 2)], :, lanes] = hot
        hot = fresh[:, : len(halves) * HALF]
        picked = lax.dot_general(
            table[...], jnp.concatenate([hot, hot], axis=0), (((1,), (0,)), ((), ())),
            preferred_element_type=F32,
        )
        for i, block in enumerate(blocks):
            mask = x_ids == jnp.bitwise_and(cell[pl.ds(block, 1), :], CX - 1)
            for f in range(2):
                part = picked[f * CX : (f + 1) * CX, i * 128 : (i + 1) * 128]
                samples[f, pl.ds(block, 1), :] = jnp.sum(
                    jnp.where(mask, part, 0.0), axis=0, keepdims=True
                )

    def pick(c):
        x, _, rows = place(c)
        got = [jnp.zeros((GRP, 128), jnp.int32)] * 2
        for r in range(ROWS):
            here = rows == r
            for w in range(2):
                line = jnp.broadcast_to(words[w, r : r + 1, :], (GRP, CX))
                taken = jnp.take_along_axis(line, x, axis=1, mode="promise_in_bounds")
                got[w] = jnp.where(here, taken, got[w])
        for w in range(2):
            found[w, blocks_of(c), :] = got[w]

    def advance(c):
        x, y, rows = place(c)
        levels = level[blocks_of(c), :]
        sample = [*unpack(found[0, blocks_of(c), :]), *unpack(found[1, blocks_of(c), :])]
        sample += [samples[0, blocks_of(c), :], samples[1, blocks_of(c), :]]
        lanes, tiles = jnp.bitwise_and(rows, 127), lax.shift_right_logical(rows, 7)
        nought = jnp.full((GRP, 128), 32768, jnp.int32)
        for side, end in ((0, 0), (1, CX - 1)):
            word = nought
            for t in range(ROWS // 128):
                line = jnp.broadcast_to(lon_edge[side, t : t + 1, :], (GRP, 128))
                taken = jnp.take_along_axis(line, lanes, axis=1, mode="promise_in_bounds")
                word = jnp.where(jnp.logical_and(tiles == t, x == end), taken, word)
            for f, value in enumerate(unpack(word)):
                sample[f] += value
        for side, end in ((0, 0), (1, CY - 1)):
            word = nought
            for z in range(LEV):
                line = jnp.broadcast_to(lat_edge[side, z : z + 1, :], (GRP, 128))
                taken = jnp.take_along_axis(line, x, axis=1, mode="promise_in_bounds")
                word = jnp.where(jnp.logical_and(levels == z, y == end), taken, word)
            for f, value in enumerate(unpack(word)):
                sample[2 + f] += value
        f_ray = jnp.zeros((GRP, 128), F32)
        for i in range(CY):
            f_ray = jnp.where(y == i, fcor[i], f_ray)
        fields = [rays[pl.ds(c * GRP * 4 + f, GRP, stride=4), :] for f in range(4)]
        out = propagate(*fields, sample, f_ray, turn[blocks_of(c), :])
        for f, value in enumerate((*out[:3], fields[3])):
            rays_out[pl.ds(c * GRP * 4 + f, GRP, stride=4), :] = value
        for j in range(3):
            high = out[3 + j].astype(BF16).astype(F32)
            fluxes[2 * j, blocks_of(c), :] = high
            fluxes[2 * j + 1, blocks_of(c), :] = out[3 + j] - high

    def hot_of(c, steps):
        return [hots[2 * c + i] for i in range(2 * steps)]

    def scatter(js, c, hot, source=None):
        source = c if source is None else source
        parts = []
        for i in range(len(hot) * GRP // 2):
            mask = x_ids == jnp.bitwise_and(cell[pl.ds(c * GRP + i, 1), :], CX - 1)
            parts.append(
                jnp.concatenate(
                    [
                        jnp.where(mask, fluxes[2 * j + p, pl.ds(source * GRP + i, 1), :], 0.0).astype(BF16)
                        for j in js
                        for p in range(2)
                    ],
                    axis=0,
                )
            )
        lanes = slice(js[0] * 2 * CX, (js[-1] + 1) * 2 * CX)
        dep[:, lanes] += lax.dot_general(
            jnp.concatenate(hot, axis=1), jnp.concatenate(parts, axis=1), (((1,), (1,)), ((), ())),
            preferred_element_type=F32,
        )

    greet = jnp.where(lon == 0, GREET + 3, jnp.where(lax.rem(lon, 4) == 0, GREET + 2, GREET))

    def before(c, carry):
        @pl.when(c == greet)
        def _():
            pl.semaphore_wait(barrier, 8)
            for each in halos:
                each.start()

        rise((2 * c, 2 * c + 1, 2 * LAG + c))
        pick(c)
        return carry

    lax.fori_loop(0, LAG, before, 0)

    for each in halos:
        each.wait()
    for side, sign in ((0, -0.5), (1, 0.5)):
        ends = [lon_in[side, w : w + 1, :] * sign for w in range(2)]
        word = pack(*ends)
        for t in range(ROWS // 128):
            lon_edge[side, t : t + 1, :] = word[:, t * 128 : (t + 1) * 128]
        closed = lat == (0 if side == 0 else nlat - 1)
        lat_edge[side] = pack(
            *[jnp.where(closed, 0.0, lat_in[side, w * LEV : (w + 1) * LEV, :] * sign) for w in range(2)]
        )
    advance(0)
    advance(1)

    def after(i, carry):
        pair = jnp.maximum(2 * i - 2, 0)
        source = jnp.where(i == 0, STEPS, 2 * i - 2)
        scatter((2,), pair, hot_of(pair, 2), source)
        advance(jnp.minimum(2 * i + 2, LAG - 2 + i))
        advance(jnp.minimum(2 * i + 3, LAG - 1 + i))
        rise((3 * LAG + i,))
        pick(LAG + i)
        return carry

    lax.fori_loop(0, STEPS - LAG, after, 0)
    advance(STEPS - 1)

    boxes = []
    for d, where in enumerate(DIRS):
        for slot in range(8):
            block = rays_out[pl.ds(leaving[d, slot] * 4, 4), :]
            box_out[d, slot * 4 : slot * 4 + 4, :] = jnp.where(slot < count[d], block, 0.0)
        boxes.append(copy(box_out.at[d], arrived.at[d], 4 + d, where))
        boxes[-1].start()

    def deposit(j):
        return dep[:, j * 2 * CX : j * 2 * CX + CX] + dep[:, j * 2 * CX + CX : (j + 1) * 2 * CX]


    def last(js, first, count, each=2):
        def step(c, carry):
            scatter(js, first + each * c, hot_of(first + each * c, each))
            return carry

        lax.fori_loop(0, count // each, step, 0)

    stores = [pltpu.make_async_copy(rays_out, rays_new, store_sem.at[0])]
    stores[0].start()
    last((2,), STEPS - 2, 2)
    zonal = deposit(2).T
    edge_out[0, 0:1, :] = zonal[CX - 1 : CX, :]
    edge_out[1, 0:1, :] = zonal[0:1, :]
    edges = [
        copy(edge_out.at[0], edge_in.at[0], 12, (0, 1)),
        copy(edge_out.at[1], edge_in.at[1], 13, (0, -1)),
    ]
    for each in edges:
        each.start()
    last((0, 1), 0, STEPS, 8)
    tend[ROWS : 2 * ROWS, :] = -level_diff(deposit(1))
    half = pl.ds(ROWS, ROWS)
    stores.append(pltpu.make_async_copy(tend.at[half], tendency.at[half], store_sem.at[1]))
    stores[1].start()
    zonal = deposit(2)
    east = jnp.where(lane == CX - 1, 0.0, pltpu.roll(zonal, CX - 1, 1))
    west = jnp.where(lane == 0, 0.0, pltpu.roll(zonal, 1, 1))
    tend[0:ROWS, :] = -level_diff(deposit(0)) - (east - west) * 0.5
    for each in edges:
        each.wait()
    beyond = jnp.where(column == CX - 1, edge_in[1, 0:1, :] * -0.5, 0.0)
    tend[0:ROWS, :] += jnp.where(column == 0, edge_in[0, 0:1, :] * 0.5, beyond).T
    half = pl.ds(0, ROWS)
    stores.append(pltpu.make_async_copy(tend.at[half], tendency.at[half], store_sem.at[2]))
    stores[2].start()
    for each in (*boxes, *stores):
        each.wait()


def deliver(*refs):
    ins, outs, held, sem_in, sem_out = refs[:3], refs[3:6], refs[6:9], refs[9], refs[10]
    loads = [pltpu.make_async_copy(ins[i], held[i], sem_in.at[i]) for i in range(3)]
    stores = [pltpu.make_async_copy(held[i], outs[i], sem_out.at[i]) for i in range(3)]
    for each in loads:
        each.start()
    for load, store in zip(loads, stores):
        load.wait()
        store.start()
    for each in stores:
        each.wait()


def on_device(winds, coriolis, rays, ray_cell, ray_level, turning, leaving, leave_count):
    hbm = pl.BlockSpec(memory_space=pltpu.HBM)
    rays_new, arrived, tendency = pl.pallas_call(
        kernel,
        out_shape=(
            jax.ShapeDtypeStruct((NB * 4, 128), F32),
            jax.ShapeDtypeStruct((8, 32, 128), F32),
            jax.ShapeDtypeStruct((2 * ROWS, CX), F32),
        ),
        in_specs=[hbm] * 8,
        out_specs=(hbm,) * 3,
        scratch_shapes=[
            pltpu.VMEM((NB * 4, 128), F32),
            pltpu.VMEM((2 * ROWS, CX), F32),
            pltpu.SMEM((8, 8), jnp.int32),
            pltpu.SMEM((8,), jnp.int32),
            pltpu.SMEM((32,), F32),
            pltpu.VMEM((2 * ROWS, CX), F32),
            pltpu.VMEM((NB * 4, 128), F32),
            pltpu.VMEM((NB, 128), jnp.int32),
            pltpu.VMEM((NB, 128), jnp.int32),
            pltpu.VMEM((NB, 128), jnp.int32),
            pltpu.VMEM((2, CX, ROWS), F32),
            pltpu.VMEM((2 * CX, 2 * ROWS), BF16),
            pltpu.VMEM((2, ROWS, CX), jnp.int32),
            pltpu.VMEM((2, LEV, CX), jnp.int32),
            pltpu.VMEM((2, ROWS // 128, 128), jnp.int32),
            pltpu.VMEM((ROWS, 3 * HALF), BF16),
            pltpu.VMEM((2 * STEPS, ROWS, HALF), BF16),
            pltpu.VMEM((2, NB, 128), jnp.int32),
            pltpu.VMEM((2, NB, 128), F32),
            pltpu.VMEM((6, NB + 2 * GRP, 128), F32),
            pltpu.VMEM((ROWS, 6 * CX), F32),
            pltpu.VMEM((2, 2, ROWS), F32),
            pltpu.VMEM((2, 2, ROWS), F32),
            pltpu.VMEM((2, 2 * LEV, CX), F32),
            pltpu.VMEM((2, 2 * LEV, CX), F32),
            pltpu.VMEM((2, 1, ROWS), F32),
            pltpu.VMEM((2, 1, ROWS), F32),
            pltpu.VMEM((8, 32, 128), F32),
            pltpu.SemaphoreType.DMA((8,)),
            pltpu.SemaphoreType.DMA((3,)),
            pltpu.SemaphoreType.DMA((14,)),
            pltpu.SemaphoreType.DMA((14,)),
        ],
        compiler_params=pltpu.CompilerParams(
            collective_id=0, has_side_effects=True, vmem_limit_bytes=62 << 20
        ),
        cost_estimate=pl.CostEstimate(flops=30_000_000_000, bytes_accessed=2_000_000, transcendentals=0),
    )(
        leaving.reshape(8, 8),
        leave_count.reshape(8),
        coriolis,
        winds.reshape(2 * ROWS, CX),
        rays.reshape(NB * 4, 128),
        ray_cell.reshape(NB, 128),
        ray_level.reshape(NB, 128),
        turning.reshape(NB, 128),
    )
    rays_new, arrived, tendency = pl.pallas_call(
        deliver,
        out_shape=tuple(jax.ShapeDtypeStruct(each.shape, F32) for each in (rays_new, arrived, tendency)),
        in_specs=[hbm] * 3,
        out_specs=(hbm,) * 3,
        scratch_shapes=[pltpu.VMEM(each.shape, F32) for each in (rays_new, arrived, tendency)]
        + [pltpu.SemaphoreType.DMA((3,)), pltpu.SemaphoreType.DMA((3,))],
        compiler_params=pltpu.CompilerParams(vmem_limit_bytes=62 << 20),
    )(rays_new, arrived, tendency)
    return (
        rays_new.reshape(rays.shape),
        arrived.reshape(1, 1, 8, 8, 4, 128),
        tendency.reshape(winds.shape),
    )


def solution(mesh):
    placed = (
        P(None, None, "lat", "lon"),
        P("lat"),
        P("lon", "lat", None, None, None),
        P("lon", "lat", None, None),
        P("lon", "lat", None, None),
        P("lon", "lat", None, None),
        P("lon", "lat", None, None),
        P("lon", "lat", None),
    )
    return jax.shard_map(
        on_device,
        mesh=mesh,
        in_specs=placed,
        out_specs=(
            P("lon", "lat", None, None, None),
            P("lon", "lat", None, None, None, None),
            P(None, None, "lat", "lon"),
        ),
        check_vma=False,
    )
```
